32 devices in a mesh: tm: 8 (over z, y), gy: 4 (over x, core).
Axes of the slice: x: 2, y: 2, z: 4, core: 2. Of those that a mesh axis runs over, the one named last changes fastest.
Arguments:
- residual: float32 [8, 8, 256, 1024], P('tm', None, 'gy'), may hold values from -0.4 to 0.4
Outputs:
- correction: float32 [8, 8, 256, 1024], P('tm', None, 'gy')
The draws below stay inside these ranges and needn't reach their ends.
All inputs are finite; a program needn't handle non-finite values.
Results may differ from the reference program's by a relative error of at most 0.00019.
Values sent between devices are 32-bit elements; how exact they have to be, the bound alone decides.
No kernel may reach another device: no remote copies, remote signals or barrier semaphores. Data moves between devices by JAX's collectives and lax.ppermute only.
A program may use at most 64 MiB of HBM per device.

```python
import math
import jax
import jax.numpy as jnp
from jax import lax

NX = 1024
NZ = 8
STEPS = 8
NY = 256


def draw_residual(key, part):
    key = jax.random.fold_in(key, 11)
    shape = (STEPS, NZ, NY, NX)
    values = 0.05 * jax.random.normal(key, shape, jnp.float32)
    return jnp.clip(values, -0.4, 0.4)


def setup_inputs(seed: int = 0) -> dict:
    key_of = jax.random.split(jax.random.key(seed), 2)
    residual = draw_residual(jax.random.fold_in(key_of[1], 71), 0)
    return {"residual": residual}


ALPHA_RATIO = 0.95
STEP_SCALE = 0.26

def spectrum_of(count):
    indices = jnp.arange(count, dtype=jnp.float32) + 1.0
    return 2.0 - 2.0 * jnp.cos(jnp.pi * indices / (count + 1))

def symbol_of(freq, count, weight_mu):
    radius = ALPHA_RATIO ** (1.0 / count)
    theta = 2.0 * jnp.pi * freq / count
    zreal = radius * jnp.cos(theta)
    zimag = -radius * jnp.sin(theta)
    first = 1.0 - zreal
    second = -zimag
    lam_re = first * first - second * second + STEP_SCALE * weight_mu * zreal
    lam_im = 2.0 * first * second + STEP_SCALE * weight_mu * zimag
    return (lam_re, lam_im)

def sine_axis(values, axis):
    count = values.shape[axis]
    moved = jnp.moveaxis(values, axis, -1)
    zero_col = jnp.zeros(moved.shape[:-1] + (1,), values.dtype)
    extended = jnp.concatenate([zero_col, moved, zero_col, -moved[..., ::-1]], axis=-1)
    transformed = jnp.fft.fft(extended, axis=-1)
    result = -jnp.imag(transformed[..., 1:count + 1]) * (0.5 * math.sqrt(2.0 / (count + 1)))
    return jnp.moveaxis(result.astype(values.dtype), -1, axis)

def spatial(block):
    return sine_axis(sine_axis(sine_axis(block, 2), 1), 0)

def reference(residual):
    steps = residual.shape[0]
    times = jnp.arange(steps, dtype=jnp.float32)
    decay = ALPHA_RATIO ** (times / steps)
    hatted = lax.map(spatial, residual * decay[:, None, None, None])
    transformed = jnp.fft.fft(hatted, axis=0)
    weight_mu = spectrum_of(NZ)[:, None, None] + spectrum_of(NY)[None, :, None] + spectrum_of(NX)[None, None, :]
    freq = jnp.arange(steps, dtype=jnp.float32)[:, None, None, None]
    lam_re, lam_im = symbol_of(freq, steps, weight_mu[None])
    solved = transformed / (lam_re + 1j * lam_im)
    timed = jnp.real(jnp.fft.ifft(solved, axis=0)).astype(residual.dtype)
    return lax.map(spatial, timed) / decay[:, None, None, None]
```

```python
import functools
import math

import jax
import jax.numpy as jnp
import numpy as np
from jax import lax
from jax.experimental import pallas as pl
from jax.experimental.pallas import tpu as pltpu
from jax.sharding import PartitionSpec as P

ALPHA_RATIO = 0.95
STEP_SCALE = 0.26
CHUNKS = 4
LANES = 128
VMEM_BYTES = 40 * 1024 * 1024


def sine_table(count):
    indices = np.arange(count, dtype=np.int64) + 1
    product = indices[:, None] * indices[None, :] % (2 * (count + 1))
    return math.sqrt(2.0 / (count + 1)) * np.sin(np.pi * product / (count + 1))


def spectrum_of(count):
    indices = np.arange(count, dtype=np.float64) + 1.0
    return 2.0 - 2.0 * np.cos(np.pi * indices / (count + 1))


def table_parts(count):
    table = sine_table(count).astype(np.float32)
    high = table.astype(jnp.bfloat16)
    low = (table - high.astype(np.float32)).astype(jnp.bfloat16)
    return jnp.asarray(high), jnp.asarray(low)


def parts_of(values):
    high = values.astype(jnp.bfloat16)
    return high, (values - high.astype(jnp.float32)).astype(jnp.bfloat16)


def dot(left, right):
    return jnp.dot(left, right, preferred_element_type=jnp.float32)


def call(kernel, out_shape, flops, moved, scratch=(), in_smem=1, n_in=1):
    specs = [pl.BlockSpec(memory_space=pltpu.SMEM)] * in_smem
    specs += [pl.BlockSpec(memory_space=pltpu.VMEM)] * (n_in - in_smem)
    return pl.pallas_call(
        kernel,
        out_shape=out_shape,
        in_specs=specs,
        out_specs=jax.tree.map(
            lambda _: pl.BlockSpec(memory_space=pltpu.VMEM), out_shape
        ),
        scratch_shapes=scratch,
        compiler_params=pltpu.CompilerParams(vmem_limit_bytes=VMEM_BYTES),
        cost_estimate=pl.CostEstimate(
            flops=flops, bytes_accessed=moved, transcendentals=0
        ),
    )


class Plan:
    def __init__(self, mesh, shape):
        self.steps = mesh.shape["tm"]
        self.groups = mesh.shape["gy"]
        self.depth, self.rows, self.width = shape[1], shape[2], shape[3]
        self.height = self.rows
        self.half = self.steps // 2
        self.across = min(self.groups, self.width // LANES)
        self.deep = self.groups // self.across
        self.block = self.width // self.across
        self.chunks = min(CHUNKS, self.depth // self.deep)
        self.planes = self.depth // self.deep // self.chunks
        self.rows_dev = self.height // self.groups
        self.piece = self.height // self.half
        self.sine_z = sine_table(self.depth)


def forward_x(plan, chunk, ids, x, sxh, sxl, *refs):
    outs, (high, low) = refs[: plan.groups], refs[plan.groups :]
    rows = plan.rows_dev
    strip = 16
    per = plan.depth // plan.deep

    def planes(index, carry):
        at = pl.multiple_of(index * strip, strip)
        total = [None] * (plan.deep * plan.planes)
        for z in range(plan.depth):
            value = x[z, pl.ds(at, strip), :]
            for jc in range(plan.deep):
                for u in range(plan.planes):
                    c = jc * per + chunk * plan.planes + u
                    term = value * np.float32(plan.sine_z[c, z])
                    slot = jc * plan.planes + u
                    total[slot] = term if z == 0 else total[slot] + term
        for slot, value in enumerate(total):
            top, rest = parts_of(value)
            high[slot, pl.ds(at, strip), :] = top
            low[slot, pl.ds(at, strip), :] = rest
        return carry

    lax.fori_loop(0, rows // strip, planes, 0)
    me = ids[1]
    for k in range(plan.groups):
        owner = me ^ k
        first = (owner // plan.across) * plan.planes
        columns = pl.ds(
            pl.multiple_of(owner % plan.across * plan.block, LANES), plan.block
        )
        top = high[pl.ds(first, plan.planes)].reshape(-1, plan.width)
        rest = low[pl.ds(first, plan.planes)].reshape(-1, plan.width)
        right = sxh[:, columns]
        value = dot(top, right) + dot(rest, right) + dot(top, sxl[:, columns])
        outs[k][...] = value.reshape(plan.planes, rows, plan.block)


def transform_y(plan, axis_in, axis_out, ids, *refs):
    size = (plan.groups, plan.half)
    rows = (plan.rows_dev, plan.piece)
    n_in, n_out = size[axis_in], size[axis_out]
    r_in, r_out = rows[axis_in], rows[axis_out]
    where = (ids[1], lax.rem(ids[0], plan.half))
    pieces = refs[:n_in]
    syh, syl = refs[n_in : n_in + 2]
    outs = refs[n_in + 2 : n_in + 2 + n_out]
    high, low, full = refs[n_in + 2 + n_out :]
    for k in range(n_in):
        at = pl.ds(pl.multiple_of((where[axis_in] ^ k) * r_in, r_in), r_in)
        for u in range(plan.planes):
            top, rest = parts_of(pieces[k][u])
            high[u, at, :] = top
            low[u, at, :] = rest
    for u in range(plan.planes):
        right = high[u]
        full[u] = dot(syh[...], right) + dot(syl[...], right) + dot(syh[...], low[u])
    for k in range(n_out):
        at = pl.ds(pl.multiple_of((where[axis_out] ^ k) * r_out, r_out), r_out)
        for u in range(plan.planes):
            outs[k][u] = full[u, at, :]


STRIP = 16


def per_strip(plan, chunk, ids, smu_z, smu_y, smu_x, body):
    me, group = ids[0], ids[1]
    first = (group // plan.across) * (plan.depth // plan.deep) + chunk * plan.planes
    columns = pl.ds(
        pl.multiple_of(group % plan.across * plan.block, LANES), plan.block
    )
    across = smu_x[:, columns]
    base = lax.rem(me, plan.half) * plan.piece

    def step(index, carry):
        at = pl.multiple_of(index * STRIP, STRIP)
        down = smu_y[pl.ds(pl.multiple_of(base + at, STRIP), STRIP), :]
        plane = across + down
        for u in range(plan.planes):
            body(u, pl.ds(at, STRIP), plane + smu_z[first + u])
        return carry

    lax.fori_loop(0, plan.piece // STRIP, step, 0)


def chebyshev(smu, count):
    kappa = 2.0 - smu
    values = [jnp.zeros_like(kappa), jnp.ones_like(kappa)]
    for _ in range(count):
        values.append(kappa * values[-1] - values[-2])
    return kappa, values


def half_end(plan, chunk, ids, smu_z, smu_y, smu_x, *refs):
    pieces, out = refs[: plan.half], refs[plan.half]
    place = lax.rem(ids[0], plan.half)
    for case in range(plan.half):

        @pl.when(place == case)
        def _():
            def body(u, rows, smu):
                kappa = 2.0 - smu
                before = pieces[case][u, rows, :]
                last = kappa * before + pieces[case ^ 1][u, rows, :]
                for j in range(2, plan.half):
                    value = pieces[case ^ j][u, rows, :]
                    before, last = last, kappa * last - before + value
                out[0, u, rows, :] = before
                out[1, u, rows, :] = last

            per_strip(plan, chunk, ids, smu_z, smu_y, smu_x, body)


def half_solve(plan, chunk, ids, smu_z, smu_y, smu_x, *refs):
    pieces = refs[: plan.half]
    mine, other = refs[plan.half : plan.half + 2]
    outs = refs[plan.half + 2 :]
    place = lax.rem(ids[0], plan.half)
    entering = jnp.where(ids[0] < plan.half, ALPHA_RATIO, 1.0).astype(jnp.float32)
    for case in range(plan.half):

        @pl.when(place == case)
        def _():
            def body(u, rows, smu):
                kappa, cheb = chebyshev(smu, plan.half)
                u_up, u_at, u_down = cheb[-1], cheb[-2], cheb[-3]
                turn = 0.5 * (u_up - u_down)
                det = (1.0 - ALPHA_RATIO) ** 2 + ALPHA_RATIO * (
                    smu * (4.0 - smu) * (u_at * u_at)
                )
                inverse = 1.0 / det
                far0 = entering * other[0, u, rows, :]
                far1 = entering * other[1, u, rows, :]
                near0 = ALPHA_RATIO * mine[0, u, rows, :]
                near1 = ALPHA_RATIO * mine[1, u, rows, :]
                p0 = u_up * far0 - u_at * far1 + near0
                p1 = u_at * far0 - u_down * far1 + near1
                even = (1.0 - ALPHA_RATIO) * turn * inverse
                odd = 0.5 * (1.0 + ALPHA_RATIO) * u_at * inverse
                before = even * p0 + odd * (2.0 * p1 - kappa * p0)
                last = even * p1 + odd * (kappa * p1 - 2.0 * p0)
                for j in range(plan.half):
                    value = pieces[case ^ j][u, rows, :]
                    before, last = last, kappa * last - before + value
                    outs[case ^ j][u, rows, :] = last

            per_strip(plan, chunk, ids, smu_z, smu_y, smu_x, body)


def rows_of(plan, ids, pieces, sxh, sxl, write):
    me = ids[1]
    for jc in range(plan.deep):
        total = None
        for ja in range(plan.across):
            k = jc * plan.across + ja
            owner = me ^ k
            at = pl.ds(
                pl.multiple_of(owner % plan.across * plan.block, LANES), plan.block
            )
            top, rest = parts_of(
                pieces[k][...].reshape(plan.planes * plan.rows_dev, plan.block)
            )
            right = sxh[at, :]
            value = dot(top, right) + dot(rest, right) + dot(top, sxl[at, :])
            total = value if total is None else total + value
        owner = (me // plan.across) ^ jc
        write(owner, total.reshape(plan.planes, plan.rows_dev, plan.width))


def backward_x(plan, ids, *refs):
    pieces = refs[: plan.groups]
    sxh, sxl, out = refs[plan.groups :]

    def write(owner, value):
        out[pl.ds(owner * plan.planes, plan.planes)] = value

    rows_of(plan, ids, pieces, sxh, sxl, write)


def backward_last(plan, ids, *refs):
    pieces = refs[: plan.groups]
    sxh, sxl = refs[plan.groups : plan.groups + 2]
    ready = refs[plan.groups + 2 : plan.groups + 1 + plan.chunks]
    out, last = refs[plan.groups + 1 + plan.chunks :]

    def write(owner, value):
        last[pl.ds(owner * plan.planes, plan.planes)] = value

    rows_of(plan, ids, pieces, sxh, sxl, write)
    strip = 8
    per = plan.depth // plan.deep
    sources = list(ready) + [last]

    def planes(index, carry):
        at = pl.ds(pl.multiple_of(index * strip, strip), strip)
        total = [None] * plan.depth
        for chunk, source in enumerate(sources):
            for jc in range(plan.deep):
                for u in range(plan.planes):
                    c = jc * per + chunk * plan.planes + u
                    value = source[jc * plan.planes + u, at, :]
                    for z in range(plan.depth):
                        term = value * np.float32(plan.sine_z[z, c])
                        total[z] = term if total[z] is None else total[z] + term
        for z in range(plan.depth):
            out[z, at, :] = total[z]
        return carry

    lax.fori_loop(0, plan.rows_dev // strip, planes, 0)


def swap(values, axis, count, distance):
    if distance == 0:
        return values
    return lax.ppermute(values, axis, [(i, i ^ distance) for i in range(count)])


def on_device(plan, residual):
    steps, groups, half = plan.steps, plan.groups, plan.half
    ids = jnp.stack([lax.axis_index("tm"), lax.axis_index("gy")]).astype(jnp.int32)
    sxh, sxl = table_parts(plan.width)
    syh, syl = table_parts(plan.height)
    smu_z = jnp.asarray(STEP_SCALE * spectrum_of(plan.depth), jnp.float32)
    smu_y = jnp.asarray(STEP_SCALE * spectrum_of(plan.height)[:, None], jnp.float32)
    smu_x = jnp.asarray(STEP_SCALE * spectrum_of(plan.width)[None, :], jnp.float32)
    field = residual[0]
    f32 = functools.partial(jax.ShapeDtypeStruct, dtype=jnp.float32)
    bf16 = jnp.bfloat16
    rows_in = f32((plan.planes, plan.rows_dev, plan.block))
    modes = f32((plan.planes, plan.piece, plan.block))
    ends = f32((2,) + modes.shape)
    count = plan.planes * plan.height * plan.block
    table_x = 4 * plan.width * plan.width
    table_y = 4 * plan.height * plan.height
    y_scratch = [
        pltpu.VMEM((plan.planes, plan.height, plan.block), bf16),
        pltpu.VMEM((plan.planes, plan.height, plan.block), bf16),
        pltpu.VMEM((plan.planes, plan.height, plan.block), jnp.float32),
    ]
    whole_planes = plan.deep * plan.planes
    ready = []
    for chunk in range(plan.chunks):
        pieces = call(
            functools.partial(forward_x, plan, chunk),
            [rows_in] * groups,
            6 * count * plan.width,
            4 * field.size + table_x + 4 * count,
            [pltpu.VMEM((whole_planes, plan.rows_dev, plan.width), bf16)] * 2,
            1,
            4,
        )(ids, field, sxh, sxl)
        pieces = [swap(v, "gy", groups, k) for k, v in enumerate(pieces)]
        pieces = call(
            functools.partial(transform_y, plan, 0, 1),
            [modes] * half,
            6 * count * plan.height,
            8 * count + table_y,
            y_scratch,
            1,
            3 + groups,
        )(ids, *pieces, syh, syl)
        pieces = [swap(v, "tm", steps, k) for k, v in enumerate(pieces)]
        mine = call(
            functools.partial(half_end, plan, chunk),
            ends,
            8 * count,
            6 * count,
            (),
            2,
            4 + half,
        )(ids, smu_z, smu_y, smu_x, *pieces)
        other = swap(mine, "tm", steps, half)
        pieces = call(
            functools.partial(half_solve, plan, chunk),
            [modes] * half,
            40 * count,
            12 * count,
            (),
            2,
            6 + half,
        )(ids, smu_z, smu_y, smu_x, *pieces, mine, other)
        pieces = [swap(v, "tm", steps, k) for k, v in enumerate(pieces)]
        pieces = call(
            functools.partial(transform_y, plan, 1, 0),
            [rows_in] * groups,
            6 * count * plan.height,
            8 * count + table_y,
            y_scratch,
            1,
            3 + half,
        )(ids, *pieces, syh, syl)
        pieces = [swap(v, "gy", groups, k) for k, v in enumerate(pieces)]
        planes = f32((whole_planes, plan.rows_dev, plan.width))
        if chunk < plan.chunks - 1:
            ready.append(
                call(
                    functools.partial(backward_x, plan),
                    planes,
                    6 * count * plan.width,
                    8 * count + table_x,
                    (),
                    1,
                    3 + groups,
                )(ids, *pieces, sxh, sxl)
            )
    result = call(
        functools.partial(backward_last, plan),
        f32(field.shape),
        6 * count * plan.width,
        8 * field.size + table_x,
        [pltpu.VMEM(planes.shape, jnp.float32)],
        1,
        2 + groups + plan.chunks,
    )(ids, *pieces, sxh, sxl, *ready)
    return result[None]


def solution(mesh):
    spec = P("tm", None, "gy", None)

    def whole(residual):
        plan = Plan(mesh, residual.shape)
        plan.height = residual.shape[2]
        return jax.shard_map(
            functools.partial(on_device, plan),
            mesh=mesh,
            in_specs=(spec,),
            out_specs=spec,
            check_vma=False,
        )(residual)

    return whole
```

```python
import functools
import math

import jax
import jax.numpy as jnp
import numpy as np
from jax import lax
from jax.experimental import pallas as pl
from jax.experimental.pallas import tpu as pltpu
from jax.sharding import PartitionSpec as P

ALPHA_RATIO = 0.95
STEP_SCALE = 0.26
CHUNKS = 2
LANES = 128
VMEM_BYTES = 40 * 1024 * 1024


def sine_table(count):
    indices = np.arange(count, dtype=np.int64) + 1
    product = indices[:, None] * indices[None, :] % (2 * (count + 1))
    return math.sqrt(2.0 / (count + 1)) * np.sin(np.pi * product / (count + 1))


def spectrum_of(count):
    indices = np.arange(count, dtype=np.float64) + 1.0
    return 2.0 - 2.0 * np.cos(np.pi * indices / (count + 1))


def table_parts(count):
    table = sine_table(count).astype(np.float32)
    high = table.astype(jnp.bfloat16)
    low = (table - high.astype(np.float32)).astype(jnp.bfloat16)
    return jnp.asarray(high), jnp.asarray(low)


def parts_of(values):
    high = values.astype(jnp.bfloat16)
    return high, (values - high.astype(jnp.float32)).astype(jnp.bfloat16)


def dot(left, right):
    return jnp.dot(left, right, preferred_element_type=jnp.float32)


def call(kernel, out_shape, flops, moved, scratch=(), in_smem=1, n_in=1):
    specs = [pl.BlockSpec(memory_space=pltpu.SMEM)] * in_smem
    specs += [pl.BlockSpec(memory_space=pltpu.VMEM)] * (n_in - in_smem)
    return pl.pallas_call(
        kernel,
        out_shape=out_shape,
        in_specs=specs,
        out_specs=jax.tree.map(
            lambda _: pl.BlockSpec(memory_space=pltpu.VMEM), out_shape
        ),
        scratch_shapes=scratch,
        compiler_params=pltpu.CompilerParams(vmem_limit_bytes=VMEM_BYTES),
        cost_estimate=pl.CostEstimate(
            flops=flops, bytes_accessed=moved, transcendentals=0
        ),
    )


class Plan:
    def __init__(self, mesh, shape):
        self.steps = mesh.shape["tm"]
        self.groups = mesh.shape["gy"]
        self.depth, self.rows, self.width = shape[1], shape[2], shape[3]
        self.height = self.rows
        self.half = self.steps // 2
        self.across = min(self.groups, self.width // LANES)
        self.deep = self.groups // self.across
        self.block = self.width // self.across
        self.chunks = min(CHUNKS, self.depth // self.deep)
        self.planes = self.depth // self.deep // self.chunks
        self.rows_dev = self.height // self.groups
        self.piece = self.height // self.half
        self.sine_z = sine_table(self.depth)


def forward_x(plan, chunk, ids, x, sxh, sxl, *refs):
    outs, (high, low) = refs[: plan.groups], refs[plan.groups :]
    rows = plan.rows_dev
    strip = 16
    per = plan.depth // plan.deep

    def planes(index, carry):
        at = pl.multiple_of(index * strip, strip)
        total = [None] * (plan.deep * plan.planes)
        for z in range(plan.depth):
            value = x[z, pl.ds(at, strip), :]
            for jc in range(plan.deep):
                for u in range(plan.planes):
                    c = jc * per + chunk * plan.planes + u
                    term = value * np.float32(plan.sine_z[c, z])
                    slot = jc * plan.planes + u
                    total[slot] = term if z == 0 else total[slot] + term
        for slot, value in enumerate(total):
            top, rest = parts_of(value)
            high[slot, pl.ds(at, strip), :] = top
            low[slot, pl.ds(at, strip), :] = rest
        return carry

    lax.fori_loop(0, rows // strip, planes, 0)
    me = ids[1]
    for k in range(plan.groups):
        owner = me ^ k
        first = (owner // plan.across) * plan.planes
        columns = pl.ds(
            pl.multiple_of(owner % plan.across * plan.block, LANES), plan.block
        )
        top = high[pl.ds(first, plan.planes)].reshape(-1, plan.width)
        rest = low[pl.ds(first, plan.planes)].reshape(-1, plan.width)
        right = sxh[:, columns]
        value = dot(top, right) + dot(rest, right) + dot(top, sxl[:, columns])
        outs[k][...] = value.reshape(plan.planes, rows, plan.block)


def transform_y(plan, axis_in, axis_out, ids, *refs):
    size = (plan.groups, plan.half)
    rows = (plan.rows_dev, plan.piece)
    n_in, n_out = size[axis_in], size[axis_out]
    r_in, r_out = rows[axis_in], rows[axis_out]
    where = (ids[1], lax.rem(ids[0], plan.half))
    pieces = refs[:n_in]
    syh, syl = refs[n_in : n_in + 2]
    outs = refs[n_in + 2 : n_in + 2 + n_out]
    high, low, full = refs[n_in + 2 + n_out :]
    for k in range(n_in):
        at = pl.ds(pl.multiple_of((where[axis_in] ^ k) * r_in, r_in), r_in)
        for u in range(plan.planes):
            top, rest = parts_of(pieces[k][u])
            high[u, at, :] = top
            low[u, at, :] = rest
    for u in range(plan.planes):
        right = high[u]
        full[u] = dot(syh[...], right) + dot(syl[...], right) + dot(syh[...], low[u])
    for k in range(n_out):
        at = pl.ds(pl.multiple_of((where[axis_out] ^ k) * r_out, r_out), r_out)
        for u in range(plan.planes):
            outs[k][u] = full[u, at, :]


STRIP = 16


def per_strip(plan, chunk, ids, smu_z, smu_y, smu_x, body):
    me, group = ids[0], ids[1]
    first = (group // plan.across) * (plan.depth // plan.deep) + chunk * plan.planes
    columns = pl.ds(
        pl.multiple_of(group % plan.across * plan.block, LANES), plan.block
    )
    across = smu_x[:, columns]
    base = lax.rem(me, plan.half) * plan.piece

    def step(index, carry):
        at = pl.multiple_of(index * STRIP, STRIP)
        down = smu_y[pl.ds(pl.multiple_of(base + at, STRIP), STRIP), :]
        plane = across + down
        for u in range(plan.planes):
            body(u, pl.ds(at, STRIP), plane + smu_z[first + u])
        return carry

    lax.fori_loop(0, plan.piece // STRIP, step, 0)


def chebyshev(smu, count):
    kappa = 2.0 - smu
    values = [jnp.zeros_like(kappa), jnp.ones_like(kappa)]
    for _ in range(count):
        values.append(kappa * values[-1] - values[-2])
    return kappa, values


def half_end(plan, chunk, ids, smu_z, smu_y, smu_x, *refs):
    pieces, out = refs[: plan.half], refs[plan.half]
    place = lax.rem(ids[0], plan.half)
    for case in range(plan.half):

        @pl.when(place == case)
        def _():
            def body(u, rows, smu):
                kappa = 2.0 - smu
                before = pieces[case][u, rows, :]
                last = kappa * before + pieces[case ^ 1][u, rows, :]
                for j in range(2, plan.half):
                    value = pieces[case ^ j][u, rows, :]
                    before, last = last, kappa * last - before + value
                out[0, u, rows, :] = before
                out[1, u, rows, :] = last

            per_strip(plan, chunk, ids, smu_z, smu_y, smu_x, body)


def half_solve(plan, chunk, ids, smu_z, smu_y, smu_x, *refs):
    pieces = refs[: plan.half]
    mine, other = refs[plan.half : plan.half + 2]
    outs = refs[plan.half + 2 :]
    place = lax.rem(ids[0], plan.half)
    entering = jnp.where(ids[0] < plan.half, ALPHA_RATIO, 1.0).astype(jnp.float32)
    for case in range(plan.half):

        @pl.when(place == case)
        def _():
            def body(u, rows, smu):
                kappa, cheb = chebyshev(smu, plan.half)
                u_up, u_at, u_down = cheb[-1], cheb[-2], cheb[-3]
                turn = 0.5 * (u_up - u_down)
                det = (1.0 - ALPHA_RATIO) ** 2 + ALPHA_RATIO * (
                    smu * (4.0 - smu) * (u_at * u_at)
                )
                inverse = 1.0 / det
                far0 = entering * other[0, u, rows, :]
                far1 = entering * other[1, u, rows, :]
                near0 = ALPHA_RATIO * mine[0, u, rows, :]
                near1 = ALPHA_RATIO * mine[1, u, rows, :]
                p0 = u_up * far0 - u_at * far1 + near0
                p1 = u_at * far0 - u_down * far1 + near1
                even = (1.0 - ALPHA_RATIO) * turn * inverse
                odd = 0.5 * (1.0 + ALPHA_RATIO) * u_at * inverse
                before = even * p0 + odd * (2.0 * p1 - kappa * p0)
                last = even * p1 + odd * (kappa * p1 - 2.0 * p0)
                for j in range(plan.half):
                    value = pieces[case ^ j][u, rows, :]
                    before, last = last, kappa * last - before + value
                    outs[case ^ j][u, rows, :] = last

            per_strip(plan, chunk, ids, smu_z, smu_y, smu_x, body)


def rows_of(plan, ids, pieces, sxh, sxl, write):
    me = ids[1]
    for jc in range(plan.deep):
        total = None
        for ja in range(plan.across):
            k = jc * plan.across + ja
            owner = me ^ k
            at = pl.ds(
                pl.multiple_of(owner % plan.across * plan.block, LANES), plan.block
            )
            top, rest = parts_of(
                pieces[k][...].reshape(plan.planes * plan.rows_dev, plan.block)
            )
            right = sxh[at, :]
            value = dot(top, right) + dot(rest, right) + dot(top, sxl[at, :])
            total = value if total is None else total + value
        owner = (me // plan.across) ^ jc
        write(owner, total.reshape(plan.planes, plan.rows_dev, plan.width))


def backward_x(plan, ids, *refs):
    pieces = refs[: plan.groups]
    sxh, sxl, out = refs[plan.groups :]

    def write(owner, value):
        out[pl.ds(owner * plan.planes, plan.planes)] = value

    rows_of(plan, ids, pieces, sxh, sxl, write)


def backward_last(plan, ids, *refs):
    pieces = refs[: plan.groups]
    sxh, sxl = refs[plan.groups : plan.groups + 2]
    ready = refs[plan.groups + 2 : plan.groups + 1 + plan.chunks]
    out, last = refs[plan.groups + 1 + plan.chunks :]

    def write(owner, value):
        last[pl.ds(owner * plan.planes, plan.planes)] = value

    rows_of(plan, ids, pieces, sxh, sxl, write)
    strip = 8
    per = plan.depth // plan.deep
    sources = list(ready) + [last]

    def planes(index, carry):
        at = pl.ds(pl.multiple_of(index * strip, strip), strip)
        total = [None] * plan.depth
        for chunk, source in enumerate(sources):
            for jc in range(plan.deep):
                for u in range(plan.planes):
                    c = jc * per + chunk * plan.planes + u
                    value = source[jc * plan.planes + u, at, :]
                    for z in range(plan.depth):
                        term = value * np.float32(plan.sine_z[z, c])
                        total[z] = term if total[z] is None else total[z] + term
        for z in range(plan.depth):
            out[z, at, :] = total[z]
        return carry

    lax.fori_loop(0, plan.rows_dev // strip, planes, 0)


def swap(values, axis, count, distance):
    if distance == 0:
        return values
    return lax.ppermute(values, axis, [(i, i ^ distance) for i in range(count)])


def on_device(plan, residual):
    steps, groups, half = plan.steps, plan.groups, plan.half
    ids = jnp.stack([lax.axis_index("tm"), lax.axis_index("gy")]).astype(jnp.int32)
    sxh, sxl = table_parts(plan.width)
    syh, syl = table_parts(plan.height)
    smu_z = jnp.asarray(STEP_SCALE * spectrum_of(plan.depth), jnp.float32)
    smu_y = jnp.asarray(STEP_SCALE * spectrum_of(plan.height)[:, None], jnp.float32)
    smu_x = jnp.asarray(STEP_SCALE * spectrum_of(plan.width)[None, :], jnp.float32)
    field = residual[0]
    f32 = functools.partial(jax.ShapeDtypeStruct, dtype=jnp.float32)
    bf16 = jnp.bfloat16
    rows_in = f32((plan.planes, plan.rows_dev, plan.block))
    modes = f32((plan.planes, plan.piece, plan.block))
    ends = f32((2,) + modes.shape)
    count = plan.planes * plan.height * plan.block
    table_x = 4 * plan.width * plan.width
    table_y = 4 * plan.height * plan.height
    y_scratch = [
        pltpu.VMEM((plan.planes, plan.height, plan.block), bf16),
        pltpu.VMEM((plan.planes, plan.height, plan.block), bf16),
        pltpu.VMEM((plan.planes, plan.height, plan.block), jnp.float32),
    ]
    whole_planes = plan.deep * plan.planes
    ready = []
    for chunk in range(plan.chunks):
        pieces = call(
            functools.partial(forward_x, plan, chunk),
            [rows_in] * groups,
            6 * count * plan.width,
            4 * field.size + table_x + 4 * count,
            [pltpu.VMEM((whole_planes, plan.rows_dev, plan.width), bf16)] * 2,
            1,
            4,
        )(ids, field, sxh, sxl)
        pieces = [swap(v, "gy", groups, k) for k, v in enumerate(pieces)]
        pieces = call(
            functools.partial(transform_y, plan, 0, 1),
            [modes] * half,
            6 * count * plan.height,
            8 * count + table_y,
            y_scratch,
            1,
            3 + groups,
        )(ids, *pieces, syh, syl)
        pieces = [swap(v, "tm", steps, k) for k, v in enumerate(pieces)]
        mine = call(
            functools.partial(half_end, plan, chunk),
            ends,
            8 * count,
            6 * count,
            (),
            2,
            4 + half,
        )(ids, smu_z, smu_y, smu_x, *pieces)
        other = swap(mine, "tm", steps, half)
        pieces = call(
            functools.partial(half_solve, plan, chunk),
            [modes] * half,
            40 * count,
            12 * count,
            (),
            2,
            6 + half,
        )(ids, smu_z, smu_y, smu_x, *pieces, mine, other)
        pieces = [swap(v, "tm", steps, k) for k, v in enumerate(pieces)]
        pieces = call(
            functools.partial(transform_y, plan, 1, 0),
            [rows_in] * groups,
            6 * count * plan.height,
            8 * count + table_y,
            y_scratch,
            1,
            3 + half,
        )(ids, *pieces, syh, syl)
        pieces = [swap(v, "gy", groups, k) for k, v in enumerate(pieces)]
        planes = f32((whole_planes, plan.rows_dev, plan.width))
        if chunk < plan.chunks - 1:
            ready.append(
                call(
                    functools.partial(backward_x, plan),
                    planes,
                    6 * count * plan.width,
                    8 * count + table_x,
                    (),
                    1,
                    3 + groups,
                )(ids, *pieces, sxh, sxl)
            )
    result = call(
        functools.partial(backward_last, plan),
        f32(field.shape),
        6 * count * plan.width,
        8 * field.size + table_x,
        [pltpu.VMEM(planes.shape, jnp.float32)],
        1,
        2 + groups + plan.chunks,
    )(ids, *pieces, sxh, sxl, *ready)
    return result[None]


def solution(mesh):
    spec = P("tm", None, "gy", None)

    def whole(residual):
        plan = Plan(mesh, residual.shape)
        plan.height = residual.shape[2]
        return jax.shard_map(
            functools.partial(on_device, plan),
            mesh=mesh,
            in_specs=(spec,),
            out_specs=spec,
            check_vma=False,
        )(residual)

    return whole
```

```python
import functools
import math

import jax
import jax.numpy as jnp
import numpy as np
from jax import lax
from jax.experimental import pallas as pl
from jax.experimental.pallas import tpu as pltpu
from jax.sharding import PartitionSpec as P

ALPHA_RATIO = 0.95
STEP_SCALE = 0.26
CHUNKS = (4, 4)
LANES = 128
STRIP = 16
VMEM_BYTES = 40 * 1024 * 1024


def sine_table(count):
    indices = np.arange(count, dtype=np.int64) + 1
    product = indices[:, None] * indices[None, :] % (2 * (count + 1))
    return math.sqrt(2.0 / (count + 1)) * np.sin(np.pi * product / (count + 1))


def spectrum_of(count):
    indices = np.arange(count, dtype=np.float64) + 1.0
    return 2.0 - 2.0 * np.cos(np.pi * indices / (count + 1))


def table_parts(table):
    table = table.astype(np.float32)
    high = table.astype(jnp.bfloat16)
    low = (table - high.astype(np.float32)).astype(jnp.bfloat16)
    return jnp.asarray(high), jnp.asarray(low)


def edge_responses(steps, depth, rows, width):
    freq = np.arange(steps // 2 + 1)
    turn = ALPHA_RATIO ** (1.0 / steps) * np.exp(-2j * np.pi * freq / steps)
    turn = turn[:, None, None]
    mu = spectrum_of(depth)[:, None] + spectrum_of(width)[None, :]
    scaled = STEP_SCALE * turn
    middle = ((1.0 - turn) ** 2 + scaled * (mu + 2.0)) / scaled
    root = np.sqrt(middle * middle / 4.0 - 1.0)
    ratio = middle / 2.0 - root
    ratio = np.where(np.abs(ratio) < 1.0, ratio, middle / 2.0 + root)
    bottom = 1.0 - ratio ** (2 * rows + 2)
    near = ratio * (1.0 - ratio ** (2 * rows)) / bottom
    far = ratio**rows * (1.0 - ratio * ratio) / bottom
    parts = np.stack([near.real, near.imag, far.real, far.imag], axis=1)
    return parts.astype(np.float32)


def parts_of(values):
    high = values.astype(jnp.bfloat16)
    return high, (values - high.astype(jnp.float32)).astype(jnp.bfloat16)


def dot(left, right):
    return jnp.dot(left, right, preferred_element_type=jnp.float32)


def dot_parts(left, right):
    return dot(left[0], right[0]) + dot(left[1], right[0]) + dot(left[0], right[1])


def call(kernel, out_shape, flops, args, scratch=()):
    smem = pl.BlockSpec(memory_space=pltpu.SMEM)
    vmem = pl.BlockSpec(memory_space=pltpu.VMEM)
    moved = sum(x.size * x.dtype.itemsize for x in args)
    return pl.pallas_call(
        kernel,
        out_shape=out_shape,
        in_specs=[smem] + [vmem] * (len(args) - 1),
        out_specs=jax.tree.map(lambda _: vmem, out_shape),
        scratch_shapes=scratch,
        compiler_params=pltpu.CompilerParams(vmem_limit_bytes=VMEM_BYTES),
        cost_estimate=pl.CostEstimate(
            flops=flops, bytes_accessed=moved, transcendentals=0
        ),
    )(*args)


class Plan:
    def __init__(self, mesh, shape):
        self.steps = mesh.shape["tm"]
        self.groups = mesh.shape["gy"]
        self.depth, self.width = shape[1], shape[3]
        self.rows = shape[2] // self.groups
        self.half = self.steps // 2
        self.block = self.width // self.half
        self.chunks = []
        first = 0
        for size in CHUNKS:
            size = min(size, self.depth - first)
            if size:
                self.chunks.append((first, size))
            first += size

    def columns(self, owner):
        return pl.ds(pl.multiple_of(owner * self.block, LANES), self.block)


def forward(plan, planes, ids, kzh, kzl, x, sxh, sxl, *outs):
    place = lax.rem(ids[0], plan.half)
    whole = parts_of(x[...].reshape(plan.depth * plan.rows, plan.width))
    left = parts_of(dot_parts((kzh[...], kzl[...]), whole))
    for k in range(plan.half):
        columns = plan.columns(place ^ k)
        value = dot_parts(left, (sxh[:, columns], sxl[:, columns]))
        outs[k][...] = value.reshape(planes, plan.rows, plan.block)


def backward(plan, planes, with_total, ids, kzh, kzl, sxh, sxl, *refs):
    place = lax.rem(ids[0], plan.half)
    pieces, out = refs[: plan.half], refs[-1]
    total = None
    for k in range(plan.half):
        at = plan.columns(place ^ k)
        piece = parts_of(pieces[k][...].reshape(planes * plan.rows, plan.block))
        value = dot_parts(piece, (sxh[at, :], sxl[at, :]))
        total = value if total is None else total + value
    value = dot_parts((kzh[...], kzl[...]), parts_of(total))
    value = value.reshape(plan.depth, plan.rows, plan.width)
    out[...] = refs[plan.half][...] + value if with_total else value


def per_strip(plan, first, planes, place, smu_z, smu_y, smu_x, edges, body):
    across = smu_x[:, plan.columns(place)]

    def step(index, carry):
        rows = pl.ds(pl.multiple_of(index * STRIP, STRIP), STRIP)
        plane = across + smu_y[rows, :]
        weights = edges[rows, 0:1], edges[rows, 1:2]
        for u in range(planes):
            body(u, rows, plane + smu_z[first + u : first + u + 1, :], weights)
        return carry

    lax.fori_loop(0, plan.rows // STRIP, step, 0)


class Cyclic:
    def __init__(self, smu, half):
        self.kappa = kappa = 2.0 - smu
        values = [jnp.zeros_like(kappa), jnp.ones_like(kappa)]
        for _ in range(half):
            values.append(kappa * values[-1] - values[-2])
        self.up, self.at, self.down = values[-1], values[-2], values[-3]
        det = (1.0 - ALPHA_RATIO) ** 2 + ALPHA_RATIO * (
            smu * (4.0 - smu) * (self.at * self.at)
        )
        inverse = 1.0 / det
        self.even = (0.5 * (1.0 - ALPHA_RATIO)) * (self.up - self.down) * inverse
        self.odd = (0.5 * (1.0 + ALPHA_RATIO)) * self.at * inverse

    def run(self, before, last, sources):
        values = []
        for source in sources:
            value = self.kappa * last - before
            before, last = last, value if source is None else value + source
            values.append(last)
        return before, last, values

    def start(self, sources):
        last = sources[0]
        before, last, _ = self.run(last, self.kappa * last + sources[1], sources[2:])
        return before, last

    def entry(self, p0, p1):
        return (
            self.even * p0 + self.odd * (2.0 * p1 - self.kappa * p0),
            self.even * p1 + self.odd * (self.kappa * p1 - 2.0 * p0),
        )

    def back(self, p0, p1):
        return self.up * p0 - self.at * p1, self.at * p0 - self.down * p1


def by_place(plan, place, body):
    for case in range(plan.half):
        pl.when(place == case)(functools.partial(body, case))


def half_end(plan, first, planes, ids, smu_z, smu_y, smu_x, edges, *refs):
    pieces = refs[: plan.half]
    ends, seen, sums = refs[plan.half :]
    steps, half = plan.steps, plan.half
    place = lax.rem(ids[0], half)
    mine = ids[0] // half
    leaving = jnp.where(mine == 0, 1.0, ALPHA_RATIO).astype(jnp.float32)
    sums[...] = jnp.zeros_like(sums)

    def with_place(case):
        def body(u, rows, smu, weights):
            cyclic = Cyclic(smu, half)
            sources = [pieces[case ^ j][u, rows, :] for j in range(half)]
            before, last = cyclic.start(sources)
            ends[0, u, rows, :] = before
            ends[1, u, rows, :] = last
            entry = cyclic.entry(ALPHA_RATIO * before, ALPHA_RATIO * last)
            before, last, own = cyclic.run(*entry, sources)
            _, _, other = cyclic.run(leaving * before, leaving * last, [None] * half)
            for values, window in ((own, mine), (other, 1 - mine)):
                for j, value in enumerate(values):
                    for edge in range(2):
                        term = weights[edge] * value
                        term = sum(term[i : i + 8] for i in range(0, STRIP, 8))
                        sums[2 * (window * half + j) + edge, u] += term

        per_strip(plan, first, planes, place, smu_z, smu_y, smu_x, edges, body)

    by_place(plan, place, with_place)
    seen[...] = jnp.sum(sums[...], axis=2)


def c_mul(a, b):
    return a[0] * b[0] - a[1] * b[1], a[0] * b[1] + a[1] * b[0]


def c_add(a, b):
    return a[0] + b[0], a[1] + b[1]


def c_gap(a, b):
    product = c_mul(a, b)
    real, imag = 1.0 - product[0], -product[1]
    inverse = 1.0 / (real * real + imag * imag)
    return real * inverse, -imag * inverse


def join_rows(plan, first, planes, ids, responses, *refs):
    groups, steps = plan.groups, plan.steps
    views = refs[:groups]
    out, seen, above, below = refs[groups:]
    place = lax.rem(ids[0], plan.half)
    me = ids[1]
    columns = plan.columns(place)
    for k in range(groups):
        seen[me ^ k] = views[k][...]
    radius = ALPHA_RATIO ** (1.0 / steps)
    grow = [radius**n for n in range(steps)]
    nothing = jnp.zeros((planes, plan.block), jnp.float32)
    for freq in range(steps // 2 + 1):
        angle = [2.0 * math.pi * (freq * n % steps) / steps for n in range(steps)]

        def spectrum(block, edge):
            real, imag = nothing, nothing
            for n in range(steps):
                value = seen[block, 2 * n + edge]
                real = real + value * np.float32(grow[n] * math.cos(angle[n]))
                if freq % (steps // 2):
                    imag = imag - value * np.float32(grow[n] * math.sin(angle[n]))
            return real, imag

        head = [spectrum(block, 0) for block in range(groups)]
        tail = [spectrum(block, 1) for block in range(groups)]
        near, far = (
            tuple(
                responses[freq, 2 * kind + part, first : first + planes, columns]
                for part in range(2)
            )
            for kind in range(2)
        )
        square = c_mul(far, far)
        gammas, downs, ups = [near], [tail[0]], [head[groups - 1]]
        for d in range(1, groups - 1):
            gamma = gammas[-1]
            gap = c_gap(gamma, near)
            through = c_mul(far, gap)
            e = groups - 1 - d
            downs.append(
                c_add(
                    tail[d], c_mul(through, c_add(downs[-1], c_mul(gamma, head[d])))
                )
            )
            ups.append(
                c_add(head[e], c_mul(through, c_add(ups[-1], c_mul(gamma, tail[e]))))
            )
            gammas.append(c_add(near, c_mul(square, c_mul(gamma, gap))))
        for d in range(groups - 1):
            down, up = downs[d], ups[groups - 2 - d]
            from_top, from_end = gammas[d], gammas[groups - 2 - d]
            gap = c_gap(from_top, from_end)
            last = c_mul(c_add(down, c_mul(from_top, up)), gap)
            start = c_mul(c_add(up, c_mul(from_end, down)), gap)
            for part in range(2):
                above[d + 1, 2 * freq + part] = last[part]
                below[d, 2 * freq + part] = start[part]
        for part in range(2):
            above[0, 2 * freq + part] = nothing
            below[groups - 1, 2 * freq + part] = nothing
    for edge, side in enumerate((above, below)):
        parts = [side[me, i] for i in range(steps + 2)]
        for n in range(steps):
            total = nothing
            shrink = STEP_SCALE / (steps * grow[n])
            if n == steps - 1:
                shrink *= ALPHA_RATIO
            for freq in range(steps // 2 + 1):
                angle = 2.0 * math.pi * (freq * n % steps) / steps
                single = freq % (steps // 2) == 0
                weight = shrink if single else 2.0 * shrink
                total = total + parts[2 * freq] * np.float32(weight * math.cos(angle))
                if not single:
                    total = total - parts[2 * freq + 1] * np.float32(
                        weight * math.sin(angle)
                    )
            out[2 * ((n + 1) % steps) + edge] = total


def half_solve(plan, first, planes, ids, smu_z, smu_y, smu_x, edges, *refs):
    pieces = refs[: plan.half]
    far, beside, beside_far = refs[plan.half : plan.half + 3]
    outs = refs[plan.half + 3 :]
    half = plan.half
    place = lax.rem(ids[0], half)
    mine = ids[0] // half
    entering = jnp.where(mine == 0, ALPHA_RATIO, 1.0).astype(jnp.float32)

    def with_place(case):
        def body(u, rows, smu, weights):
            cyclic = Cyclic(smu, half)

            def source(window, j):
                total = None
                for edge in range(2):
                    at = 2 * (window * half + j) + edge
                    row = beside[at, u : u + 1, :] + beside_far[at, u : u + 1, :]
                    term = weights[edge] * row
                    total = term if total is None else total + term
                return total

            own = [pieces[case ^ j][u, rows, :] + source(mine, j) for j in range(half)]
            other = [source(1 - mine, j) for j in range(half)]
            before, last = cyclic.start(other)
            before = entering * (before + far[0, u, rows, :])
            last = entering * (last + far[1, u, rows, :])
            before, last = cyclic.back(before, last)
            near = cyclic.start(own)
            entry = cyclic.entry(
                before + ALPHA_RATIO * near[0], last + ALPHA_RATIO * near[1]
            )
            _, _, values = cyclic.run(*entry, own)
            for j, value in enumerate(values):
                outs[case ^ j][u, rows, :] = value

        per_strip(plan, first, planes, place, smu_z, smu_y, smu_x, edges, body)

    by_place(plan, place, with_place)


def swap(values, axis, count, distance):
    if distance == 0:
        return values
    return lax.ppermute(values, axis, [(i, i ^ distance) for i in range(count)])


def on_device(plan, residual):
    steps, groups, half = plan.steps, plan.groups, plan.half
    ids = jnp.stack([lax.axis_index("tm"), lax.axis_index("gy")]).astype(jnp.int32)
    sine_rows = sine_table(plan.rows)
    sxh, sxl = table_parts(sine_table(plan.width))
    both = np.kron(sine_table(plan.depth), sine_rows)
    smu_z, smu_y, smu_x = (
        jnp.asarray(STEP_SCALE * spectrum_of(count).reshape(shape), jnp.float32)
        for count, shape in (
            (plan.depth, (-1, 1)),
            (plan.rows, (-1, 1)),
            (plan.width, (1, -1)),
        )
    )
    edges = jnp.asarray(sine_rows[:, [0, plan.rows - 1]], jnp.float32)
    responses = jnp.asarray(edge_responses(steps, plan.depth, plan.rows, plan.width))
    field = residual[0]
    f32 = functools.partial(jax.ShapeDtypeStruct, dtype=jnp.float32)
    total = None
    for first, planes in plan.chunks:
        modes = f32((planes, plan.rows, plan.block))
        ends = f32((2,) + modes.shape)
        seen = f32((2 * steps, planes, plan.block))
        count = planes * plan.rows * plan.width
        flops = 6 * count * (plan.width + plan.depth * plan.rows)
        span = slice(first * plan.rows, (first + planes) * plan.rows)
        small = (smu_z, smu_y, smu_x, edges)
        pieces = call(
            functools.partial(forward, plan, planes),
            [modes] * half,
            flops,
            (ids, *table_parts(both[span]), field, sxh, sxl),
        )
        pieces = [swap(v, "tm", steps, k) for k, v in enumerate(pieces)]
        mine, view = call(
            functools.partial(half_end, plan, first, planes),
            [ends, seen],
            100 * count,
            (ids, *small, *pieces),
            [pltpu.VMEM((2 * steps, planes, 8, plan.block), jnp.float32)],
        )
        far = swap(mine, "tm", steps, half)
        views = [swap(view, "gy", groups, k) for k in range(groups)]
        sides = pltpu.VMEM((groups, steps + 2, planes, plan.block), jnp.float32)
        beside = call(
            functools.partial(join_rows, plan, first, planes),
            seen,
            100 * count // plan.rows,
            (ids, responses, *views),
            [pltpu.VMEM((groups,) + seen.shape, jnp.float32), sides, sides],
        )
        beside_far = swap(beside, "tm", steps, half)
        pieces = call(
            functools.partial(half_solve, plan, first, planes),
            [modes] * half,
            100 * count,
            (ids, *small, *pieces, far, beside, beside_far),
        )
        pieces = [swap(v, "tm", steps, k) for k, v in enumerate(pieces)]
        ready = () if total is None else (total,)
        total = call(
            functools.partial(backward, plan, planes, total is not None),
            f32(field.shape),
            flops,
            (ids, *table_parts(both[:, span]), sxh, sxl, *pieces, *ready),
        )
    return total[None]


def solution(mesh):
    spec = P("tm", None, "gy", None)

    def whole(residual):
        plan = Plan(mesh, residual.shape)
        return jax.shard_map(
            functools.partial(on_device, plan),
            mesh=mesh,
            in_specs=(spec,),
            out_specs=spec,
            check_vma=False,
        )(residual)

    return whole
```

```python
import functools
import math

import jax
import jax.numpy as jnp
import numpy as np
from jax import lax
from jax.experimental import pallas as pl
from jax.experimental.pallas import tpu as pltpu
from jax.sharding import PartitionSpec as P

ALPHA_RATIO = 0.95
STEP_SCALE = 0.26
CHUNKS = (2, 4, 2)
LANES = 128
STRIP = 16
VMEM_BYTES = 40 * 1024 * 1024


def sine_table(count):
    indices = np.arange(count, dtype=np.int64) + 1
    product = indices[:, None] * indices[None, :] % (2 * (count + 1))
    return math.sqrt(2.0 / (count + 1)) * np.sin(np.pi * product / (count + 1))


def spectrum_of(count):
    indices = np.arange(count, dtype=np.float64) + 1.0
    return 2.0 - 2.0 * np.cos(np.pi * indices / (count + 1))


def table_parts(table):
    table = table.astype(np.float32)
    high = table.astype(jnp.bfloat16)
    low = (table - high.astype(np.float32)).astype(jnp.bfloat16)
    return jnp.asarray(high), jnp.asarray(low)


def edge_responses(steps, depth, rows, width):
    freq = np.arange(steps // 2 + 1)
    turn = ALPHA_RATIO ** (1.0 / steps) * np.exp(-2j * np.pi * freq / steps)
    turn = turn[:, None, None]
    mu = spectrum_of(depth)[:, None] + spectrum_of(width)[None, :]
    scaled = STEP_SCALE * turn
    middle = ((1.0 - turn) ** 2 + scaled * (mu + 2.0)) / scaled
    root = np.sqrt(middle * middle / 4.0 - 1.0)
    ratio = middle / 2.0 - root
    ratio = np.where(np.abs(ratio) < 1.0, ratio, middle / 2.0 + root)
    bottom = 1.0 - ratio ** (2 * rows + 2)
    near = ratio * (1.0 - ratio ** (2 * rows)) / bottom
    far = ratio**rows * (1.0 - ratio * ratio) / bottom
    parts = np.stack([near.real, near.imag, far.real, far.imag], axis=1)
    return parts.astype(np.float32)


def parts_of(values):
    high = values.astype(jnp.bfloat16)
    return high, (values - high.astype(jnp.float32)).astype(jnp.bfloat16)


def dot(left, right):
    return jnp.dot(left, right, preferred_element_type=jnp.float32)


def dot_parts(left, right):
    return dot(left[0], right[0]) + dot(left[1], right[0]) + dot(left[0], right[1])


def call(kernel, out_shape, flops, args, scratch=(), stay=()):
    smem = pl.BlockSpec(memory_space=pltpu.SMEM)
    vmem = pl.BlockSpec(memory_space=pltpu.VMEM)
    hbm = pl.BlockSpec(memory_space=pl.ANY)
    moved = sum(x.size * x.dtype.itemsize for x in args)
    return pl.pallas_call(
        kernel,
        out_shape=out_shape,
        in_specs=[smem] + [hbm if i in stay else vmem for i in range(1, len(args))],
        out_specs=jax.tree.map(lambda _: vmem, out_shape),
        scratch_shapes=scratch,
        compiler_params=pltpu.CompilerParams(vmem_limit_bytes=VMEM_BYTES),
        cost_estimate=pl.CostEstimate(
            flops=flops, bytes_accessed=moved, transcendentals=0
        ),
    )(*args)


class Plan:
    def __init__(self, mesh, shape):
        self.steps = mesh.shape["tm"]
        self.groups = mesh.shape["gy"]
        self.depth, self.width = shape[1], shape[3]
        self.rows = shape[2] // self.groups
        self.half = self.steps // 2
        self.block = self.width // self.half
        self.chunks = []
        first = 0
        for size in CHUNKS:
            size = min(size, self.depth - first)
            if size:
                self.chunks.append((first, size))
            first += size

    def columns(self, owner):
        return pl.ds(pl.multiple_of(owner * self.block, LANES), self.block)


def forward(plan, planes, ids, kzh, kzl, x, sxh, sxl, *refs):
    place = lax.rem(ids[0], plan.half)
    outs, fetched = refs[: plan.half], refs[plan.half :]
    if fetched:
        x_all, sxh_all, sxl_all, arrived = fetched
        copies = [pltpu.make_async_copy(x, x_all, arrived.at[0])]
        for k in range(plan.half):
            for part, (table, held) in enumerate(((sxh, sxh_all), (sxl, sxl_all))):
                columns = plan.columns(place ^ k)
                copies.append(
                    pltpu.make_async_copy(
                        table.at[:, columns],
                        held.at[:, columns],
                        arrived.at[1 + 2 * k + part],
                    )
                )
        for copy in copies:
            copy.start()
        copies[0].wait()
        x, sxh, sxl = x_all, sxh_all, sxl_all
    whole = parts_of(x[...].reshape(plan.depth * plan.rows, plan.width))
    left = parts_of(dot_parts((kzh[...], kzl[...]), whole))
    for k in range(plan.half):
        if fetched:
            copies[1 + 2 * k].wait()
            copies[2 + 2 * k].wait()
        columns = plan.columns(place ^ k)
        value = dot_parts(left, (sxh[:, columns], sxl[:, columns]))
        outs[k][...] = value.reshape(planes, plan.rows, plan.block)


def backward(plan, planes, with_total, ids, kzh, kzl, sxh, sxl, *refs):
    place = lax.rem(ids[0], plan.half)
    pieces, out = refs[: plan.half], refs[-1]
    total = None
    for k in range(plan.half):
        at = plan.columns(place ^ k)
        piece = parts_of(pieces[k][...].reshape(planes * plan.rows, plan.block))
        value = dot_parts(piece, (sxh[at, :], sxl[at, :]))
        total = value if total is None else total + value
    value = dot_parts((kzh[...], kzl[...]), parts_of(total))
    value = value.reshape(plan.depth, plan.rows, plan.width)
    out[...] = refs[plan.half][...] + value if with_total else value


def per_strip(plan, first, planes, place, smu_z, smu_y, smu_x, edges, body):
    across = smu_x[:, plan.columns(place)]

    def step(index, carry):
        rows = pl.ds(pl.multiple_of(index * STRIP, STRIP), STRIP)
        plane = across + smu_y[rows, :]
        weights = edges[rows, 0:1], edges[rows, 1:2]
        for u in range(planes):
            body(u, rows, plane + smu_z[first + u : first + u + 1, :], weights)
        return carry

    lax.fori_loop(0, plan.rows // STRIP, step, 0)


class Cyclic:
    def __init__(self, smu, half):
        self.kappa = kappa = 2.0 - smu
        values = [jnp.zeros_like(kappa), jnp.ones_like(kappa)]
        for _ in range(half):
            values.append(kappa * values[-1] - values[-2])
        self.up, self.at, self.down = values[-1], values[-2], values[-3]
        det = (1.0 - ALPHA_RATIO) ** 2 + ALPHA_RATIO * (
            smu * (4.0 - smu) * (self.at * self.at)
        )
        inverse = 1.0 / det
        self.even = (0.5 * (1.0 - ALPHA_RATIO)) * (self.up - self.down) * inverse
        self.odd = (0.5 * (1.0 + ALPHA_RATIO)) * self.at * inverse

    def run(self, before, last, sources):
        values = []
        for source in sources:
            value = self.kappa * last - before
            before, last = last, value if source is None else value + source
            values.append(last)
        return before, last, values

    def start(self, sources):
        last = sources[0]
        before, last, _ = self.run(last, self.kappa * last + sources[1], sources[2:])
        return before, last

    def entry(self, p0, p1):
        return (
            self.even * p0 + self.odd * (2.0 * p1 - self.kappa * p0),
            self.even * p1 + self.odd * (self.kappa * p1 - 2.0 * p0),
        )

    def back(self, p0, p1):
        return self.up * p0 - self.at * p1, self.at * p0 - self.down * p1


def by_place(plan, place, body):
    for case in range(plan.half):
        pl.when(place == case)(functools.partial(body, case))


def half_end(plan, first, planes, ids, smu_z, smu_y, smu_x, edges, *refs):
    pieces = refs[: plan.half]
    ends, seen, sums = refs[plan.half :]
    steps, half = plan.steps, plan.half
    place = lax.rem(ids[0], half)
    mine = ids[0] // half
    leaving = jnp.where(mine == 0, 1.0, ALPHA_RATIO).astype(jnp.float32)
    sums[...] = jnp.zeros_like(sums)

    def with_place(case):
        def body(u, rows, smu, weights):
            cyclic = Cyclic(smu, half)
            sources = [pieces[case ^ j][u, rows, :] for j in range(half)]
            before, last = cyclic.start(sources)
            ends[0, u, rows, :] = before
            ends[1, u, rows, :] = last
            entry = cyclic.entry(ALPHA_RATIO * before, ALPHA_RATIO * last)
            before, last, own = cyclic.run(*entry, sources)
            _, _, other = cyclic.run(leaving * before, leaving * last, [None] * half)
            for values, window in ((own, mine), (other, 1 - mine)):
                for j, value in enumerate(values):
                    for edge in range(2):
                        term = weights[edge] * value
                        term = sum(term[i : i + 8] for i in range(0, STRIP, 8))
                        sums[2 * (window * half + j) + edge, u] += term

        per_strip(plan, first, planes, place, smu_z, smu_y, smu_x, edges, body)

    by_place(plan, place, with_place)
    seen[...] = jnp.sum(sums[...], axis=2)


def c_mul(a, b):
    return a[0] * b[0] - a[1] * b[1], a[0] * b[1] + a[1] * b[0]


def c_add(a, b):
    return a[0] + b[0], a[1] + b[1]


def c_gap(a, b):
    product = c_mul(a, b)
    real, imag = 1.0 - product[0], -product[1]
    inverse = 1.0 / (real * real + imag * imag)
    return real * inverse, -imag * inverse


def join_rows(plan, first, planes, ids, responses, *refs):
    groups, steps = plan.groups, plan.steps
    views = refs[:groups]
    out, seen, above, below = refs[groups:]
    place = lax.rem(ids[0], plan.half)
    me = ids[1]
    columns = plan.columns(place)
    for k in range(groups):
        seen[me ^ k] = views[k][...]
    radius = ALPHA_RATIO ** (1.0 / steps)
    grow = [radius**n for n in range(steps)]
    nothing = jnp.zeros((planes, plan.block), jnp.float32)
    for freq in range(steps // 2 + 1):
        angle = [2.0 * math.pi * (freq * n % steps) / steps for n in range(steps)]

        def spectrum(block, edge):
            real, imag = nothing, nothing
            for n in range(steps):
                value = seen[block, 2 * n + edge]
                real = real + value * np.float32(grow[n] * math.cos(angle[n]))
                if freq % (steps // 2):
                    imag = imag - value * np.float32(grow[n] * math.sin(angle[n]))
            return real, imag

        head = [spectrum(block, 0) for block in range(groups)]
        tail = [spectrum(block, 1) for block in range(groups)]
        near, far = (
            tuple(
                responses[freq, 2 * kind + part, first : first + planes, columns]
                for part in range(2)
            )
            for kind in range(2)
        )
        square = c_mul(far, far)
        gammas, downs, ups = [near], [tail[0]], [head[groups - 1]]
        for d in range(1, groups - 1):
            gamma = gammas[-1]
            gap = c_gap(gamma, near)
            through = c_mul(far, gap)
            e = groups - 1 - d
            downs.append(
                c_add(
                    tail[d], c_mul(through, c_add(downs[-1], c_mul(gamma, head[d])))
                )
            )
            ups.append(
                c_add(head[e], c_mul(through, c_add(ups[-1], c_mul(gamma, tail[e]))))
            )
            gammas.append(c_add(near, c_mul(square, c_mul(gamma, gap))))
        for d in range(groups - 1):
            down, up = downs[d], ups[groups - 2 - d]
            from_top, from_end = gammas[d], gammas[groups - 2 - d]
            gap = c_gap(from_top, from_end)
            last = c_mul(c_add(down, c_mul(from_top, up)), gap)
            start = c_mul(c_add(up, c_mul(from_end, down)), gap)
            for part in range(2):
                above[d + 1, 2 * freq + part] = last[part]
                below[d, 2 * freq + part] = start[part]
        for part in range(2):
            above[0, 2 * freq + part] = nothing
            below[groups - 1, 2 * freq + part] = nothing
    for edge, side in enumerate((above, below)):
        parts = [side[me, i] for i in range(steps + 2)]
        for n in range(steps):
            total = nothing
            shrink = STEP_SCALE / (steps * grow[n])
            if n == steps - 1:
                shrink *= ALPHA_RATIO
            for freq in range(steps // 2 + 1):
                angle = 2.0 * math.pi * (freq * n % steps) / steps
                single = freq % (steps // 2) == 0
                weight = shrink if single else 2.0 * shrink
                total = total + parts[2 * freq] * np.float32(weight * math.cos(angle))
                if not single:
                    total = total - parts[2 * freq + 1] * np.float32(
                        weight * math.sin(angle)
                    )
            out[2 * ((n + 1) % steps) + edge] = total


def half_solve(plan, first, planes, ids, smu_z, smu_y, smu_x, edges, *refs):
    pieces = refs[: plan.half]
    far, beside, beside_far = refs[plan.half : plan.half + 3]
    outs = refs[plan.half + 3 :]
    half = plan.half
    place = lax.rem(ids[0], half)
    mine = ids[0] // half
    entering = jnp.where(mine == 0, ALPHA_RATIO, 1.0).astype(jnp.float32)

    def with_place(case):
        def body(u, rows, smu, weights):
            cyclic = Cyclic(smu, half)

            def source(window, j):
                total = None
                for edge in range(2):
                    at = 2 * (window * half + j) + edge
                    row = beside[at, u : u + 1, :] + beside_far[at, u : u + 1, :]
                    term = weights[edge] * row
                    total = term if total is None else total + term
                return total

            own = [pieces[case ^ j][u, rows, :] + source(mine, j) for j in range(half)]
            other = [source(1 - mine, j) for j in range(half)]
            before, last = cyclic.start(other)
            before = entering * (before + far[0, u, rows, :])
            last = entering * (last + far[1, u, rows, :])
            before, last = cyclic.back(before, last)
            near = cyclic.start(own)
            entry = cyclic.entry(
                before + ALPHA_RATIO * near[0], last + ALPHA_RATIO * near[1]
            )
            _, _, values = cyclic.run(*entry, own)
            for j, value in enumerate(values):
                outs[case ^ j][u, rows, :] = value

        per_strip(plan, first, planes, place, smu_z, smu_y, smu_x, edges, body)

    by_place(plan, place, with_place)


def swap(values, axis, count, distance):
    if distance == 0:
        return values
    return lax.ppermute(values, axis, [(i, i ^ distance) for i in range(count)])


def on_device(plan, residual):
    steps, groups, half = plan.steps, plan.groups, plan.half
    ids = jnp.stack([lax.axis_index("tm"), lax.axis_index("gy")]).astype(jnp.int32)
    sine_rows = sine_table(plan.rows)
    sxh, sxl = table_parts(sine_table(plan.width))
    both = np.kron(sine_table(plan.depth), sine_rows)
    smu_z, smu_y, smu_x = (
        jnp.asarray(STEP_SCALE * spectrum_of(count).reshape(shape), jnp.float32)
        for count, shape in (
            (plan.depth, (-1, 1)),
            (plan.rows, (-1, 1)),
            (plan.width, (1, -1)),
        )
    )
    edges = jnp.asarray(sine_rows[:, [0, plan.rows - 1]], jnp.float32)
    responses = jnp.asarray(edge_responses(steps, plan.depth, plan.rows, plan.width))
    field = residual[0]
    f32 = functools.partial(jax.ShapeDtypeStruct, dtype=jnp.float32)
    held = [
        pltpu.VMEM(field.shape, jnp.float32),
        pltpu.VMEM(sxh.shape, sxh.dtype),
        pltpu.VMEM(sxl.shape, sxl.dtype),
        pltpu.SemaphoreType.DMA((1 + 2 * half,)),
    ]
    total = beside = None
    for first, planes in plan.chunks:
        modes = f32((planes, plan.rows, plan.block))
        ends = f32((2,) + modes.shape)
        seen = f32((2 * steps, planes, plan.block))
        count = planes * plan.rows * plan.width
        flops = 6 * count * (plan.width + plan.depth * plan.rows)
        span = slice(first * plan.rows, (first + planes) * plan.rows)
        small = (smu_z, smu_y, smu_x, edges)
        pieces = call(
            functools.partial(forward, plan, planes),
            [modes] * half,
            flops,
            (ids, *table_parts(both[span]), field, sxh, sxl),
            held if beside is None else (),
            (3, 4, 5) if beside is None else (),
        )
        pieces = [swap(v, "tm", steps, k) for k, v in enumerate(pieces)]
        if beside is not None:
            beside, *pieces = lax.optimization_barrier((beside, *pieces))
        mine, view = call(
            functools.partial(half_end, plan, first, planes),
            [ends, seen],
            100 * count,
            (ids, *small, *pieces),
            [pltpu.VMEM((2 * steps, planes, 8, plan.block), jnp.float32)],
        )
        far = swap(mine, "tm", steps, half)
        views = [swap(view, "gy", groups, k) for k in range(groups)]
        sides = pltpu.VMEM((groups, steps + 2, planes, plan.block), jnp.float32)
        beside = call(
            functools.partial(join_rows, plan, first, planes),
            seen,
            100 * count // plan.rows,
            (ids, responses, *views),
            [pltpu.VMEM((groups,) + seen.shape, jnp.float32), sides, sides],
        )
        beside_far = swap(beside, "tm", steps, half)
        pieces = call(
            functools.partial(half_solve, plan, first, planes),
            [modes] * half,
            100 * count,
            (ids, *small, *pieces, far, beside, beside_far),
        )
        pieces = [swap(v, "tm", steps, k) for k, v in enumerate(pieces)]
        ready = () if total is None else (total,)
        total = call(
            functools.partial(backward, plan, planes, total is not None),
            f32(field.shape),
            flops,
            (ids, *table_parts(both[:, span]), sxh, sxl, *pieces, *ready),
        )
    return total[None]


def solution(mesh):
    spec = P("tm", None, "gy", None)

    def whole(residual):
        plan = Plan(mesh, residual.shape)
        return jax.shard_map(
            functools.partial(on_device, plan),
            mesh=mesh,
            in_specs=(spec,),
            out_specs=spec,
            check_vma=False,
        )(residual)

    return whole
```

```python
import functools
import math

import jax
import jax.numpy as jnp
import numpy as np
from jax import lax
from jax.experimental import pallas as pl
from jax.experimental.pallas import tpu as pltpu
from jax.sharding import PartitionSpec as P

ALPHA_RATIO = 0.95
STEP_SCALE = 0.26
CHUNKS = (4, 4)
LANES = 128
STRIP = 16
VMEM_BYTES = 40 * 1024 * 1024
ALL_VMEM = 60 * 1024 * 1024


def sine_table(count):
    indices = np.arange(count, dtype=np.int64) + 1
    product = indices[:, None] * indices[None, :] % (2 * (count + 1))
    return math.sqrt(2.0 / (count + 1)) * np.sin(np.pi * product / (count + 1))


def spectrum_of(count):
    indices = np.arange(count, dtype=np.float64) + 1.0
    return 2.0 - 2.0 * np.cos(np.pi * indices / (count + 1))


def table_parts(table):
    table = table.astype(np.float32)
    high = table.astype(jnp.bfloat16)
    low = (table - high.astype(np.float32)).astype(jnp.bfloat16)
    return jnp.asarray(high), jnp.asarray(low)


def edge_responses(steps, depth, rows, width):
    freq = np.arange(steps // 2 + 1)
    turn = ALPHA_RATIO ** (1.0 / steps) * np.exp(-2j * np.pi * freq / steps)
    turn = turn[:, None, None]
    mu = spectrum_of(depth)[:, None] + spectrum_of(width)[None, :]
    scaled = STEP_SCALE * turn
    middle = ((1.0 - turn) ** 2 + scaled * (mu + 2.0)) / scaled
    root = np.sqrt(middle * middle / 4.0 - 1.0)
    ratio = middle / 2.0 - root
    ratio = np.where(np.abs(ratio) < 1.0, ratio, middle / 2.0 + root)
    bottom = 1.0 - ratio ** (2 * rows + 2)
    near = ratio * (1.0 - ratio ** (2 * rows)) / bottom
    far = ratio**rows * (1.0 - ratio * ratio) / bottom
    parts = np.stack([near.real, near.imag, far.real, far.imag], axis=1)
    return parts.astype(np.float32)


def parts_of(values):
    high = values.astype(jnp.bfloat16)
    return high, (values - high.astype(jnp.float32)).astype(jnp.bfloat16)


def dot(left, right):
    return jnp.dot(left, right, preferred_element_type=jnp.float32)


def dot_parts(left, right):
    return dot(left[0], right[0]) + dot(left[1], right[0]) + dot(left[0], right[1])


def call(
    kernel, out_shape, flops, args, scratch=(), specs=None, grid=(), out=None, room=None
):
    smem = pl.BlockSpec(memory_space=pltpu.SMEM)
    vmem = pl.BlockSpec(memory_space=pltpu.VMEM)
    specs = specs or {}
    moved = sum(x.size * x.dtype.itemsize for x in args)
    return pl.pallas_call(
        kernel,
        grid=grid,
        out_shape=out_shape,
        in_specs=[smem] + [specs.get(i, vmem) for i in range(1, len(args))],
        out_specs=out or jax.tree.map(lambda _: vmem, out_shape),
        scratch_shapes=scratch,
        compiler_params=pltpu.CompilerParams(vmem_limit_bytes=room or VMEM_BYTES),
        cost_estimate=pl.CostEstimate(
            flops=flops, bytes_accessed=moved, transcendentals=0
        ),
    )(*args)


class Plan:
    def __init__(self, mesh, shape):
        self.steps = mesh.shape["tm"]
        self.groups = mesh.shape["gy"]
        self.depth, self.width = shape[1], shape[3]
        self.rows = shape[2] // self.groups
        self.half = self.steps // 2
        self.block = self.width // self.half
        self.chunks = []
        first = 0
        for size in CHUNKS:
            size = min(size, self.depth - first)
            if size:
                self.chunks.append((first, size))
            first += size

    def columns(self, owner):
        return pl.ds(pl.multiple_of(owner * self.block, LANES), self.block)


def forward(plan, planes, ids, kzh, kzl, x, sxh, sxl, *refs):
    place = lax.rem(ids[0], plan.half)
    outs = refs[: plan.half]
    x_all, high, low, arrived = refs[plan.half :]
    parts = x_all.shape[0]
    deep = plan.depth // parts
    fields = [
        pltpu.make_async_copy(x.at[pl.ds(i * deep, deep)], x_all.at[i], arrived.at[i])
        for i in range(parts)
    ]
    tables = []
    for k in range(plan.half):
        columns = plan.columns(place ^ k)
        tables.append(
            [
                pltpu.make_async_copy(
                    table.at[:, columns], held.at[k], arrived.at[parts + 2 * k + i]
                )
                for i, (table, held) in enumerate(((sxh, high), (sxl, low)))
            ]
        )
    for copy in fields + sum(tables, []):
        copy.start()
    total = None
    for i in range(parts):
        fields[i].wait()
        field = parts_of(x_all[i].reshape(deep * plan.rows, plan.width))
        span = slice(i * deep * plan.rows, (i + 1) * deep * plan.rows)
        value = dot_parts((kzh[:, span], kzl[:, span]), field)
        total = value if total is None else total + value
    left = parts_of(total)
    for k in range(plan.half):
        for copy in tables[k]:
            copy.wait()
        value = dot_parts(left, (high[k], low[k]))
        outs[k][...] = value.reshape(planes, plan.rows, plan.block)


def backward(plan, planes, with_total, ids, kzh, kzl, sxh, sxl, *refs):
    place = lax.rem(ids[0], plan.half)
    pieces = refs[: plan.half]
    out, high, low = refs[-3:]

    @pl.when(pl.program_id(0) == 0)
    def _():
        for k in range(plan.half):
            columns = plan.columns(place ^ k)
            piece = pieces[k][...].reshape(planes * plan.rows, plan.block)
            high[:, columns], low[:, columns] = parts_of(piece)

    total = dot_parts((high[...], low[...]), (sxh[...], sxl[...]))
    value = dot_parts((kzh[...], kzl[...]), parts_of(total))
    value = value.reshape(out.shape)
    out[...] = refs[plan.half][...] + value if with_total else value


def per_strip(plan, first, planes, place, smu_z, smu_y, smu_x, edges, body):
    across = smu_x[:, plan.columns(place)]

    def step(index, carry):
        rows = pl.ds(pl.multiple_of(index * STRIP, STRIP), STRIP)
        plane = across + smu_y[rows, :]
        weights = edges[rows, 0:1], edges[rows, 1:2]
        for u in range(planes):
            body(u, rows, plane + smu_z[first + u : first + u + 1, :], weights)
        return carry

    lax.fori_loop(0, plan.rows // STRIP, step, 0)


class Cyclic:
    def __init__(self, smu, half):
        self.kappa = kappa = 2.0 - smu
        values = [jnp.zeros_like(kappa), jnp.ones_like(kappa)]
        for _ in range(half):
            values.append(kappa * values[-1] - values[-2])
        self.up, self.at, self.down = values[-1], values[-2], values[-3]
        det = (1.0 - ALPHA_RATIO) ** 2 + ALPHA_RATIO * (
            smu * (4.0 - smu) * (self.at * self.at)
        )
        inverse = 1.0 / det
        self.even = (0.5 * (1.0 - ALPHA_RATIO)) * (self.up - self.down) * inverse
        self.odd = (0.5 * (1.0 + ALPHA_RATIO)) * self.at * inverse

    def run(self, before, last, sources):
        values = []
        for source in sources:
            value = self.kappa * last - before
            before, last = last, value if source is None else value + source
            values.append(last)
        return before, last, values

    def start(self, sources):
        last = sources[0]
        before, last, _ = self.run(last, self.kappa * last + sources[1], sources[2:])
        return before, last

    def entry(self, p0, p1):
        return (
            self.even * p0 + self.odd * (2.0 * p1 - self.kappa * p0),
            self.even * p1 + self.odd * (self.kappa * p1 - 2.0 * p0),
        )

    def back(self, p0, p1):
        return self.up * p0 - self.at * p1, self.at * p0 - self.down * p1


def by_place(plan, place, body):
    for case in range(plan.half):
        pl.when(place == case)(functools.partial(body, case))


def half_end(plan, first, planes, ids, smu_z, smu_y, smu_x, edges, *refs):
    pieces = refs[: plan.half]
    ends, seen, sums = refs[plan.half :]
    steps, half = plan.steps, plan.half
    place = lax.rem(ids[0], half)
    mine = ids[0] // half
    leaving = jnp.where(mine == 0, 1.0, ALPHA_RATIO).astype(jnp.float32)
    sums[...] = jnp.zeros_like(sums)

    def with_place(case):
        def body(u, rows, smu, weights):
            cyclic = Cyclic(smu, half)
            sources = [pieces[case ^ j][u, rows, :] for j in range(half)]
            before, last = cyclic.start(sources)
            ends[0, u, rows, :] = before
            ends[1, u, rows, :] = last
            entry = cyclic.entry(ALPHA_RATIO * before, ALPHA_RATIO * last)
            before, last, own = cyclic.run(*entry, sources)
            _, _, other = cyclic.run(leaving * before, leaving * last, [None] * half)
            for values, window in ((own, mine), (other, 1 - mine)):
                for j, value in enumerate(values):
                    for edge in range(2):
                        term = weights[edge] * value
                        term = sum(term[i : i + 8] for i in range(0, STRIP, 8))
                        sums[2 * (window * half + j) + edge, u] += term

        per_strip(plan, first, planes, place, smu_z, smu_y, smu_x, edges, body)

    by_place(plan, place, with_place)
    seen[...] = jnp.sum(sums[...], axis=2)


def c_mul(a, b):
    return a[0] * b[0] - a[1] * b[1], a[0] * b[1] + a[1] * b[0]


def c_add(a, b):
    return a[0] + b[0], a[1] + b[1]


def c_gap(a, b):
    product = c_mul(a, b)
    real, imag = 1.0 - product[0], -product[1]
    inverse = 1.0 / (real * real + imag * imag)
    return real * inverse, -imag * inverse


def join_rows(plan, first, planes, ids, responses, *refs):
    groups, steps = plan.groups, plan.steps
    views = refs[:groups]
    out, seen, above, below = refs[groups:]
    place = lax.rem(ids[0], plan.half)
    me = ids[1]
    columns = plan.columns(place)
    for k in range(groups):
        seen[me ^ k] = views[k][...]
    radius = ALPHA_RATIO ** (1.0 / steps)
    grow = [radius**n for n in range(steps)]
    nothing = jnp.zeros((planes, plan.block), jnp.float32)
    for freq in range(steps // 2 + 1):
        angle = [2.0 * math.pi * (freq * n % steps) / steps for n in range(steps)]

        def spectrum(block, edge):
            real, imag = nothing, nothing
            for n in range(steps):
                value = seen[block, 2 * n + edge]
                real = real + value * np.float32(grow[n] * math.cos(angle[n]))
                if freq % (steps // 2):
                    imag = imag - value * np.float32(grow[n] * math.sin(angle[n]))
            return real, imag

        head = [spectrum(block, 0) for block in range(groups)]
        tail = [spectrum(block, 1) for block in range(groups)]
        near, far = (
            tuple(
                responses[freq, 2 * kind + part, first : first + planes, columns]
                for part in range(2)
            )
            for kind in range(2)
        )
        square = c_mul(far, far)
        gammas, downs, ups = [near], [tail[0]], [head[groups - 1]]
        for d in range(1, groups - 1):
            gamma = gammas[-1]
            gap = c_gap(gamma, near)
            through = c_mul(far, gap)
            e = groups - 1 - d
            downs.append(
                c_add(
                    tail[d], c_mul(through, c_add(downs[-1], c_mul(gamma, head[d])))
                )
            )
            ups.append(
                c_add(head[e], c_mul(through, c_add(ups[-1], c_mul(gamma, tail[e]))))
            )
            gammas.append(c_add(near, c_mul(square, c_mul(gamma, gap))))
        for d in range(groups - 1):
            down, up = downs[d], ups[groups - 2 - d]
            from_top, from_end = gammas[d], gammas[groups - 2 - d]
            gap = c_gap(from_top, from_end)
            last = c_mul(c_add(down, c_mul(from_top, up)), gap)
            start = c_mul(c_add(up, c_mul(from_end, down)), gap)
            for part in range(2):
                above[d + 1, 2 * freq + part] = last[part]
                below[d, 2 * freq + part] = start[part]
        for part in range(2):
            above[0, 2 * freq + part] = nothing
            below[groups - 1, 2 * freq + part] = nothing
    for edge, side in enumerate((above, below)):
        parts = [side[me, i] for i in range(steps + 2)]
        for n in range(steps):
            total = nothing
            shrink = STEP_SCALE / (steps * grow[n])
            if n == steps - 1:
                shrink *= ALPHA_RATIO
            for freq in range(steps // 2 + 1):
                angle = 2.0 * math.pi * (freq * n % steps) / steps
                single = freq % (steps // 2) == 0
                weight = shrink if single else 2.0 * shrink
                total = total + parts[2 * freq] * np.float32(weight * math.cos(angle))
                if not single:
                    total = total - parts[2 * freq + 1] * np.float32(
                        weight * math.sin(angle)
                    )
            out[2 * ((n + 1) % steps) + edge] = total


def half_solve(plan, first, planes, ids, smu_z, smu_y, smu_x, edges, *refs):
    pieces = refs[: plan.half]
    far, beside, beside_far = refs[plan.half : plan.half + 3]
    outs = refs[plan.half + 3 :]
    half = plan.half
    place = lax.rem(ids[0], half)
    mine = ids[0] // half
    entering = jnp.where(mine == 0, ALPHA_RATIO, 1.0).astype(jnp.float32)

    def with_place(case):
        def body(u, rows, smu, weights):
            cyclic = Cyclic(smu, half)

            def source(window, j):
                total = None
                for edge in range(2):
                    at = 2 * (window * half + j) + edge
                    row = beside[at, u : u + 1, :] + beside_far[at, u : u + 1, :]
                    term = weights[edge] * row
                    total = term if total is None else total + term
                return total

            own = [pieces[case ^ j][u, rows, :] + source(mine, j) for j in range(half)]
            other = [source(1 - mine, j) for j in range(half)]
            before, last = cyclic.start(other)
            before = entering * (before + far[0, u, rows, :])
            last = entering * (last + far[1, u, rows, :])
            before, last = cyclic.back(before, last)
            near = cyclic.start(own)
            entry = cyclic.entry(
                before + ALPHA_RATIO * near[0], last + ALPHA_RATIO * near[1]
            )
            _, _, values = cyclic.run(*entry, own)
            for j, value in enumerate(values):
                outs[case ^ j][u, rows, :] = value

        per_strip(plan, first, planes, place, smu_z, smu_y, smu_x, edges, body)

    by_place(plan, place, with_place)


def swap(values, axis, count, distance):
    if distance == 0:
        return values
    return lax.ppermute(values, axis, [(i, i ^ distance) for i in range(count)])


def on_device(plan, residual):
    steps, groups, half = plan.steps, plan.groups, plan.half
    ids = jnp.stack([lax.axis_index("tm"), lax.axis_index("gy")]).astype(jnp.int32)
    sine_rows = sine_table(plan.rows)
    sxh, sxl = table_parts(sine_table(plan.width))
    both = np.kron(sine_table(plan.depth), sine_rows)
    smu_z, smu_y, smu_x = (
        jnp.asarray(STEP_SCALE * spectrum_of(count).reshape(shape), jnp.float32)
        for count, shape in (
            (plan.depth, (-1, 1)),
            (plan.rows, (-1, 1)),
            (plan.width, (1, -1)),
        )
    )
    edges = jnp.asarray(sine_rows[:, [0, plan.rows - 1]], jnp.float32)
    responses = jnp.asarray(edge_responses(steps, plan.depth, plan.rows, plan.width))
    field = residual[0]
    f32 = functools.partial(jax.ShapeDtypeStruct, dtype=jnp.float32)
    parts = 2
    table = pltpu.VMEM((half, plan.width, plan.block), sxh.dtype)
    held = [
        pltpu.VMEM((parts, plan.depth // parts) + field.shape[1:], jnp.float32),
        table,
        table,
        pltpu.SemaphoreType.DMA((parts + 2 * half,)),
    ]
    far_away = dict.fromkeys((3, 4, 5), pl.BlockSpec(memory_space=pltpu.HBM))
    table = pl.BlockSpec((plan.width, plan.block), lambda j: (0, j))
    columns = pl.BlockSpec(field.shape[:2] + (plan.block,), lambda j: (0, 0, j))
    by_columns = {3: table, 4: table, 5 + half: columns}
    total = far = None
    sent = []
    for first, planes in plan.chunks:
        modes = f32((planes, plan.rows, plan.block))
        span = slice(first * plan.rows, (first + planes) * plan.rows)
        pieces = call(
            functools.partial(forward, plan, planes),
            [modes] * half,
            6 * planes * plan.rows * plan.width * (plan.width + plan.depth * plan.rows),
            (ids, *table_parts(both[span]), field, sxh, sxl),
            held,
            far_away,
            room=ALL_VMEM,
        )
        sent.append([swap(v, "tm", steps, k) for k, v in enumerate(pieces)])
    sent[0][0], sent[-1][0] = lax.optimization_barrier((sent[0][0], sent[-1][0]))
    for (first, planes), pieces in zip(plan.chunks, sent):
        modes = f32((planes, plan.rows, plan.block))
        ends = f32((2,) + modes.shape)
        seen = f32((2 * steps, planes, plan.block))
        count = planes * plan.rows * plan.width
        flops = 6 * count * (plan.width + plan.depth * plan.rows)
        span = slice(first * plan.rows, (first + planes) * plan.rows)
        small = (smu_z, smu_y, smu_x, edges)
        mine, view = call(
            functools.partial(half_end, plan, first, planes),
            [ends, seen],
            100 * count,
            (ids, *small, *pieces),
            [pltpu.VMEM((2 * steps, planes, 8, plan.block), jnp.float32)],
        )
        if far is not None:
            mine, far, beside_far = lax.optimization_barrier((mine, far, beside_far))
        far = swap(mine, "tm", steps, half)
        views = [swap(view, "gy", groups, k) for k in range(groups)]
        sides = pltpu.VMEM((groups, steps + 2, planes, plan.block), jnp.float32)
        beside = call(
            functools.partial(join_rows, plan, first, planes),
            seen,
            100 * count // plan.rows,
            (ids, responses, *views),
            [pltpu.VMEM((groups,) + seen.shape, jnp.float32), sides, sides],
        )
        beside_far = swap(beside, "tm", steps, half)
        pieces = call(
            functools.partial(half_solve, plan, first, planes),
            [modes] * half,
            100 * count,
            (ids, *small, *pieces, far, beside, beside_far),
        )
        pieces = [swap(v, "tm", steps, k) for k, v in enumerate(pieces)]
        ready = () if total is None else (total,)
        total = call(
            functools.partial(backward, plan, planes, total is not None),
            f32(field.shape),
            flops,
            (ids, *table_parts(both[:, span]), sxh, sxl, *pieces, *ready),
            [pltpu.VMEM((planes * plan.rows, plan.width), jnp.bfloat16)] * 2,
            by_columns,
            (half,),
            columns,
        )
    return total[None]


def solution(mesh):
    spec = P("tm", None, "gy", None)

    def whole(residual):
        plan = Plan(mesh, residual.shape)
        return jax.shard_map(
            functools.partial(on_device, plan),
            mesh=mesh,
            in_specs=(spec,),
            out_specs=spec,
            check_vma=False,
        )(residual)

    return whole
```

```python
import functools
import math

import jax
import jax.numpy as jnp
import numpy as np
from jax import lax
from jax.experimental import pallas as pl
from jax.experimental.pallas import tpu as pltpu
from jax.sharding import PartitionSpec as P

ALPHA_RATIO = 0.95
STEP_SCALE = 0.26
LANES = 128
STRIP = 16
FINE_ROWS = 32
VMEM_BYTES = 40 * 1024 * 1024


def sine_table(count):
    indices = np.arange(count, dtype=np.int64) + 1
    product = indices[:, None] * indices[None, :] % (2 * (count + 1))
    return math.sqrt(2.0 / (count + 1)) * np.sin(np.pi * product / (count + 1))


def spectrum_of(count):
    indices = np.arange(count, dtype=np.float64) + 1.0
    return 2.0 - 2.0 * np.cos(np.pi * indices / (count + 1))


def table_parts(table):
    table = table.astype(np.float32)
    high = table.astype(jnp.bfloat16)
    low = (table - high.astype(np.float32)).astype(jnp.bfloat16)
    return jnp.asarray(high), jnp.asarray(low)


def edge_responses(steps, depth, rows, width):
    freq = np.arange(steps // 2 + 1)
    turn = ALPHA_RATIO ** (1.0 / steps) * np.exp(-2j * np.pi * freq / steps)
    turn = turn[:, None, None]
    mu = spectrum_of(depth)[:, None] + spectrum_of(width)[None, :]
    scaled = STEP_SCALE * turn
    middle = ((1.0 - turn) ** 2 + scaled * (mu + 2.0)) / scaled
    root = np.sqrt(middle * middle / 4.0 - 1.0)
    ratio = middle / 2.0 - root
    ratio = np.where(np.abs(ratio) < 1.0, ratio, middle / 2.0 + root)
    bottom = 1.0 - ratio ** (2 * rows + 2)
    near = ratio * (1.0 - ratio ** (2 * rows)) / bottom
    far = ratio**rows * (1.0 - ratio * ratio) / bottom
    parts = np.stack([near.real, near.imag, far.real, far.imag], axis=1)
    return parts.astype(np.float32)


def parts_of(values):
    high = values.astype(jnp.bfloat16)
    return high, (values - high.astype(jnp.float32)).astype(jnp.bfloat16)


def dot(left, right):
    return jnp.dot(left, right, preferred_element_type=jnp.float32)


def dot_parts(left, right):
    return dot(left[0], right[0]) + dot(left[1], right[0]) + dot(left[0], right[1])


def call(kernel, out_shape, flops, args, scratch=(), out=None):
    smem = pl.BlockSpec(memory_space=pltpu.SMEM)
    vmem = pl.BlockSpec(memory_space=pltpu.VMEM)
    moved = sum(x.size * x.dtype.itemsize for x in args)
    return pl.pallas_call(
        kernel,
        out_shape=out_shape,
        in_specs=[smem] + [vmem] * (len(args) - 1),
        out_specs=out or jax.tree.map(lambda _: vmem, out_shape),
        scratch_shapes=scratch,
        compiler_params=pltpu.CompilerParams(vmem_limit_bytes=VMEM_BYTES),
        cost_estimate=pl.CostEstimate(
            flops=flops, bytes_accessed=moved, transcendentals=0
        ),
    )(*args)


class Plan:
    def __init__(self, mesh, shape):
        self.steps = mesh.shape["tm"]
        self.groups = mesh.shape["gy"]
        self.depth, self.width = shape[1], shape[3]
        self.rows = shape[2] // self.groups
        self.half = self.steps // 2
        self.block = self.width // self.half
        self.planes = self.depth // 2

    def columns(self, owner):
        return pl.ds(pl.multiple_of(owner * self.block, LANES), self.block)


def fill_table(plan, ids, coarse_sin, coarse_cos, fine_sin, fine_cos, high, low):
    fine = fine_sin.shape[0]

    def step(index, carry):
        rows = pl.ds(pl.multiple_of(index * fine, fine), fine)
        row = pl.ds(index, 1)
        value = coarse_sin[row, :] * fine_cos[...] + coarse_cos[row, :] * fine_sin[...]
        high[rows, :], low[rows, :] = parts_of(value)
        return carry

    lax.fori_loop(0, plan.width // fine, step, 0)


def angle_tables(count, fine):
    scale = math.sqrt(2.0 / (count + 1))
    columns = np.arange(count, dtype=np.int64) + 1
    tables = []
    for rows, factor in (
        (np.arange(count // fine, dtype=np.int64) * fine, scale),
        (np.arange(fine, dtype=np.int64) + 1, 1.0),
    ):
        turns = rows[:, None] * columns[None, :] % (2 * (count + 1))
        angle = np.pi * turns / (count + 1)
        tables += [factor * np.sin(angle), factor * np.cos(angle)]
    return [jnp.asarray(table, jnp.float32) for table in tables]


def forward(plan, parity, ids, kzh, kzl, x, sxh, sxl, *outs):
    place = lax.rem(ids[0], plan.half)
    planes = plan.planes
    mirror = jnp.stack([x[plan.depth - 1 - z] for z in range(planes)])
    folded = x[:planes] - mirror if parity else x[:planes] + mirror
    folded = parts_of(folded.reshape(planes * plan.rows, plan.width))
    left = parts_of(dot_parts((kzh[...], kzl[...]), folded))
    for k in range(plan.half):
        columns = plan.columns(place ^ k)
        value = dot_parts(left, (sxh[:, columns], sxl[:, columns]))
        outs[k][...] = value.reshape(planes, plan.rows, plan.block)


def backward(plan, ids, kzh, kzl, sxh, sxl, *refs):
    place = lax.rem(ids[0], plan.half)
    pieces, rest = refs[: plan.half], refs[plan.half :]
    high, low = rest[-2:]
    planes = plan.planes
    for k in range(plan.half):
        columns = plan.columns(place ^ k)
        piece = pieces[k][...].reshape(planes * plan.rows, plan.block)
        high[:, columns], low[:, columns] = parts_of(piece)
    for j in range(plan.half):
        columns = pl.ds(j * plan.block, plan.block)
        total = dot_parts((high[...], low[...]), (sxh[:, columns], sxl[:, columns]))
        value = dot_parts((kzh[...], kzl[...]), parts_of(total))
        value = value.reshape(planes, plan.rows, plan.block)
        if len(rest) == 3:
            rest[0][:, :, columns] = value
            continue
        even, out, held, sent = rest[:4]
        other = even[:, :, columns]
        held[j, :planes] = other + value
        for z in range(planes):
            held[j, plan.depth - 1 - z] = other[z] - value[z]
        pltpu.make_async_copy(held.at[j], out.at[:, :, columns], sent.at[j]).start()
    if len(rest) > 3:
        for j in range(plan.half):
            columns = pl.ds(j * plan.block, plan.block)
            pltpu.make_async_copy(held.at[j], out.at[:, :, columns], sent.at[j]).wait()


def per_strip(plan, place, smu_z, smu_y, smu_x, edges, body):
    across = smu_x[:, plan.columns(place)]

    def step(index, carry):
        rows = pl.ds(pl.multiple_of(index * STRIP, STRIP), STRIP)
        plane = across + smu_y[rows, :]
        weights = edges[rows, 0:1], edges[rows, 1:2]
        for u in range(plan.planes):
            body(u, rows, plane + smu_z[u : u + 1, :], weights)
        return carry

    lax.fori_loop(0, plan.rows // STRIP, step, 0)


class Cyclic:
    def __init__(self, smu, half):
        self.kappa = kappa = 2.0 - smu
        values = [jnp.zeros_like(kappa), jnp.ones_like(kappa)]
        for _ in range(half):
            values.append(kappa * values[-1] - values[-2])
        self.up, self.at, self.down = values[-1], values[-2], values[-3]
        det = (1.0 - ALPHA_RATIO) ** 2 + ALPHA_RATIO * (
            smu * (4.0 - smu) * (self.at * self.at)
        )
        inverse = 1.0 / det
        self.even = (0.5 * (1.0 - ALPHA_RATIO)) * (self.up - self.down) * inverse
        self.odd = (0.5 * (1.0 + ALPHA_RATIO)) * self.at * inverse

    def run(self, before, last, sources):
        values = []
        for source in sources:
            value = self.kappa * last - before
            before, last = last, value if source is None else value + source
            values.append(last)
        return before, last, values

    def start(self, sources):
        last = sources[0]
        before, last, _ = self.run(last, self.kappa * last + sources[1], sources[2:])
        return before, last

    def entry(self, p0, p1):
        return (
            self.even * p0 + self.odd * (2.0 * p1 - self.kappa * p0),
            self.even * p1 + self.odd * (self.kappa * p1 - 2.0 * p0),
        )

    def back(self, p0, p1):
        return self.up * p0 - self.at * p1, self.at * p0 - self.down * p1


def by_place(plan, place, body):
    for case in range(plan.half):
        pl.when(place == case)(functools.partial(body, case))


def half_end(plan, ids, smu_z, smu_y, smu_x, edges, *refs):
    pieces = refs[: plan.half]
    *before_seen, ends, seen, sums = refs[plan.half :]
    steps, half = plan.steps, plan.half
    place = lax.rem(ids[0], half)
    mine = ids[0] // half
    leaving = jnp.where(mine == 0, 1.0, ALPHA_RATIO).astype(jnp.float32)
    sums[...] = jnp.zeros_like(sums)

    def with_place(case):
        def body(u, rows, smu, weights):
            cyclic = Cyclic(smu, half)
            sources = [pieces[case ^ j][u, rows, :] for j in range(half)]
            before, last = cyclic.start(sources)
            ends[0, u, rows, :] = before
            ends[1, u, rows, :] = last
            entry = cyclic.entry(ALPHA_RATIO * before, ALPHA_RATIO * last)
            before, last, own = cyclic.run(*entry, sources)
            _, _, other = cyclic.run(leaving * before, leaving * last, [None] * half)
            for values, window in ((own, mine), (other, 1 - mine)):
                for j, value in enumerate(values):
                    for edge in range(2):
                        term = weights[edge] * value
                        term = sum(term[i : i + 8] for i in range(0, STRIP, 8))
                        sums[2 * (window * half + j) + edge, u] += term

        per_strip(plan, place, smu_z, smu_y, smu_x, edges, body)

    by_place(plan, place, with_place)
    own = jnp.sum(sums[...], axis=2)
    if before_seen:
        seen[:, : plan.planes] = before_seen[0][...]
        seen[:, plan.planes :] = own
    else:
        seen[...] = own


def c_mul(a, b):
    return a[0] * b[0] - a[1] * b[1], a[0] * b[1] + a[1] * b[0]


def c_add(a, b):
    return a[0] + b[0], a[1] + b[1]


def c_gap(a, b):
    product = c_mul(a, b)
    real, imag = 1.0 - product[0], -product[1]
    inverse = 1.0 / (real * real + imag * imag)
    return real * inverse, -imag * inverse


def join_rows(plan, ids, responses, *refs):
    groups, steps = plan.groups, plan.steps
    views = refs[:groups]
    out, seen, above, below = refs[groups:]
    place = lax.rem(ids[0], plan.half)
    me = ids[1]
    columns = plan.columns(place)
    for k in range(groups):
        seen[me ^ k] = views[k][...]
    radius = ALPHA_RATIO ** (1.0 / steps)
    grow = [radius**n for n in range(steps)]
    nothing = jnp.zeros((plan.depth, plan.block), jnp.float32)
    for freq in range(steps // 2 + 1):
        angle = [2.0 * math.pi * (freq * n % steps) / steps for n in range(steps)]

        def spectrum(block, edge):
            real, imag = nothing, nothing
            for n in range(steps):
                value = seen[block, 2 * n + edge]
                real = real + value * np.float32(grow[n] * math.cos(angle[n]))
                if freq % (steps // 2):
                    imag = imag - value * np.float32(grow[n] * math.sin(angle[n]))
            return real, imag

        head = [spectrum(block, 0) for block in range(groups)]
        tail = [spectrum(block, 1) for block in range(groups)]
        near, far = (
            tuple(
                responses[freq, 2 * kind + part, :, columns]
                for part in range(2)
            )
            for kind in range(2)
        )
        square = c_mul(far, far)
        gammas, downs, ups = [near], [tail[0]], [head[groups - 1]]
        for d in range(1, groups - 1):
            gamma = gammas[-1]
            gap = c_gap(gamma, near)
            through = c_mul(far, gap)
            e = groups - 1 - d
            downs.append(
                c_add(
                    tail[d], c_mul(through, c_add(downs[-1], c_mul(gamma, head[d])))
                )
            )
            ups.append(
                c_add(head[e], c_mul(through, c_add(ups[-1], c_mul(gamma, tail[e]))))
            )
            gammas.append(c_add(near, c_mul(square, c_mul(gamma, gap))))
        for d in range(groups - 1):
            down, up = downs[d], ups[groups - 2 - d]
            from_top, from_end = gammas[d], gammas[groups - 2 - d]
            gap = c_gap(from_top, from_end)
            last = c_mul(c_add(down, c_mul(from_top, up)), gap)
            start = c_mul(c_add(up, c_mul(from_end, down)), gap)
            for part in range(2):
                above[d + 1, 2 * freq + part] = last[part]
                below[d, 2 * freq + part] = start[part]
        for part in range(2):
            above[0, 2 * freq + part] = nothing
            below[groups - 1, 2 * freq + part] = nothing
    for edge, side in enumerate((above, below)):
        parts = [side[me, i] for i in range(steps + 2)]
        for n in range(steps):
            total = nothing
            shrink = STEP_SCALE / (steps * grow[n])
            if n == steps - 1:
                shrink *= ALPHA_RATIO
            for freq in range(steps // 2 + 1):
                angle = 2.0 * math.pi * (freq * n % steps) / steps
                single = freq % (steps // 2) == 0
                weight = shrink if single else 2.0 * shrink
                total = total + parts[2 * freq] * np.float32(weight * math.cos(angle))
                if not single:
                    total = total - parts[2 * freq + 1] * np.float32(
                        weight * math.sin(angle)
                    )
            out[2 * ((n + 1) % steps) + edge] = total


def half_solve(plan, parity, ids, smu_z, smu_y, smu_x, edges, *refs):
    pieces = refs[: plan.half]
    far, beside, beside_far = refs[plan.half : plan.half + 3]
    outs = refs[plan.half + 3 :]
    half = plan.half
    place = lax.rem(ids[0], half)
    mine = ids[0] // half
    entering = jnp.where(mine == 0, ALPHA_RATIO, 1.0).astype(jnp.float32)

    def with_place(case):
        def body(u, rows, smu, weights):
            cyclic = Cyclic(smu, half)

            def source(window, j):
                total = None
                for edge in range(2):
                    at = 2 * (window * half + j) + edge
                    plane = pl.ds(parity * plan.planes + u, 1)
                    row = beside[at, plane, :] + beside_far[at, plane, :]
                    term = weights[edge] * row
                    total = term if total is None else total + term
                return total

            own = [pieces[case ^ j][u, rows, :] + source(mine, j) for j in range(half)]
            other = [source(1 - mine, j) for j in range(half)]
            before, last = cyclic.start(other)
            before = entering * (before + far[0, u, rows, :])
            last = entering * (last + far[1, u, rows, :])
            before, last = cyclic.back(before, last)
            near = cyclic.start(own)
            entry = cyclic.entry(
                before + ALPHA_RATIO * near[0], last + ALPHA_RATIO * near[1]
            )
            _, _, values = cyclic.run(*entry, own)
            for j, value in enumerate(values):
                outs[case ^ j][u, rows, :] = value

        per_strip(plan, place, smu_z, smu_y, smu_x, edges, body)

    by_place(plan, place, with_place)


def swap(values, axis, count, distance):
    if distance == 0:
        return values
    return lax.ppermute(values, axis, [(i, i ^ distance) for i in range(count)])


def on_device(plan, residual):
    steps, groups, half, planes = plan.steps, plan.groups, plan.half, plan.planes
    ids = jnp.stack([lax.axis_index("tm"), lax.axis_index("gy")]).astype(jnp.int32)
    sine_rows = sine_table(plan.rows)
    sine_depth = sine_table(plan.depth)
    smu_z, smu_y, smu_x = (
        STEP_SCALE * spectrum_of(count) for count in (plan.depth, plan.rows, plan.width)
    )
    smu_y = jnp.asarray(smu_y[:, None], jnp.float32)
    smu_x = jnp.asarray(smu_x[None, :], jnp.float32)
    edges = jnp.asarray(sine_rows[:, [0, plan.rows - 1]], jnp.float32)
    by_parity = np.arange(plan.depth).reshape(planes, 2).T.reshape(-1)
    responses = edge_responses(steps, plan.depth, plan.rows, plan.width)
    responses = jnp.asarray(responses[:, :, by_parity])
    field = residual[0]
    f32 = functools.partial(jax.ShapeDtypeStruct, dtype=jnp.float32)
    modes = f32((planes, plan.rows, plan.block))
    ends = f32((2,) + modes.shape)
    count = planes * plan.rows * plan.width
    flops = 6 * count * (plan.width + planes * plan.rows)
    tables = call(
        functools.partial(fill_table, plan),
        [jax.ShapeDtypeStruct((plan.width, plan.width), jnp.bfloat16)] * 2,
        8 * plan.width * plan.width,
        (ids, *angle_tables(plan.width, FINE_ROWS)),
    )
    sent, small = [], []
    for parity in range(2):
        both = np.kron(sine_depth[parity::2, :planes], sine_rows)
        pieces = call(
            functools.partial(forward, plan, parity),
            [modes] * half,
            flops,
            (ids, *table_parts(both), field, *tables),
        )
        sent.append([swap(v, "tm", steps, k) for k, v in enumerate(pieces)])
        smu_own = jnp.asarray(smu_z[parity::2, None], jnp.float32)
        small.append((ids, smu_own, smu_y, smu_x, edges))
    sent[0][0], sent[1][0] = lax.optimization_barrier((sent[0][0], sent[1][0]))
    mine, seen = [], ()
    for parity in range(2):
        end, *seen = call(
            functools.partial(half_end, plan),
            [ends, f32((2 * steps, planes * (1 + parity), plan.block))],
            100 * count,
            (*small[parity], *sent[parity], *seen),
            [pltpu.VMEM((2 * steps, planes, 8, plan.block), jnp.float32)],
        )
        mine.append(end)
    far = swap(mine[0], "tm", steps, half)
    views = [swap(seen[0], "gy", groups, k) for k in range(groups)]
    sides = pltpu.VMEM((groups, steps + 2, plan.depth, plan.block), jnp.float32)
    beside = call(
        functools.partial(join_rows, plan),
        f32(seen[0].shape),
        100 * plan.depth * plan.block * steps,
        (ids, responses, *views),
        [pltpu.VMEM((groups,) + seen[0].shape, jnp.float32), sides, sides],
    )
    beside_far = swap(beside, "tm", steps, half)
    second, far, beside_far = lax.optimization_barrier((mine[1], far, beside_far))
    far = [far, swap(second, "tm", steps, half)]
    even = ()
    for parity in range(2):
        pieces = call(
            functools.partial(half_solve, plan, parity),
            [modes] * half,
            100 * count,
            (*small[parity], *sent[parity], far[parity], beside, beside_far),
        )
        pieces = [swap(v, "tm", steps, k) for k, v in enumerate(pieces)]
        both = np.kron(sine_depth[:planes, parity::2], sine_rows)
        hold = [pltpu.VMEM((planes * plan.rows, plan.width), jnp.bfloat16)] * 2
        if parity:
            hold = [
                pltpu.VMEM((half,) + field.shape[:2] + (plan.block,), jnp.float32),
                pltpu.SemaphoreType.DMA((half,)),
            ] + hold
        result = call(
            functools.partial(backward, plan),
            f32(field.shape if parity else (planes,) + field.shape[1:]),
            flops,
            (ids, *table_parts(both), *tables, *pieces, *even),
            hold,
            pl.BlockSpec(memory_space=pltpu.HBM) if parity else None,
        )
        even = (result,)
    return result[None]


def solution(mesh):
    spec = P("tm", None, "gy", None)

    def whole(residual):
        plan = Plan(mesh, residual.shape)
        return jax.shard_map(
            functools.partial(on_device, plan),
            mesh=mesh,
            in_specs=(spec,),
            out_specs=spec,
            check_vma=False,
        )(residual)

    return whole
```

```python
import functools
import math

import jax
import jax.numpy as jnp
import numpy as np
from jax import lax
from jax.experimental import pallas as pl
from jax.experimental.pallas import tpu as pltpu
from jax.sharding import PartitionSpec as P

ALPHA_RATIO = 0.95
STEP_SCALE = 0.26
LANES = 128
STRIP = 16
FINE_ROWS = 32
CHUNKS = ((0, 2, 4, 6), (1, 3, 5, 7))
VMEM_BYTES = 40 * 1024 * 1024


def sine_table(count):
    indices = np.arange(count, dtype=np.int64) + 1
    product = indices[:, None] * indices[None, :] % (2 * (count + 1))
    return math.sqrt(2.0 / (count + 1)) * np.sin(np.pi * product / (count + 1))


def spectrum_of(count):
    indices = np.arange(count, dtype=np.float64) + 1.0
    return 2.0 - 2.0 * np.cos(np.pi * indices / (count + 1))


def table_parts(table):
    table = table.astype(np.float32)
    high = table.astype(jnp.bfloat16)
    low = (table - high.astype(np.float32)).astype(jnp.bfloat16)
    return jnp.asarray(high), jnp.asarray(low)


def edge_responses(steps, depth, rows, width):
    freq = np.arange(steps // 2 + 1)
    turn = ALPHA_RATIO ** (1.0 / steps) * np.exp(-2j * np.pi * freq / steps)
    turn = turn[:, None, None]
    mu = spectrum_of(depth)[:, None] + spectrum_of(width)[None, :]
    scaled = STEP_SCALE * turn
    middle = ((1.0 - turn) ** 2 + scaled * (mu + 2.0)) / scaled
    root = np.sqrt(middle * middle / 4.0 - 1.0)
    ratio = middle / 2.0 - root
    ratio = np.where(np.abs(ratio) < 1.0, ratio, middle / 2.0 + root)
    bottom = 1.0 - ratio ** (2 * rows + 2)
    near = ratio * (1.0 - ratio ** (2 * rows)) / bottom
    far = ratio**rows * (1.0 - ratio * ratio) / bottom
    parts = np.stack([near.real, near.imag, far.real, far.imag], axis=1)
    return parts.astype(np.float32)


def parts_of(values):
    high = values.astype(jnp.bfloat16)
    return high, (values - high.astype(jnp.float32)).astype(jnp.bfloat16)


def dot(left, right):
    return jnp.dot(left, right, preferred_element_type=jnp.float32)


def dot_parts(left, right):
    return dot(left[0], right[0]) + dot(left[1], right[0]) + dot(left[0], right[1])


def call(kernel, out_shape, flops, args, scratch=(), out=None):
    smem = pl.BlockSpec(memory_space=pltpu.SMEM)
    vmem = pl.BlockSpec(memory_space=pltpu.VMEM)
    moved = sum(x.size * x.dtype.itemsize for x in args)
    return pl.pallas_call(
        kernel,
        out_shape=out_shape,
        in_specs=[smem] + [vmem] * (len(args) - 1),
        out_specs=out or jax.tree.map(lambda _: vmem, out_shape),
        scratch_shapes=scratch,
        compiler_params=pltpu.CompilerParams(vmem_limit_bytes=VMEM_BYTES),
        cost_estimate=pl.CostEstimate(
            flops=flops, bytes_accessed=moved, transcendentals=0
        ),
    )(*args)


class Plan:
    def __init__(self, mesh, shape):
        self.steps = mesh.shape["tm"]
        self.groups = mesh.shape["gy"]
        self.depth, self.width = shape[1], shape[3]
        self.rows = shape[2] // self.groups
        self.half = self.steps // 2
        self.block = self.width // self.half
        self.folds = self.depth // 2

    def columns(self, owner):
        return pl.ds(pl.multiple_of(owner * self.block, LANES), self.block)


def fill_table(plan, fine, ids, angles, high, low):
    coarse = plan.width // fine
    sine, cosine = (
        angles[2 * coarse + part * fine : 2 * coarse + (part + 1) * fine]
        for part in range(2)
    )

    def step(index, carry):
        rows = pl.ds(pl.multiple_of(index * fine, fine), fine)
        value = angles[pl.ds(index, 1), :] * cosine
        value = value + angles[pl.ds(coarse + index, 1), :] * sine
        high[rows, :], low[rows, :] = parts_of(value)
        return carry

    lax.fori_loop(0, plan.width // fine, step, 0)


def angle_tables(count, fine):
    scale = math.sqrt(2.0 / (count + 1))
    columns = np.arange(count, dtype=np.int64) + 1
    tables = []
    for rows, factor in (
        (np.arange(count // fine, dtype=np.int64) * fine, scale),
        (np.arange(fine, dtype=np.int64) + 1, 1.0),
    ):
        turns = rows[:, None] * columns[None, :] % (2 * (count + 1))
        angle = np.pi * turns / (count + 1)
        tables += [factor * np.sin(angle), factor * np.cos(angle)]
    return jnp.asarray(np.concatenate(tables), jnp.float32)


def fold_tables(plan):
    rows, folds = sine_table(plan.rows), plan.folds
    depth = sine_table(plan.depth)
    tables = [np.kron(depth[parity::2, :folds], rows) for parity in range(2)]
    forth = jnp.stack(table_parts(np.stack(tables)))
    back = jnp.stack(table_parts(np.stack([table.T for table in tables])))
    return forth, back


def by_parity(plan, chunk):
    start = 0
    for parity in range(2):
        places = [c // 2 for c in chunk if c % 2 == parity]
        if places:
            assert places == list(range(places[0], places[0] + len(places)))
            count = len(places) * plan.rows
            first = places[0] * plan.rows
            yield parity, slice(start, start + count), slice(first, first + count)
            start += count


def forward(plan, chunk, ids, both, x, sxh, sxl, *outs):
    place = lax.rem(ids[0], plan.half)
    folds = plan.folds
    mirror = jnp.stack([x[plan.depth - 1 - z] for z in range(folds)])
    left = []
    for parity, _, at in by_parity(plan, chunk):
        folded = x[:folds] - mirror if parity else x[:folds] + mirror
        folded = parts_of(folded.reshape(folds * plan.rows, plan.width))
        table = both[0, parity, at], both[1, parity, at]
        left.append(parts_of(dot_parts(table, folded)))
    for k in range(plan.half):
        columns = plan.columns(place ^ k)
        right = sxh[:, columns], sxl[:, columns]
        value = jnp.concatenate([dot_parts(part, right) for part in left])
        outs[k][...] = value.reshape(len(chunk), plan.rows, plan.block)


def backward(plan, chunk, ready, last, ids, both, sxh, sxl, *refs):
    place = lax.rem(ids[0], plan.half)
    pieces, refs = refs[: plan.half], refs[plan.half :]
    before = dict(zip(ready, refs))
    outs, (high, low) = refs[len(ready) : -2], refs[-2:]
    folds = plan.folds
    shape = folds, plan.rows, plan.block
    for k in range(plan.half):
        piece = pieces[k][...].reshape(len(chunk) * plan.rows, plan.block)
        high[k], low[k] = parts_of(piece)
    for j in range(plan.half):
        columns = pl.ds(j * plan.block, plan.block)
        total = None
        for k in range(plan.half):
            at = plan.columns(place ^ k)
            value = dot_parts((high[k], low[k]), (sxh[at, columns], sxl[at, columns]))
            total = value if total is None else total + value
        total = parts_of(total)
        sums = {parity: before[parity][:, :, columns] for parity in ready}
        for parity, rows, at in by_parity(plan, chunk):
            table = both[0, parity, :, at], both[1, parity, :, at]
            value = dot_parts(table, (total[0][rows], total[1][rows])).reshape(shape)
            sums[parity] = sums[parity] + value if parity in sums else value
        if not last:
            for parity, out in zip(sorted(sums), outs):
                out[:, :, columns] = sums[parity]
            continue
        out, held, sent = outs
        held[j, :folds] = sums[0] + sums[1]
        other = sums[0] - sums[1]
        for z in range(folds):
            held[j, plan.depth - 1 - z] = other[z]
        pltpu.make_async_copy(held.at[j], out.at[:, :, columns], sent.at[j]).start()
    if last:
        for j in range(plan.half):
            columns = pl.ds(j * plan.block, plan.block)
            pltpu.make_async_copy(held.at[j], out.at[:, :, columns], sent.at[j]).wait()


def per_strip(plan, place, smu_z, smu_y, smu_x, edges, body):
    across = smu_x[:, plan.columns(place)]

    def step(index, carry):
        rows = pl.ds(pl.multiple_of(index * STRIP, STRIP), STRIP)
        plane = across + smu_y[rows, :]
        weights = edges[rows, 0:1], edges[rows, 1:2]
        for u in range(smu_z.shape[0]):
            body(u, rows, plane + smu_z[u : u + 1, :], weights)
        return carry

    lax.fori_loop(0, plan.rows // STRIP, step, 0)


class Cyclic:
    def __init__(self, smu, half):
        self.kappa = kappa = 2.0 - smu
        values = [jnp.zeros_like(kappa), jnp.ones_like(kappa)]
        for _ in range(half):
            values.append(kappa * values[-1] - values[-2])
        self.up, self.at, self.down = values[-1], values[-2], values[-3]
        det = (1.0 - ALPHA_RATIO) ** 2 + ALPHA_RATIO * (
            smu * (4.0 - smu) * (self.at * self.at)
        )
        inverse = 1.0 / det
        self.even = (0.5 * (1.0 - ALPHA_RATIO)) * (self.up - self.down) * inverse
        self.odd = (0.5 * (1.0 + ALPHA_RATIO)) * self.at * inverse

    def run(self, before, last, sources):
        values = []
        for source in sources:
            value = self.kappa * last - before
            before, last = last, value if source is None else value + source
            values.append(last)
        return before, last, values

    def start(self, sources):
        last = sources[0]
        before, last, _ = self.run(last, self.kappa * last + sources[1], sources[2:])
        return before, last

    def entry(self, p0, p1):
        return (
            self.even * p0 + self.odd * (2.0 * p1 - self.kappa * p0),
            self.even * p1 + self.odd * (self.kappa * p1 - 2.0 * p0),
        )

    def back(self, p0, p1):
        return self.up * p0 - self.at * p1, self.at * p0 - self.down * p1


def by_place(plan, place, body):
    for case in range(plan.half):
        pl.when(place == case)(functools.partial(body, case))


def half_end(plan, ids, smu_z, smu_y, smu_x, edges, *refs):
    pieces = refs[: plan.half]
    ends, seen, sums = refs[plan.half :]
    steps, half = plan.steps, plan.half
    place = lax.rem(ids[0], half)
    mine = ids[0] // half
    leaving = jnp.where(mine == 0, 1.0, ALPHA_RATIO).astype(jnp.float32)
    sums[...] = jnp.zeros_like(sums)

    def with_place(case):
        def body(u, rows, smu, weights):
            cyclic = Cyclic(smu, half)
            sources = [pieces[case ^ j][u, rows, :] for j in range(half)]
            before, last = cyclic.start(sources)
            ends[0, u, rows, :] = before
            ends[1, u, rows, :] = last
            entry = cyclic.entry(ALPHA_RATIO * before, ALPHA_RATIO * last)
            before, last, own = cyclic.run(*entry, sources)
            _, _, other = cyclic.run(leaving * before, leaving * last, [None] * half)
            for values, window in ((own, mine), (other, 1 - mine)):
                for j, value in enumerate(values):
                    for edge in range(2):
                        term = weights[edge] * value
                        term = sum(term[i : i + 8] for i in range(0, STRIP, 8))
                        sums[2 * (window * half + j) + edge, u] += term

        per_strip(plan, place, smu_z, smu_y, smu_x, edges, body)

    by_place(plan, place, with_place)
    seen[...] = jnp.sum(sums[...], axis=2)


def c_mul(a, b):
    return a[0] * b[0] - a[1] * b[1], a[0] * b[1] + a[1] * b[0]


def c_add(a, b):
    return a[0] + b[0], a[1] + b[1]


def c_gap(a, b):
    product = c_mul(a, b)
    real, imag = 1.0 - product[0], -product[1]
    inverse = 1.0 / (real * real + imag * imag)
    return real * inverse, -imag * inverse


def join_rows(plan, ids, responses, *refs):
    groups, steps = plan.groups, plan.steps
    views = refs[:groups]
    out, seen, above, below = refs[groups:]
    place = lax.rem(ids[0], plan.half)
    me = ids[1]
    columns = plan.columns(place)
    for k in range(groups):
        seen[me ^ k] = views[k][...]
    radius = ALPHA_RATIO ** (1.0 / steps)
    grow = [radius**n for n in range(steps)]
    nothing = jnp.zeros(out.shape[1:], jnp.float32)
    for freq in range(steps // 2 + 1):
        angle = [2.0 * math.pi * (freq * n % steps) / steps for n in range(steps)]

        def spectrum(block, edge):
            real, imag = nothing, nothing
            for n in range(steps):
                value = seen[block, 2 * n + edge]
                real = real + value * np.float32(grow[n] * math.cos(angle[n]))
                if freq % (steps // 2):
                    imag = imag - value * np.float32(grow[n] * math.sin(angle[n]))
            return real, imag

        head = [spectrum(block, 0) for block in range(groups)]
        tail = [spectrum(block, 1) for block in range(groups)]
        near, far = (
            tuple(
                responses[freq, 2 * kind + part, :, columns]
                for part in range(2)
            )
            for kind in range(2)
        )
        square = c_mul(far, far)
        gammas, downs, ups = [near], [tail[0]], [head[groups - 1]]
        for d in range(1, groups - 1):
            gamma = gammas[-1]
            gap = c_gap(gamma, near)
            through = c_mul(far, gap)
            e = groups - 1 - d
            downs.append(
                c_add(
                    tail[d], c_mul(through, c_add(downs[-1], c_mul(gamma, head[d])))
                )
            )
            ups.append(
                c_add(head[e], c_mul(through, c_add(ups[-1], c_mul(gamma, tail[e]))))
            )
            gammas.append(c_add(near, c_mul(square, c_mul(gamma, gap))))
        for d in range(groups - 1):
            down, up = downs[d], ups[groups - 2 - d]
            from_top, from_end = gammas[d], gammas[groups - 2 - d]
            gap = c_gap(from_top, from_end)
            last = c_mul(c_add(down, c_mul(from_top, up)), gap)
            start = c_mul(c_add(up, c_mul(from_end, down)), gap)
            for part in range(2):
                above[d + 1, 2 * freq + part] = last[part]
                below[d, 2 * freq + part] = start[part]
        for part in range(2):
            above[0, 2 * freq + part] = nothing
            below[groups - 1, 2 * freq + part] = nothing
    for edge, side in enumerate((above, below)):
        parts = [side[me, i] for i in range(steps + 2)]
        for n in range(steps):
            total = nothing
            shrink = STEP_SCALE / (steps * grow[n])
            if n == steps - 1:
                shrink *= ALPHA_RATIO
            for freq in range(steps // 2 + 1):
                angle = 2.0 * math.pi * (freq * n % steps) / steps
                single = freq % (steps // 2) == 0
                weight = shrink if single else 2.0 * shrink
                total = total + parts[2 * freq] * np.float32(weight * math.cos(angle))
                if not single:
                    total = total - parts[2 * freq + 1] * np.float32(
                        weight * math.sin(angle)
                    )
            out[2 * ((n + 1) % steps) + edge] = total


def half_solve(plan, ids, smu_z, smu_y, smu_x, edges, *refs):
    pieces = refs[: plan.half]
    far, beside, beside_far = refs[plan.half : plan.half + 3]
    outs = refs[plan.half + 3 :]
    half = plan.half
    place = lax.rem(ids[0], half)
    mine = ids[0] // half
    entering = jnp.where(mine == 0, ALPHA_RATIO, 1.0).astype(jnp.float32)

    def with_place(case):
        def body(u, rows, smu, weights):
            cyclic = Cyclic(smu, half)

            def source(window, j):
                total = None
                for edge in range(2):
                    at = 2 * (window * half + j) + edge
                    row = beside[at, u : u + 1, :] + beside_far[at, u : u + 1, :]
                    term = weights[edge] * row
                    total = term if total is None else total + term
                return total

            own = [pieces[case ^ j][u, rows, :] + source(mine, j) for j in range(half)]
            other = [source(1 - mine, j) for j in range(half)]
            before, last = cyclic.start(other)
            before = entering * (before + far[0, u, rows, :])
            last = entering * (last + far[1, u, rows, :])
            before, last = cyclic.back(before, last)
            near = cyclic.start(own)
            entry = cyclic.entry(
                before + ALPHA_RATIO * near[0], last + ALPHA_RATIO * near[1]
            )
            _, _, values = cyclic.run(*entry, own)
            for j, value in enumerate(values):
                outs[case ^ j][u, rows, :] = value

        per_strip(plan, place, smu_z, smu_y, smu_x, edges, body)

    by_place(plan, place, with_place)


def swap(values, axis, count, distance):
    if distance == 0:
        return values
    return lax.ppermute(values, axis, [(i, i ^ distance) for i in range(count)])


def on_device(plan, residual):
    steps, groups, half = plan.steps, plan.groups, plan.half
    ids = jnp.stack([lax.axis_index("tm"), lax.axis_index("gy")]).astype(jnp.int32)
    sine_rows = sine_table(plan.rows)
    smu_z, smu_y, smu_x = (
        STEP_SCALE * spectrum_of(count) for count in (plan.depth, plan.rows, plan.width)
    )
    smu_y = jnp.asarray(smu_y[:, None], jnp.float32)
    smu_x = jnp.asarray(smu_x[None, :], jnp.float32)
    edges = jnp.asarray(sine_rows[:, [0, plan.rows - 1]], jnp.float32)
    responses = edge_responses(steps, plan.depth, plan.rows, plan.width)
    field = residual[0]
    f32 = functools.partial(jax.ShapeDtypeStruct, dtype=jnp.float32)
    forth, back = fold_tables(plan)
    tables = call(
        functools.partial(fill_table, plan, FINE_ROWS),
        [jax.ShapeDtypeStruct((plan.width, plan.width), jnp.bfloat16)] * 2,
        4000 * plan.width * plan.width,
        (ids, angle_tables(plan.width, FINE_ROWS)),
    )
    work = []
    for chunk in CHUNKS:
        modes = f32((len(chunk), plan.rows, plan.block))
        count = len(chunk) * plan.rows * plan.width
        flops = 6 * count * (plan.width + plan.folds * plan.rows)
        pieces = call(
            functools.partial(forward, plan, chunk),
            [modes] * half,
            flops,
            (ids, forth, field, *tables),
        )
        pieces = [swap(v, "tm", steps, k) for k, v in enumerate(pieces)]
        smu_own = jnp.asarray(smu_z[list(chunk), None], jnp.float32)
        work.append((chunk, modes, flops, (ids, smu_own, smu_y, smu_x, edges), pieces))
    first, second = work[0][-1], work[1][-1]
    first[0], second[0] = lax.optimization_barrier((first[0], second[0]))
    sums = {}
    far = None
    for chunk, modes, flops, small, pieces in work:
        seen = f32((2 * steps, len(chunk), plan.block))
        ends, view = call(
            functools.partial(half_end, plan),
            [f32((2,) + modes.shape), seen],
            100 * modes.size * half,
            (*small, *pieces),
            [pltpu.VMEM((2 * steps, len(chunk), 8, plan.block), jnp.float32)],
        )
        if far is not None:
            ends, far, beside_far = lax.optimization_barrier((ends, far, beside_far))
        far = swap(ends, "tm", steps, half)
        views = [swap(view, "gy", groups, k) for k in range(groups)]
        sides = pltpu.VMEM((groups, steps + 2) + seen.shape[1:], jnp.float32)
        beside = call(
            functools.partial(join_rows, plan),
            seen,
            100 * seen.size,
            (ids, jnp.asarray(responses[:, :, list(chunk)]), *views),
            [pltpu.VMEM((groups,) + seen.shape, jnp.float32), sides, sides],
        )
        beside_far = swap(beside, "tm", steps, half)
        pieces = call(
            functools.partial(half_solve, plan),
            [modes] * half,
            100 * modes.size * half,
            (*small, *pieces, far, beside, beside_far),
        )
        pieces = [swap(v, "tm", steps, k) for k, v in enumerate(pieces)]
        last = chunk == CHUNKS[-1]
        part = pltpu.VMEM((half, len(chunk) * plan.rows, plan.block), jnp.bfloat16)
        hold = [part, part]
        if last:
            block = field.shape[:2] + (plan.block,)
            hold = [
                pltpu.VMEM((half,) + block, jnp.float32),
                pltpu.SemaphoreType.DMA((half,)),
            ] + hold
        ready = tuple(sorted(sums))
        parities = sorted(set(ready) | {c % 2 for c in chunk})
        result = call(
            functools.partial(backward, plan, chunk, ready, last),
            f32(field.shape)
            if last
            else [f32((plan.folds,) + field.shape[1:])] * len(parities),
            flops,
            (ids, back, *tables, *pieces, *(sums[parity] for parity in ready)),
            hold,
            pl.BlockSpec(memory_space=pltpu.HBM) if last else None,
        )
        if not last:
            sums = dict(zip(parities, result))
    return result[None]


def solution(mesh):
    spec = P("tm", None, "gy", None)

    def whole(residual):
        plan = Plan(mesh, residual.shape)
        return jax.shard_map(
            functools.partial(on_device, plan),
            mesh=mesh,
            in_specs=(spec,),
            out_specs=spec,
            check_vma=False,
        )(residual)

    return whole
```

```python
import functools
import math

import jax
import jax.numpy as jnp
import numpy as np
from jax import lax
from jax.experimental import pallas as pl
from jax.experimental.pallas import tpu as pltpu
from jax.sharding import PartitionSpec as P

ALPHA_RATIO = 0.95
STEP_SCALE = 0.26
LANES = 128
STRIP = 16
FINE_ROWS = 32
CHUNKS = ((0, 2, 4, 6), (1, 3, 5, 7))
VMEM_BYTES = 40 * 1024 * 1024


def sine_table(count):
    indices = np.arange(count, dtype=np.int64) + 1
    product = indices[:, None] * indices[None, :] % (2 * (count + 1))
    return math.sqrt(2.0 / (count + 1)) * np.sin(np.pi * product / (count + 1))


def spectrum_of(count):
    indices = np.arange(count, dtype=np.float64) + 1.0
    return 2.0 - 2.0 * np.cos(np.pi * indices / (count + 1))


def table_parts(table):
    table = table.astype(np.float32)
    high = table.astype(jnp.bfloat16)
    low = (table - high.astype(np.float32)).astype(jnp.bfloat16)
    return jnp.asarray(high), jnp.asarray(low)


def edge_responses(steps, depth, rows, width):
    freq = np.arange(steps // 2 + 1)
    turn = ALPHA_RATIO ** (1.0 / steps) * np.exp(-2j * np.pi * freq / steps)
    turn = turn[:, None, None]
    mu = spectrum_of(depth)[:, None] + spectrum_of(width)[None, :]
    scaled = STEP_SCALE * turn
    middle = ((1.0 - turn) ** 2 + scaled * (mu + 2.0)) / scaled
    root = np.sqrt(middle * middle / 4.0 - 1.0)
    ratio = middle / 2.0 - root
    ratio = np.where(np.abs(ratio) < 1.0, ratio, middle / 2.0 + root)
    bottom = 1.0 - ratio ** (2 * rows + 2)
    near = ratio * (1.0 - ratio ** (2 * rows)) / bottom
    far = ratio**rows * (1.0 - ratio * ratio) / bottom
    parts = np.stack([near.real, near.imag, far.real, far.imag], axis=1)
    return parts.astype(np.float32)


def parts_of(values):
    high = values.astype(jnp.bfloat16)
    return high, (values - high.astype(jnp.float32)).astype(jnp.bfloat16)


def dot(left, right):
    return jnp.dot(left, right, preferred_element_type=jnp.float32)


def dot_parts(left, right):
    return dot(left[0], right[0]) + dot(left[1], right[0]) + dot(left[0], right[1])


def call(kernel, out_shape, flops, args, scratch=(), out=None):
    smem = pl.BlockSpec(memory_space=pltpu.SMEM)
    vmem = pl.BlockSpec(memory_space=pltpu.VMEM)
    moved = sum(x.size * x.dtype.itemsize for x in args)
    return pl.pallas_call(
        kernel,
        out_shape=out_shape,
        in_specs=[smem] + [vmem] * (len(args) - 1),
        out_specs=out or jax.tree.map(lambda _: vmem, out_shape),
        scratch_shapes=scratch,
        compiler_params=pltpu.CompilerParams(vmem_limit_bytes=VMEM_BYTES),
        cost_estimate=pl.CostEstimate(
            flops=flops, bytes_accessed=moved, transcendentals=0
        ),
    )(*args)


class Plan:
    def __init__(self, mesh, shape):
        self.steps = mesh.shape["tm"]
        self.groups = mesh.shape["gy"]
        self.depth, self.width = shape[1], shape[3]
        self.rows = shape[2] // self.groups
        self.half = self.steps // 2
        self.block = self.width // self.half
        self.folds = self.depth // 2

    def columns(self, owner):
        return pl.ds(pl.multiple_of(owner * self.block, LANES), self.block)


def fill_table(plan, fine, ids, angles, high, low):
    coarse = plan.width // fine
    sine, cosine = (
        angles[2 * coarse + part * fine : 2 * coarse + (part + 1) * fine]
        for part in range(2)
    )

    def step(index, carry):
        rows = pl.ds(pl.multiple_of(index * fine, fine), fine)
        value = angles[pl.ds(index, 1), :] * cosine
        value = value + angles[pl.ds(coarse + index, 1), :] * sine
        high[rows, :], low[rows, :] = parts_of(value)
        return carry

    lax.fori_loop(0, plan.width // fine, step, 0)


def angle_tables(count, fine):
    scale = math.sqrt(2.0 / (count + 1))
    columns = np.arange(count, dtype=np.int64) + 1
    tables = []
    for rows, factor in (
        (np.arange(count // fine, dtype=np.int64) * fine, scale),
        (np.arange(fine, dtype=np.int64) + 1, 1.0),
    ):
        turns = rows[:, None] * columns[None, :] % (2 * (count + 1))
        angle = np.pi * turns / (count + 1)
        tables += [factor * np.sin(angle), factor * np.cos(angle)]
    return jnp.asarray(np.concatenate(tables), jnp.float32)


def fold_tables(plan):
    rows, folds = sine_table(plan.rows), plan.folds
    depth = sine_table(plan.depth)
    tables = [np.kron(depth[parity::2, :folds], rows) for parity in range(2)]
    forth = jnp.stack(table_parts(np.stack(tables)))
    back = jnp.stack(table_parts(np.stack([table.T for table in tables])))
    return forth, back


def by_parity(plan, chunk):
    start = 0
    for parity in range(2):
        places = [c // 2 for c in chunk if c % 2 == parity]
        if places:
            assert places == list(range(places[0], places[0] + len(places)))
            count = len(places) * plan.rows
            first = places[0] * plan.rows
            yield parity, slice(start, start + count), slice(first, first + count)
            start += count


def forward(plan, chunk, ids, both, x, sxh, sxl, *outs):
    place = lax.rem(ids[0], plan.half)
    folds = plan.folds
    mirror = jnp.stack([x[plan.depth - 1 - z] for z in range(folds)])
    left = []
    for parity, _, at in by_parity(plan, chunk):
        folded = x[:folds] - mirror if parity else x[:folds] + mirror
        folded = parts_of(folded.reshape(folds * plan.rows, plan.width))
        table = both[0, parity, at], both[1, parity, at]
        left.append(parts_of(dot_parts(table, folded)))
    for k in range(plan.half):
        columns = plan.columns(place ^ k)
        right = sxh[:, columns], sxl[:, columns]
        value = jnp.concatenate([dot_parts(part, right) for part in left])
        outs[k][...] = value.reshape(len(chunk), plan.rows, plan.block)


def backward(plan, chunk, ready, last, ids, both, sxh, sxl, *refs):
    place = lax.rem(ids[0], plan.half)
    pieces, refs = refs[: plan.half], refs[plan.half :]
    before = dict(zip(ready, refs))
    outs, (high, low) = refs[len(ready) : -2], refs[-2:]
    folds = plan.folds
    shape = folds, plan.rows, plan.block
    total = None
    for k in range(plan.half):
        at = plan.columns(place ^ k)
        piece = parts_of(pieces[k][...].reshape(-1, plan.block))
        value = dot_parts(piece, (sxh[at, :], sxl[at, :]))
        total = value if total is None else total + value
    high[...], low[...] = parts_of(total)
    for j in range(plan.half):
        columns = pl.ds(j * plan.block, plan.block)
        sums = {parity: before[parity][:, :, columns] for parity in ready}
        for parity, rows, at in by_parity(plan, chunk):
            table = both[0, parity, :, at], both[1, parity, :, at]
            value = dot_parts(table, (high[rows, columns], low[rows, columns]))
            value = value.reshape(shape)
            sums[parity] = sums[parity] + value if parity in sums else value
        if not last:
            for parity, out in zip(sorted(sums), outs):
                out[:, :, columns] = sums[parity]
            continue
        out, held, sent = outs
        held[j, :folds] = sums[0] + sums[1]
        other = sums[0] - sums[1]
        for z in range(folds):
            held[j, plan.depth - 1 - z] = other[z]
        pltpu.make_async_copy(held.at[j], out.at[:, :, columns], sent.at[j]).start()
    if last:
        for j in range(plan.half):
            columns = pl.ds(j * plan.block, plan.block)
            pltpu.make_async_copy(held.at[j], out.at[:, :, columns], sent.at[j]).wait()


def per_strip(plan, place, smu_z, smu_y, smu_x, edges, body):
    across = smu_x[:, plan.columns(place)]

    def step(index, carry):
        rows = pl.ds(pl.multiple_of(index * STRIP, STRIP), STRIP)
        plane = across + smu_y[rows, :]
        weights = edges[rows, 0:1], edges[rows, 1:2]
        for u in range(smu_z.shape[0]):
            body(u, rows, plane + smu_z[u : u + 1, :], weights)
        return carry

    lax.fori_loop(0, plan.rows // STRIP, step, 0)


class Cyclic:
    def __init__(self, smu, half):
        self.kappa = kappa = 2.0 - smu
        values = [jnp.zeros_like(kappa), jnp.ones_like(kappa)]
        for _ in range(half):
            values.append(kappa * values[-1] - values[-2])
        self.up, self.at, self.down = values[-1], values[-2], values[-3]
        det = (1.0 - ALPHA_RATIO) ** 2 + ALPHA_RATIO * (
            smu * (4.0 - smu) * (self.at * self.at)
        )
        inverse = 1.0 / det
        self.even = (0.5 * (1.0 - ALPHA_RATIO)) * (self.up - self.down) * inverse
        self.odd = (0.5 * (1.0 + ALPHA_RATIO)) * self.at * inverse

    def run(self, before, last, sources):
        values = []
        for source in sources:
            value = self.kappa * last - before
            before, last = last, value if source is None else value + source
            values.append(last)
        return before, last, values

    def start(self, sources):
        last = sources[0]
        before, last, _ = self.run(last, self.kappa * last + sources[1], sources[2:])
        return before, last

    def entry(self, p0, p1):
        return (
            self.even * p0 + self.odd * (2.0 * p1 - self.kappa * p0),
            self.even * p1 + self.odd * (self.kappa * p1 - 2.0 * p0),
        )

    def back(self, p0, p1):
        return self.up * p0 - self.at * p1, self.at * p0 - self.down * p1


def by_place(plan, place, body):
    for case in range(plan.half):
        pl.when(place == case)(functools.partial(body, case))


def half_end(plan, ids, smu_z, smu_y, smu_x, edges, *refs):
    pieces = refs[: plan.half]
    ends, seen, sums = refs[plan.half :]
    steps, half = plan.steps, plan.half
    place = lax.rem(ids[0], half)
    mine = ids[0] // half
    leaving = jnp.where(mine == 0, 1.0, ALPHA_RATIO).astype(jnp.float32)
    sums[...] = jnp.zeros_like(sums)

    def with_place(case):
        def body(u, rows, smu, weights):
            cyclic = Cyclic(smu, half)
            sources = [pieces[case ^ j][u, rows, :] for j in range(half)]
            before, last = cyclic.start(sources)
            ends[0, u, rows, :] = before
            ends[1, u, rows, :] = last
            entry = cyclic.entry(ALPHA_RATIO * before, ALPHA_RATIO * last)
            before, last, own = cyclic.run(*entry, sources)
            _, _, other = cyclic.run(leaving * before, leaving * last, [None] * half)
            for values, window in ((own, mine), (other, 1 - mine)):
                for j, value in enumerate(values):
                    for edge in range(2):
                        term = weights[edge] * value
                        term = sum(term[i : i + 8] for i in range(0, STRIP, 8))
                        sums[2 * (window * half + j) + edge, u] += term

        per_strip(plan, place, smu_z, smu_y, smu_x, edges, body)

    by_place(plan, place, with_place)
    seen[...] = jnp.sum(sums[...], axis=2)


def c_mul(a, b):
    return a[0] * b[0] - a[1] * b[1], a[0] * b[1] + a[1] * b[0]


def c_add(a, b):
    return a[0] + b[0], a[1] + b[1]


def c_gap(a, b):
    product = c_mul(a, b)
    real, imag = 1.0 - product[0], -product[1]
    inverse = 1.0 / (real * real + imag * imag)
    return real * inverse, -imag * inverse


def join_rows(plan, ids, responses, *refs):
    groups, steps = plan.groups, plan.steps
    seen, out, above, below = refs
    place = lax.rem(ids[0], plan.half)
    me = ids[1]
    columns = plan.columns(place)
    radius = ALPHA_RATIO ** (1.0 / steps)
    grow = [radius**n for n in range(steps)]
    nothing = jnp.zeros(out.shape[1:], jnp.float32)
    for freq in range(steps // 2 + 1):
        angle = [2.0 * math.pi * (freq * n % steps) / steps for n in range(steps)]

        def spectrum(block, edge):
            real, imag = nothing, nothing
            for n in range(steps):
                value = seen[block, 2 * n + edge]
                real = real + value * np.float32(grow[n] * math.cos(angle[n]))
                if freq % (steps // 2):
                    imag = imag - value * np.float32(grow[n] * math.sin(angle[n]))
            return real, imag

        head = [spectrum(block, 0) for block in range(groups)]
        tail = [spectrum(block, 1) for block in range(groups)]
        near, far = (
            tuple(
                responses[freq, 2 * kind + part, :, columns]
                for part in range(2)
            )
            for kind in range(2)
        )
        square = c_mul(far, far)
        gammas, downs, ups = [near], [tail[0]], [head[groups - 1]]
        for d in range(1, groups - 1):
            gamma = gammas[-1]
            gap = c_gap(gamma, near)
            through = c_mul(far, gap)
            e = groups - 1 - d
            downs.append(
                c_add(
                    tail[d], c_mul(through, c_add(downs[-1], c_mul(gamma, head[d])))
                )
            )
            ups.append(
                c_add(head[e], c_mul(through, c_add(ups[-1], c_mul(gamma, tail[e]))))
            )
            gammas.append(c_add(near, c_mul(square, c_mul(gamma, gap))))
        for d in range(groups - 1):
            down, up = downs[d], ups[groups - 2 - d]
            from_top, from_end = gammas[d], gammas[groups - 2 - d]
            gap = c_gap(from_top, from_end)
            last = c_mul(c_add(down, c_mul(from_top, up)), gap)
            start = c_mul(c_add(up, c_mul(from_end, down)), gap)
            for part in range(2):
                above[d + 1, 2 * freq + part] = last[part]
                below[d, 2 * freq + part] = start[part]
        for part in range(2):
            above[0, 2 * freq + part] = nothing
            below[groups - 1, 2 * freq + part] = nothing
    for edge, side in enumerate((above, below)):
        parts = [side[me, i] for i in range(steps + 2)]
        for n in range(steps):
            total = nothing
            shrink = STEP_SCALE / (steps * grow[n])
            if n == steps - 1:
                shrink *= ALPHA_RATIO
            for freq in range(steps // 2 + 1):
                angle = 2.0 * math.pi * (freq * n % steps) / steps
                single = freq % (steps // 2) == 0
                weight = shrink if single else 2.0 * shrink
                total = total + parts[2 * freq] * np.float32(weight * math.cos(angle))
                if not single:
                    total = total - parts[2 * freq + 1] * np.float32(
                        weight * math.sin(angle)
                    )
            out[2 * ((n + 1) % steps) + edge] = total


def half_solve(plan, ids, smu_z, smu_y, smu_x, edges, *refs):
    pieces = refs[: plan.half]
    far, beside, beside_far = refs[plan.half : plan.half + 3]
    outs = refs[plan.half + 3 :]
    half = plan.half
    place = lax.rem(ids[0], half)
    mine = ids[0] // half
    entering = jnp.where(mine == 0, ALPHA_RATIO, 1.0).astype(jnp.float32)

    def with_place(case):
        def body(u, rows, smu, weights):
            cyclic = Cyclic(smu, half)

            def source(window, j):
                total = None
                for edge in range(2):
                    at = 2 * (window * half + j) + edge
                    row = beside[at, u : u + 1, :] + beside_far[at, u : u + 1, :]
                    term = weights[edge] * row
                    total = term if total is None else total + term
                return total

            own = [pieces[case ^ j][u, rows, :] + source(mine, j) for j in range(half)]
            other = [source(1 - mine, j) for j in range(half)]
            before, last = cyclic.start(other)
            before = entering * (before + far[0, u, rows, :])
            last = entering * (last + far[1, u, rows, :])
            before, last = cyclic.back(before, last)
            near = cyclic.start(own)
            entry = cyclic.entry(
                before + ALPHA_RATIO * near[0], last + ALPHA_RATIO * near[1]
            )
            _, _, values = cyclic.run(*entry, own)
            for j, value in enumerate(values):
                outs[case ^ j][u, rows, :] = value

        per_strip(plan, place, smu_z, smu_y, smu_x, edges, body)

    by_place(plan, place, with_place)


def spread(plan, pieces):
    moved = [swap(pieces[k], "tm", plan.steps, k) for k in range(plan.half - 1, -1, -1)]
    return moved[::-1]


def swap(values, axis, count, distance):
    if distance == 0:
        return values
    return lax.ppermute(values, axis, [(i, i ^ distance) for i in range(count)])


def on_device(plan, residual):
    steps, groups, half = plan.steps, plan.groups, plan.half
    ids = jnp.stack([lax.axis_index("tm"), lax.axis_index("gy")]).astype(jnp.int32)
    sine_rows = sine_table(plan.rows)
    smu_z, smu_y, smu_x = (
        STEP_SCALE * spectrum_of(count) for count in (plan.depth, plan.rows, plan.width)
    )
    smu_y = jnp.asarray(smu_y[:, None], jnp.float32)
    smu_x = jnp.asarray(smu_x[None, :], jnp.float32)
    edges = jnp.asarray(sine_rows[:, [0, plan.rows - 1]], jnp.float32)
    responses = edge_responses(steps, plan.depth, plan.rows, plan.width)
    field = residual[0]
    f32 = functools.partial(jax.ShapeDtypeStruct, dtype=jnp.float32)
    forth, back = fold_tables(plan)
    tables = call(
        functools.partial(fill_table, plan, FINE_ROWS),
        [jax.ShapeDtypeStruct((plan.width, plan.width), jnp.bfloat16)] * 2,
        4000 * plan.width * plan.width,
        (ids, angle_tables(plan.width, FINE_ROWS)),
    )
    work = []
    for chunk in CHUNKS:
        modes = f32((len(chunk), plan.rows, plan.block))
        count = len(chunk) * plan.rows * plan.width
        flops = 6 * count * (plan.width + plan.folds * plan.rows)
        pieces = call(
            functools.partial(forward, plan, chunk),
            [modes] * half,
            flops,
            (ids, forth, field, *tables),
        )
        pieces = spread(plan, pieces)
        smu_own = jnp.asarray(smu_z[list(chunk), None], jnp.float32)
        work.append((chunk, modes, flops, (ids, smu_own, smu_y, smu_x, edges), pieces))
    first, second = work[0][-1], work[1][-1]
    first[0], second[0] = lax.optimization_barrier((first[0], second[0]))
    ended = []
    for chunk, modes, flops, small, pieces in work:
        seen = f32((2 * steps, len(chunk), plan.block))
        ends, view = call(
            functools.partial(half_end, plan),
            [f32((2,) + modes.shape), seen],
            40000 * modes.size * half,
            (*small, *pieces),
            [pltpu.VMEM((2 * steps, len(chunk), 8, plan.block), jnp.float32)],
        )
        ended.append([ends, seen, lax.all_gather(view, "gy")])
    for now, later in zip(ended, ended[1:]):
        now[2], later[0] = lax.optimization_barrier((now[2], later[0]))
    sums = {}
    far = None
    for (chunk, modes, flops, small, pieces), (ends, seen, views) in zip(work, ended):
        if far is not None:
            ends, far, beside_far = lax.optimization_barrier((ends, far, beside_far))
        far = swap(ends, "tm", steps, half)
        sides = pltpu.VMEM((groups, steps + 2) + seen.shape[1:], jnp.float32)
        beside = call(
            functools.partial(join_rows, plan),
            seen,
            (100 if chunk == CHUNKS[-1] else 80000) * modes.size * half,
            (ids, jnp.asarray(responses[:, :, list(chunk)]), views),
            [sides, sides],
        )
        beside_far = swap(beside, "tm", steps, half)
        pieces = call(
            functools.partial(half_solve, plan),
            [modes] * half,
            100 * modes.size * half,
            (*small, *pieces, far, beside, beside_far),
        )
        pieces = spread(plan, pieces)
        last = chunk == CHUNKS[-1]
        part = pltpu.VMEM((len(chunk) * plan.rows, plan.width), jnp.bfloat16)
        hold = [part, part]
        if last:
            block = field.shape[:2] + (plan.block,)
            hold = [
                pltpu.VMEM((half,) + block, jnp.float32),
                pltpu.SemaphoreType.DMA((half,)),
            ] + hold
        ready = tuple(sorted(sums))
        parities = sorted(set(ready) | {c % 2 for c in chunk})
        result = call(
            functools.partial(backward, plan, chunk, ready, last),
            f32(field.shape)
            if last
            else [f32((plan.folds,) + field.shape[1:])] * len(parities),
            flops,
            (ids, back, *tables, *pieces, *(sums[parity] for parity in ready)),
            hold,
            pl.BlockSpec(memory_space=pltpu.HBM) if last else None,
        )
        if not last:
            sums = dict(zip(parities, result))
    return result[None]


def solution(mesh):
    spec = P("tm", None, "gy", None)

    def whole(residual):
        plan = Plan(mesh, residual.shape)
        return jax.shard_map(
            functools.partial(on_device, plan),
            mesh=mesh,
            in_specs=(spec,),
            out_specs=spec,
            check_vma=False,
        )(residual)

    return whole
```

```python
import functools
import math

import jax
import jax.numpy as jnp
import numpy as np
from jax import lax
from jax.experimental import pallas as pl
from jax.experimental.pallas import tpu as pltpu
from jax.sharding import PartitionSpec as P

ALPHA_RATIO = 0.95
STEP_SCALE = 0.26
LANES = 128
STRIP = 16
FINE_ROWS = 32
CHUNKS = ((0, 2, 4, 6), (1, 3, 5, 7))
VMEM_BYTES = 40 * 1024 * 1024


def sine_table(count):
    indices = np.arange(count, dtype=np.int64) + 1
    product = indices[:, None] * indices[None, :] % (2 * (count + 1))
    return math.sqrt(2.0 / (count + 1)) * np.sin(np.pi * product / (count + 1))


def spectrum_of(count):
    indices = np.arange(count, dtype=np.float64) + 1.0
    return 2.0 - 2.0 * np.cos(np.pi * indices / (count + 1))


def table_parts(table):
    table = table.astype(np.float32)
    high = table.astype(jnp.bfloat16)
    low = (table - high.astype(np.float32)).astype(jnp.bfloat16)
    return jnp.asarray(high), jnp.asarray(low)


def edge_responses(steps, depth, rows, width):
    freq = np.arange(steps // 2 + 1)
    turn = ALPHA_RATIO ** (1.0 / steps) * np.exp(-2j * np.pi * freq / steps)
    turn = turn[:, None, None]
    mu = spectrum_of(depth)[:, None] + spectrum_of(width)[None, :]
    scaled = STEP_SCALE * turn
    middle = ((1.0 - turn) ** 2 + scaled * (mu + 2.0)) / scaled
    root = np.sqrt(middle * middle / 4.0 - 1.0)
    ratio = middle / 2.0 - root
    ratio = np.where(np.abs(ratio) < 1.0, ratio, middle / 2.0 + root)
    bottom = 1.0 - ratio ** (2 * rows + 2)
    near = ratio * (1.0 - ratio ** (2 * rows)) / bottom
    far = ratio**rows * (1.0 - ratio * ratio) / bottom
    parts = np.stack([near.real, near.imag, far.real, far.imag], axis=1)
    return parts.astype(np.float32)


def parts_of(values):
    high = values.astype(jnp.bfloat16)
    return high, (values - high.astype(jnp.float32)).astype(jnp.bfloat16)


def dot(left, right):
    return jnp.dot(left, right, preferred_element_type=jnp.float32)


def dot_parts(left, right):
    return dot(left[0], right[0]) + dot(left[1], right[0]) + dot(left[0], right[1])


def call(kernel, out_shape, flops, args, scratch=(), out=None):
    smem = pl.BlockSpec(memory_space=pltpu.SMEM)
    vmem = pl.BlockSpec(memory_space=pltpu.VMEM)
    moved = sum(x.size * x.dtype.itemsize for x in args)
    return pl.pallas_call(
        kernel,
        out_shape=out_shape,
        in_specs=[smem] + [vmem] * (len(args) - 1),
        out_specs=out or jax.tree.map(lambda _: vmem, out_shape),
        scratch_shapes=scratch,
        compiler_params=pltpu.CompilerParams(vmem_limit_bytes=VMEM_BYTES),
        cost_estimate=pl.CostEstimate(
            flops=flops, bytes_accessed=moved, transcendentals=0
        ),
    )(*args)


class Plan:
    def __init__(self, mesh, shape):
        self.steps = mesh.shape["tm"]
        self.groups = mesh.shape["gy"]
        self.depth, self.width = shape[1], shape[3]
        self.rows = shape[2] // self.groups
        self.half = self.steps // 2
        self.block = self.width // self.half
        self.folds = self.depth // 2

    def columns(self, owner):
        return pl.ds(pl.multiple_of(owner * self.block, LANES), self.block)


def fill_table(plan, fine, ids, angles, high, low):
    coarse = plan.width // fine
    sine, cosine = (
        angles[2 * coarse + part * fine : 2 * coarse + (part + 1) * fine]
        for part in range(2)
    )

    def step(index, carry):
        rows = pl.ds(pl.multiple_of(index * fine, fine), fine)
        value = angles[pl.ds(index, 1), :] * cosine
        value = value + angles[pl.ds(coarse + index, 1), :] * sine
        high[rows, :], low[rows, :] = parts_of(value)
        return carry

    lax.fori_loop(0, plan.width // fine, step, 0)


def angle_tables(count, fine):
    scale = math.sqrt(2.0 / (count + 1))
    columns = np.arange(count, dtype=np.int64) + 1
    tables = []
    for rows, factor in (
        (np.arange(count // fine, dtype=np.int64) * fine, scale),
        (np.arange(fine, dtype=np.int64) + 1, 1.0),
    ):
        turns = rows[:, None] * columns[None, :] % (2 * (count + 1))
        angle = np.pi * turns / (count + 1)
        tables += [factor * np.sin(angle), factor * np.cos(angle)]
    return jnp.asarray(np.concatenate(tables), jnp.float32)


def fold_tables(plan):
    rows, folds = sine_table(plan.rows), plan.folds
    depth = sine_table(plan.depth)
    tables = [np.kron(depth[parity::2, :folds], rows) for parity in range(2)]
    forth = jnp.stack(table_parts(np.stack(tables)))
    back = jnp.stack(table_parts(np.stack([table.T for table in tables])))
    return forth, back


def by_parity(plan, chunk):
    start = 0
    for parity in range(2):
        places = [c // 2 for c in chunk if c % 2 == parity]
        if places:
            assert places == list(range(places[0], places[0] + len(places)))
            count = len(places) * plan.rows
            first = places[0] * plan.rows
            yield parity, slice(start, start + count), slice(first, first + count)
            start += count


def forward(plan, chunk, ids, both, x, sxh, sxl, *outs):
    place = lax.rem(ids[0], plan.half)
    folds = plan.folds
    mirror = jnp.stack([x[plan.depth - 1 - z] for z in range(folds)])
    left = []
    for parity, _, at in by_parity(plan, chunk):
        folded = x[:folds] - mirror if parity else x[:folds] + mirror
        folded = parts_of(folded.reshape(folds * plan.rows, plan.width))
        table = both[0, parity, at], both[1, parity, at]
        left.append(parts_of(dot_parts(table, folded)))
    for k in range(plan.half):
        columns = plan.columns(place ^ k)
        right = sxh[:, columns], sxl[:, columns]
        value = jnp.concatenate([dot_parts(part, right) for part in left])
        outs[k][...] = value.reshape(len(chunk), plan.rows, plan.block)


def backward(plan, chunk, ready, last, ids, both, sxh, sxl, *refs):
    place = lax.rem(ids[0], plan.half)
    pieces, refs = refs[: plan.half], refs[plan.half :]
    before = dict(zip(ready, refs))
    outs, (high, low) = refs[len(ready) : -2], refs[-2:]
    folds = plan.folds
    shape = folds, plan.rows, plan.block
    total = None
    for k in range(plan.half):
        at = plan.columns(place ^ k)
        piece = parts_of(pieces[k][...].reshape(-1, plan.block))
        value = dot_parts(piece, (sxh[at, :], sxl[at, :]))
        total = value if total is None else total + value
    high[...], low[...] = parts_of(total)
    for j in range(plan.half):
        columns = pl.ds(j * plan.block, plan.block)
        sums = {parity: before[parity][:, :, columns] for parity in ready}
        for parity, rows, at in by_parity(plan, chunk):
            table = both[0, parity, :, at], both[1, parity, :, at]
            value = dot_parts(table, (high[rows, columns], low[rows, columns]))
            value = value.reshape(shape)
            sums[parity] = sums[parity] + value if parity in sums else value
        if not last:
            for parity, out in zip(sorted(sums), outs):
                out[:, :, columns] = sums[parity]
            continue
        out, held, sent = outs
        held[j, :folds] = sums[0] + sums[1]
        other = sums[0] - sums[1]
        for z in range(folds):
            held[j, plan.depth - 1 - z] = other[z]
        pltpu.make_async_copy(held.at[j], out.at[:, :, columns], sent.at[j]).start()
    if last:
        for j in range(plan.half):
            columns = pl.ds(j * plan.block, plan.block)
            pltpu.make_async_copy(held.at[j], out.at[:, :, columns], sent.at[j]).wait()


def per_strip(plan, place, smu_z, smu_y, smu_x, edges, body):
    across = smu_x[:, plan.columns(place)]

    def step(index, carry):
        rows = pl.ds(pl.multiple_of(index * STRIP, STRIP), STRIP)
        plane = across + smu_y[rows, :]
        weights = edges[rows, 0:1], edges[rows, 1:2]
        for u in range(smu_z.shape[0]):
            body(u, rows, plane + smu_z[u : u + 1, :], weights)
        return carry

    lax.fori_loop(0, plan.rows // STRIP, step, 0)


class Cyclic:
    def __init__(self, smu, half):
        self.kappa = kappa = 2.0 - smu
        values = [jnp.zeros_like(kappa), jnp.ones_like(kappa)]
        for _ in range(half):
            values.append(kappa * values[-1] - values[-2])
        self.up, self.at, self.down = values[-1], values[-2], values[-3]
        det = (1.0 - ALPHA_RATIO) ** 2 + ALPHA_RATIO * (
            smu * (4.0 - smu) * (self.at * self.at)
        )
        inverse = 1.0 / det
        self.even = (0.5 * (1.0 - ALPHA_RATIO)) * (self.up - self.down) * inverse
        self.odd = (0.5 * (1.0 + ALPHA_RATIO)) * self.at * inverse

    def run(self, before, last, sources):
        values = []
        for source in sources:
            value = self.kappa * last - before
            before, last = last, value if source is None else value + source
            values.append(last)
        return before, last, values

    def start(self, sources):
        last = sources[0]
        before, last, _ = self.run(last, self.kappa * last + sources[1], sources[2:])
        return before, last

    def entry(self, p0, p1):
        return (
            self.even * p0 + self.odd * (2.0 * p1 - self.kappa * p0),
            self.even * p1 + self.odd * (self.kappa * p1 - 2.0 * p0),
        )

    def back(self, p0, p1):
        return self.up * p0 - self.at * p1, self.at * p0 - self.down * p1


def by_place(plan, place, body):
    for case in range(plan.half):
        pl.when(place == case)(functools.partial(body, case))


def half_end(plan, ids, smu_z, smu_y, smu_x, edges, *refs):
    pieces = refs[: plan.half]
    ends, seen, sums = refs[plan.half :]
    steps, half = plan.steps, plan.half
    place = lax.rem(ids[0], half)
    mine = ids[0] // half
    leaving = jnp.where(mine == 0, 1.0, ALPHA_RATIO).astype(jnp.float32)
    sums[...] = jnp.zeros_like(sums)

    def with_place(case):
        def body(u, rows, smu, weights):
            cyclic = Cyclic(smu, half)
            sources = [pieces[case ^ j][u, rows, :] for j in range(half)]
            before, last = cyclic.start(sources)
            ends[0, u, rows, :] = before
            ends[1, u, rows, :] = last
            entry = cyclic.entry(ALPHA_RATIO * before, ALPHA_RATIO * last)
            before, last, own = cyclic.run(*entry, sources)
            _, _, other = cyclic.run(leaving * before, leaving * last, [None] * half)
            for values, window in ((own, mine), (other, 1 - mine)):
                for j, value in enumerate(values):
                    for edge in range(2):
                        term = weights[edge] * value
                        term = sum(term[i : i + 8] for i in range(0, STRIP, 8))
                        sums[2 * (window * half + j) + edge, u] += term

        per_strip(plan, place, smu_z, smu_y, smu_x, edges, body)

    by_place(plan, place, with_place)
    seen[...] = jnp.sum(sums[...], axis=2)


def c_mul(a, b):
    return a[0] * b[0] - a[1] * b[1], a[0] * b[1] + a[1] * b[0]


def c_add(a, b):
    return a[0] + b[0], a[1] + b[1]


def c_gap(a, b):
    product = c_mul(a, b)
    real, imag = 1.0 - product[0], -product[1]
    inverse = 1.0 / (real * real + imag * imag)
    return real * inverse, -imag * inverse


def join_rows(plan, ids, responses, *refs):
    groups, steps = plan.groups, plan.steps
    views = refs[:groups]
    out, seen, above, below = refs[groups:]
    place = lax.rem(ids[0], plan.half)
    me = ids[1]
    columns = plan.columns(place)
    for k in range(groups):
        seen[me ^ k] = views[k][...]
    radius = ALPHA_RATIO ** (1.0 / steps)
    grow = [radius**n for n in range(steps)]
    nothing = jnp.zeros(out.shape[1:], jnp.float32)
    for freq in range(steps // 2 + 1):
        angle = [2.0 * math.pi * (freq * n % steps) / steps for n in range(steps)]

        def spectrum(block, edge):
            real, imag = nothing, nothing
            for n in range(steps):
                value = seen[block, 2 * n + edge]
                real = real + value * np.float32(grow[n] * math.cos(angle[n]))
                if freq % (steps // 2):
                    imag = imag - value * np.float32(grow[n] * math.sin(angle[n]))
            return real, imag

        head = [spectrum(block, 0) for block in range(groups)]
        tail = [spectrum(block, 1) for block in range(groups)]
        near, far = (
            tuple(
                responses[freq, 2 * kind + part, :, columns]
                for part in range(2)
            )
            for kind in range(2)
        )
        square = c_mul(far, far)
        gammas, downs, ups = [near], [tail[0]], [head[groups - 1]]
        for d in range(1, groups - 1):
            gamma = gammas[-1]
            gap = c_gap(gamma, near)
            through = c_mul(far, gap)
            e = groups - 1 - d
            downs.append(
                c_add(
                    tail[d], c_mul(through, c_add(downs[-1], c_mul(gamma, head[d])))
                )
            )
            ups.append(
                c_add(head[e], c_mul(through, c_add(ups[-1], c_mul(gamma, tail[e]))))
            )
            gammas.append(c_add(near, c_mul(square, c_mul(gamma, gap))))
        for d in range(groups - 1):
            down, up = downs[d], ups[groups - 2 - d]
            from_top, from_end = gammas[d], gammas[groups - 2 - d]
            gap = c_gap(from_top, from_end)
            last = c_mul(c_add(down, c_mul(from_top, up)), gap)
            start = c_mul(c_add(up, c_mul(from_end, down)), gap)
            for part in range(2):
                above[d + 1, 2 * freq + part] = last[part]
                below[d, 2 * freq + part] = start[part]
        for part in range(2):
            above[0, 2 * freq + part] = nothing
            below[groups - 1, 2 * freq + part] = nothing
    for edge, side in enumerate((above, below)):
        parts = [side[me, i] for i in range(steps + 2)]
        for n in range(steps):
            total = nothing
            shrink = STEP_SCALE / (steps * grow[n])
            if n == steps - 1:
                shrink *= ALPHA_RATIO
            for freq in range(steps // 2 + 1):
                angle = 2.0 * math.pi * (freq * n % steps) / steps
                single = freq % (steps // 2) == 0
                weight = shrink if single else 2.0 * shrink
                total = total + parts[2 * freq] * np.float32(weight * math.cos(angle))
                if not single:
                    total = total - parts[2 * freq + 1] * np.float32(
                        weight * math.sin(angle)
                    )
            out[2 * ((n + 1) % steps) + edge] = total


def half_solve(plan, ids, smu_z, smu_y, smu_x, edges, *refs):
    pieces = refs[: plan.half]
    far, beside, beside_far = refs[plan.half : plan.half + 3]
    outs = refs[plan.half + 3 :]
    half = plan.half
    place = lax.rem(ids[0], half)
    mine = ids[0] // half
    entering = jnp.where(mine == 0, ALPHA_RATIO, 1.0).astype(jnp.float32)

    def with_place(case):
        def body(u, rows, smu, weights):
            cyclic = Cyclic(smu, half)

            def source(window, j):
                total = None
                for edge in range(2):
                    at = 2 * (window * half + j) + edge
                    row = beside[at, u : u + 1, :] + beside_far[at, u : u + 1, :]
                    term = weights[edge] * row
                    total = term if total is None else total + term
                return total

            own = [pieces[case ^ j][u, rows, :] + source(mine, j) for j in range(half)]
            other = [source(1 - mine, j) for j in range(half)]
            before, last = cyclic.start(other)
            before = entering * (before + far[0, u, rows, :])
            last = entering * (last + far[1, u, rows, :])
            before, last = cyclic.back(before, last)
            near = cyclic.start(own)
            entry = cyclic.entry(
                before + ALPHA_RATIO * near[0], last + ALPHA_RATIO * near[1]
            )
            _, _, values = cyclic.run(*entry, own)
            for j, value in enumerate(values):
                outs[case ^ j][u, rows, :] = value

        per_strip(plan, place, smu_z, smu_y, smu_x, edges, body)

    by_place(plan, place, with_place)


def spread(plan, pieces):
    moved = [swap(pieces[k], "tm", plan.steps, k) for k in range(plan.half - 1, -1, -1)]
    return moved[::-1]


def swap(values, axis, count, distance):
    if distance == 0:
        return values
    return lax.ppermute(values, axis, [(i, i ^ distance) for i in range(count)])


def on_device(plan, residual):
    steps, groups, half = plan.steps, plan.groups, plan.half
    ids = jnp.stack([lax.axis_index("tm"), lax.axis_index("gy")]).astype(jnp.int32)
    sine_rows = sine_table(plan.rows)
    smu_z, smu_y, smu_x = (
        STEP_SCALE * spectrum_of(count) for count in (plan.depth, plan.rows, plan.width)
    )
    smu_y = jnp.asarray(smu_y[:, None], jnp.float32)
    smu_x = jnp.asarray(smu_x[None, :], jnp.float32)
    edges = jnp.asarray(sine_rows[:, [0, plan.rows - 1]], jnp.float32)
    responses = edge_responses(steps, plan.depth, plan.rows, plan.width)
    field = residual[0]
    f32 = functools.partial(jax.ShapeDtypeStruct, dtype=jnp.float32)
    forth, back = fold_tables(plan)
    tables = call(
        functools.partial(fill_table, plan, FINE_ROWS),
        [jax.ShapeDtypeStruct((plan.width, plan.width), jnp.bfloat16)] * 2,
        4000 * plan.width * plan.width,
        (ids, angle_tables(plan.width, FINE_ROWS)),
    )
    work = []
    for chunk in CHUNKS:
        modes = f32((len(chunk), plan.rows, plan.block))
        count = len(chunk) * plan.rows * plan.width
        flops = 6 * count * (plan.width + plan.folds * plan.rows)
        pieces = call(
            functools.partial(forward, plan, chunk),
            [modes] * half,
            flops,
            (ids, forth, field, *tables),
        )
        pieces = spread(plan, pieces)
        smu_own = jnp.asarray(smu_z[list(chunk), None], jnp.float32)
        work.append((chunk, modes, flops, (ids, smu_own, smu_y, smu_x, edges), pieces))
    first, second = work[0][-1], work[1][-1]
    first[0], second[0] = lax.optimization_barrier((first[0], second[0]))
    ended = []
    for at, (chunk, modes, flops, small, pieces) in enumerate(work):
        seen = f32((2 * steps, len(chunk), plan.block))
        ends, view = call(
            functools.partial(half_end, plan),
            [f32((2,) + modes.shape), seen],
            (12000 if at else 40000) * modes.size * half,
            (*small, *pieces),
            [pltpu.VMEM((2 * steps, len(chunk), 8, plan.block), jnp.float32)],
        )
        if at + 1 < len(work):
            later = work[at + 1][-1]
            view, *later[:] = lax.optimization_barrier((view, *later))
        ended.append([ends, seen, view])
    sums = {}
    far = None
    for (chunk, modes, flops, small, pieces), (ends, seen, view) in zip(work, ended):
        if far is not None:
            ends, far, beside_far = lax.optimization_barrier((ends, far, beside_far))
        far = swap(ends, "tm", steps, half)
        views = [swap(view, "gy", groups, k) for k in range(groups)]
        sides = pltpu.VMEM((groups, steps + 2) + seen.shape[1:], jnp.float32)
        beside = call(
            functools.partial(join_rows, plan),
            seen,
            100 * seen.size,
            (ids, jnp.asarray(responses[:, :, list(chunk)]), *views),
            [pltpu.VMEM((groups,) + seen.shape, jnp.float32), sides, sides],
        )
        beside_far = swap(beside, "tm", steps, half)
        pieces = call(
            functools.partial(half_solve, plan),
            [modes] * half,
            100 * modes.size * half,
            (*small, *pieces, far, beside, beside_far),
        )
        pieces = spread(plan, pieces)
        last = chunk == CHUNKS[-1]
        part = pltpu.VMEM((len(chunk) * plan.rows, plan.width), jnp.bfloat16)
        hold = [part, part]
        if last:
            block = field.shape[:2] + (plan.block,)
            hold = [
                pltpu.VMEM((half,) + block, jnp.float32),
                pltpu.SemaphoreType.DMA((half,)),
            ] + hold
        ready = tuple(sorted(sums))
        parities = sorted(set(ready) | {c % 2 for c in chunk})
        result = call(
            functools.partial(backward, plan, chunk, ready, last),
            f32(field.shape)
            if last
            else [f32((plan.folds,) + field.shape[1:])] * len(parities),
            flops,
            (ids, back, *tables, *pieces, *(sums[parity] for parity in ready)),
            hold,
            pl.BlockSpec(memory_space=pltpu.HBM) if last else None,
        )
        if not last:
            sums = dict(zip(parities, result))
    return result[None]


def solution(mesh):
    spec = P("tm", None, "gy", None)

    def whole(residual):
        plan = Plan(mesh, residual.shape)
        return jax.shard_map(
            functools.partial(on_device, plan),
            mesh=mesh,
            in_specs=(spec,),
            out_specs=spec,
            check_vma=False,
        )(residual)

    return whole
```

```python
import functools
import math

import jax
import jax.numpy as jnp
import numpy as np
from jax import lax
from jax.experimental import pallas as pl
from jax.experimental.pallas import tpu as pltpu
from jax.sharding import PartitionSpec as P

ALPHA_RATIO = 0.95
STEP_SCALE = 0.26
LANES = 128
STRIP = 16
FINE_ROWS = 32
CHUNKS = ((0, 2, 4, 6), (1, 3, 5, 7))
VMEM_BYTES = 40 * 1024 * 1024


def sine_table(count):
    indices = np.arange(count, dtype=np.int64) + 1
    product = indices[:, None] * indices[None, :] % (2 * (count + 1))
    return math.sqrt(2.0 / (count + 1)) * np.sin(np.pi * product / (count + 1))


def spectrum_of(count):
    indices = np.arange(count, dtype=np.float64) + 1.0
    return 2.0 - 2.0 * np.cos(np.pi * indices / (count + 1))


def table_parts(table):
    table = table.astype(np.float32)
    high = table.astype(jnp.bfloat16)
    low = (table - high.astype(np.float32)).astype(jnp.bfloat16)
    return jnp.asarray(high), jnp.asarray(low)


def edge_responses(steps, depth, rows, width):
    freq = np.arange(steps // 2 + 1)
    turn = ALPHA_RATIO ** (1.0 / steps) * np.exp(-2j * np.pi * freq / steps)
    turn = turn[:, None, None]
    mu = spectrum_of(depth)[:, None] + spectrum_of(width)[None, :]
    scaled = STEP_SCALE * turn
    middle = ((1.0 - turn) ** 2 + scaled * (mu + 2.0)) / scaled
    root = np.sqrt(middle * middle / 4.0 - 1.0)
    ratio = middle / 2.0 - root
    ratio = np.where(np.abs(ratio) < 1.0, ratio, middle / 2.0 + root)
    bottom = 1.0 - ratio ** (2 * rows + 2)
    near = ratio * (1.0 - ratio ** (2 * rows)) / bottom
    far = ratio**rows * (1.0 - ratio * ratio) / bottom
    parts = np.stack([near.real, near.imag, far.real, far.imag], axis=1)
    return parts.astype(np.float32)


def parts_of(values):
    high = values.astype(jnp.bfloat16)
    return high, (values - high.astype(jnp.float32)).astype(jnp.bfloat16)


def dot(left, right):
    return jnp.dot(left, right, preferred_element_type=jnp.float32)


def dot_parts(left, right):
    return dot(left[0], right[0]) + dot(left[1], right[0]) + dot(left[0], right[1])


def call(kernel, out_shape, flops, args, scratch=(), out=None):
    smem = pl.BlockSpec(memory_space=pltpu.SMEM)
    vmem = pl.BlockSpec(memory_space=pltpu.VMEM)
    moved = sum(x.size * x.dtype.itemsize for x in args)
    return pl.pallas_call(
        kernel,
        out_shape=out_shape,
        in_specs=[smem] + [vmem] * (len(args) - 1),
        out_specs=out or jax.tree.map(lambda _: vmem, out_shape),
        scratch_shapes=scratch,
        compiler_params=pltpu.CompilerParams(vmem_limit_bytes=VMEM_BYTES),
        cost_estimate=pl.CostEstimate(
            flops=flops, bytes_accessed=moved, transcendentals=0
        ),
    )(*args)


class Plan:
    def __init__(self, mesh, shape):
        self.steps = mesh.shape["tm"]
        self.groups = mesh.shape["gy"]
        self.depth, self.width = shape[1], shape[3]
        self.rows = shape[2] // self.groups
        self.half = self.steps // 2
        self.block = self.width // self.half
        self.folds = self.depth // 2

    def columns(self, owner):
        return pl.ds(pl.multiple_of(owner * self.block, LANES), self.block)


def fill_table(plan, fine, ids, angles, high, low):
    coarse = plan.width // fine
    sine, cosine = (
        angles[2 * coarse + part * fine : 2 * coarse + (part + 1) * fine]
        for part in range(2)
    )

    def step(index, carry):
        rows = pl.ds(pl.multiple_of(index * fine, fine), fine)
        value = angles[pl.ds(index, 1), :] * cosine
        value = value + angles[pl.ds(coarse + index, 1), :] * sine
        high[rows, :], low[rows, :] = parts_of(value)
        return carry

    lax.fori_loop(0, plan.width // fine, step, 0)


def angle_tables(count, fine):
    scale = math.sqrt(2.0 / (count + 1))
    columns = np.arange(count, dtype=np.int64) + 1
    tables = []
    for rows, factor in (
        (np.arange(count // fine, dtype=np.int64) * fine, scale),
        (np.arange(fine, dtype=np.int64) + 1, 1.0),
    ):
        turns = rows[:, None] * columns[None, :] % (2 * (count + 1))
        angle = np.pi * turns / (count + 1)
        tables += [factor * np.sin(angle), factor * np.cos(angle)]
    return jnp.asarray(np.concatenate(tables), jnp.float32)


def fold_tables(plan):
    rows, folds = sine_table(plan.rows), plan.folds
    depth = sine_table(plan.depth)
    tables = [np.kron(depth[parity::2, :folds], rows) for parity in range(2)]
    forth = jnp.stack(table_parts(np.stack(tables)))
    back = jnp.stack(table_parts(np.stack([table.T for table in tables])))
    return forth, back


def by_parity(plan, chunk):
    start = 0
    for parity in range(2):
        places = [c // 2 for c in chunk if c % 2 == parity]
        if places:
            assert places == list(range(places[0], places[0] + len(places)))
            count = len(places) * plan.rows
            first = places[0] * plan.rows
            yield parity, slice(start, start + count), slice(first, first + count)
            start += count


def forward(plan, chunk, ids, both, x, sxh, sxl, *outs):
    place = lax.rem(ids[0], plan.half)
    folds = plan.folds
    mirror = jnp.stack([x[plan.depth - 1 - z] for z in range(folds)])
    left = []
    for parity, _, at in by_parity(plan, chunk):
        folded = x[:folds] - mirror if parity else x[:folds] + mirror
        folded = parts_of(folded.reshape(folds * plan.rows, plan.width))
        table = both[0, parity, at], both[1, parity, at]
        left.append(parts_of(dot_parts(table, folded)))
    for k in range(plan.half):
        columns = plan.columns(place ^ k)
        right = sxh[:, columns], sxl[:, columns]
        value = jnp.concatenate([dot_parts(part, right) for part in left])
        outs[k][...] = value.reshape(len(chunk), plan.rows, plan.block)


def backward(plan, chunk, ready, last, ids, both, sxh, sxl, *refs):
    place = lax.rem(ids[0], plan.half)
    pieces, refs = refs[: plan.half], refs[plan.half :]
    before = dict(zip(ready, refs))
    outs, (high, low) = refs[len(ready) : -2], refs[-2:]
    folds = plan.folds
    shape = folds, plan.rows, plan.block
    total = None
    for k in range(plan.half):
        at = plan.columns(place ^ k)
        piece = parts_of(pieces[k][...].reshape(-1, plan.block))
        value = dot_parts(piece, (sxh[at, :], sxl[at, :]))
        total = value if total is None else total + value
    high[...], low[...] = parts_of(total)
    for j in range(plan.half):
        columns = pl.ds(j * plan.block, plan.block)
        sums = {parity: before[parity][:, :, columns] for parity in ready}
        for parity, rows, at in by_parity(plan, chunk):
            table = both[0, parity, :, at], both[1, parity, :, at]
            value = dot_parts(table, (high[rows, columns], low[rows, columns]))
            value = value.reshape(shape)
            sums[parity] = sums[parity] + value if parity in sums else value
        if not last:
            for parity, out in zip(sorted(sums), outs):
                out[:, :, columns] = sums[parity]
            continue
        out, held, sent = outs
        held[j, :folds] = sums[0] + sums[1]
        other = sums[0] - sums[1]
        for z in range(folds):
            held[j, plan.depth - 1 - z] = other[z]
        pltpu.make_async_copy(held.at[j], out.at[:, :, columns], sent.at[j]).start()
    if last:
        for j in range(plan.half):
            columns = pl.ds(j * plan.block, plan.block)
            pltpu.make_async_copy(held.at[j], out.at[:, :, columns], sent.at[j]).wait()


def per_strip(plan, place, smu_z, smu_y, smu_x, edges, body):
    across = smu_x[:, plan.columns(place)]

    def step(index, carry):
        rows = pl.ds(pl.multiple_of(index * STRIP, STRIP), STRIP)
        plane = across + smu_y[rows, :]
        weights = edges[rows, 0:1], edges[rows, 1:2]
        for u in range(smu_z.shape[0]):
            body(u, rows, plane + smu_z[u : u + 1, :], weights)
        return carry

    lax.fori_loop(0, plan.rows // STRIP, step, 0)


class Cyclic:
    def __init__(self, smu, half):
        self.kappa = kappa = 2.0 - smu
        values = [jnp.zeros_like(kappa), jnp.ones_like(kappa)]
        for _ in range(half):
            values.append(kappa * values[-1] - values[-2])
        self.up, self.at, self.down = values[-1], values[-2], values[-3]
        det = (1.0 - ALPHA_RATIO) ** 2 + ALPHA_RATIO * (
            smu * (4.0 - smu) * (self.at * self.at)
        )
        inverse = 1.0 / det
        self.even = (0.5 * (1.0 - ALPHA_RATIO)) * (self.up - self.down) * inverse
        self.odd = (0.5 * (1.0 + ALPHA_RATIO)) * self.at * inverse

    def run(self, before, last, sources):
        values = []
        for source in sources:
            value = self.kappa * last - before
            before, last = last, value if source is None else value + source
            values.append(last)
        return before, last, values

    def start(self, sources):
        last = sources[0]
        before, last, _ = self.run(last, self.kappa * last + sources[1], sources[2:])
        return before, last

    def entry(self, p0, p1):
        return (
            self.even * p0 + self.odd * (2.0 * p1 - self.kappa * p0),
            self.even * p1 + self.odd * (self.kappa * p1 - 2.0 * p0),
        )

    def back(self, p0, p1):
        return self.up * p0 - self.at * p1, self.at * p0 - self.down * p1


def by_place(plan, place, body):
    for case in range(plan.half):
        pl.when(place == case)(functools.partial(body, case))


def half_end(plan, ids, smu_z, smu_y, smu_x, edges, *refs):
    pieces = refs[: plan.half]
    ends, seen, sums = refs[plan.half :]
    steps, half = plan.steps, plan.half
    place = lax.rem(ids[0], half)
    mine = ids[0] // half
    leaving = jnp.where(mine == 0, 1.0, ALPHA_RATIO).astype(jnp.float32)
    sums[...] = jnp.zeros_like(sums)

    def with_place(case):
        def body(u, rows, smu, weights):
            cyclic = Cyclic(smu, half)
            sources = [pieces[case ^ j][u, rows, :] for j in range(half)]
            before, last = cyclic.start(sources)
            ends[0, u, rows, :] = before
            ends[1, u, rows, :] = last
            entry = cyclic.entry(ALPHA_RATIO * before, ALPHA_RATIO * last)
            before, last, own = cyclic.run(*entry, sources)
            _, _, other = cyclic.run(leaving * before, leaving * last, [None] * half)
            for values, window in ((own, mine), (other, 1 - mine)):
                for j, value in enumerate(values):
                    for edge in range(2):
                        term = weights[edge] * value
                        term = sum(term[i : i + 8] for i in range(0, STRIP, 8))
                        sums[2 * (window * half + j) + edge, u] += term

        per_strip(plan, place, smu_z, smu_y, smu_x, edges, body)

    by_place(plan, place, with_place)
    seen[...] = jnp.sum(sums[...], axis=2)


def c_mul(a, b):
    return a[0] * b[0] - a[1] * b[1], a[0] * b[1] + a[1] * b[0]


def c_add(a, b):
    return a[0] + b[0], a[1] + b[1]


def c_gap(a, b):
    product = c_mul(a, b)
    real, imag = 1.0 - product[0], -product[1]
    inverse = 1.0 / (real * real + imag * imag)
    return real * inverse, -imag * inverse


def join_rows(plan, ids, responses, *refs):
    groups, steps = plan.groups, plan.steps
    views, out, seen, above, below = refs
    place = lax.rem(ids[0], plan.half)
    me = ids[1]
    columns = plan.columns(place)
    for k in range(groups):
        seen[me ^ k] = views[k]
    radius = ALPHA_RATIO ** (1.0 / steps)
    grow = [radius**n for n in range(steps)]
    nothing = jnp.zeros(out.shape[1:], jnp.float32)
    for freq in range(steps // 2 + 1):
        angle = [2.0 * math.pi * (freq * n % steps) / steps for n in range(steps)]

        def spectrum(block, edge):
            real, imag = nothing, nothing
            for n in range(steps):
                value = seen[block, 2 * n + edge]
                real = real + value * np.float32(grow[n] * math.cos(angle[n]))
                if freq % (steps // 2):
                    imag = imag - value * np.float32(grow[n] * math.sin(angle[n]))
            return real, imag

        head = [spectrum(block, 0) for block in range(groups)]
        tail = [spectrum(block, 1) for block in range(groups)]
        near, far = (
            tuple(
                responses[freq, 2 * kind + part, :, columns]
                for part in range(2)
            )
            for kind in range(2)
        )
        square = c_mul(far, far)
        gammas, downs, ups = [near], [tail[0]], [head[groups - 1]]
        for d in range(1, groups - 1):
            gamma = gammas[-1]
            gap = c_gap(gamma, near)
            through = c_mul(far, gap)
            e = groups - 1 - d
            downs.append(
                c_add(
                    tail[d], c_mul(through, c_add(downs[-1], c_mul(gamma, head[d])))
                )
            )
            ups.append(
                c_add(head[e], c_mul(through, c_add(ups[-1], c_mul(gamma, tail[e]))))
            )
            gammas.append(c_add(near, c_mul(square, c_mul(gamma, gap))))
        for d in range(groups - 1):
            down, up = downs[d], ups[groups - 2 - d]
            from_top, from_end = gammas[d], gammas[groups - 2 - d]
            gap = c_gap(from_top, from_end)
            last = c_mul(c_add(down, c_mul(from_top, up)), gap)
            start = c_mul(c_add(up, c_mul(from_end, down)), gap)
            for part in range(2):
                above[d + 1, 2 * freq + part] = last[part]
                below[d, 2 * freq + part] = start[part]
        for part in range(2):
            above[0, 2 * freq + part] = nothing
            below[groups - 1, 2 * freq + part] = nothing
    for edge, side in enumerate((above, below)):
        parts = [side[me, i] for i in range(steps + 2)]
        for n in range(steps):
            total = nothing
            shrink = STEP_SCALE / (steps * grow[n])
            if n == steps - 1:
                shrink *= ALPHA_RATIO
            for freq in range(steps // 2 + 1):
                angle = 2.0 * math.pi * (freq * n % steps) / steps
                single = freq % (steps // 2) == 0
                weight = shrink if single else 2.0 * shrink
                total = total + parts[2 * freq] * np.float32(weight * math.cos(angle))
                if not single:
                    total = total - parts[2 * freq + 1] * np.float32(
                        weight * math.sin(angle)
                    )
            out[2 * ((n + 1) % steps) + edge] = total


def half_solve(plan, ids, smu_z, smu_y, smu_x, edges, *refs):
    pieces = refs[: plan.half]
    far, beside, beside_far = refs[plan.half : plan.half + 3]
    outs = refs[plan.half + 3 :]
    half = plan.half
    place = lax.rem(ids[0], half)
    mine = ids[0] // half
    entering = jnp.where(mine == 0, ALPHA_RATIO, 1.0).astype(jnp.float32)

    def with_place(case):
        def body(u, rows, smu, weights):
            cyclic = Cyclic(smu, half)

            def source(window, j):
                total = None
                for edge in range(2):
                    at = 2 * (window * half + j) + edge
                    row = beside[at, u : u + 1, :] + beside_far[at, u : u + 1, :]
                    term = weights[edge] * row
                    total = term if total is None else total + term
                return total

            own = [pieces[case ^ j][u, rows, :] + source(mine, j) for j in range(half)]
            other = [source(1 - mine, j) for j in range(half)]
            before, last = cyclic.start(other)
            before = entering * (before + far[0, u, rows, :])
            last = entering * (last + far[1, u, rows, :])
            before, last = cyclic.back(before, last)
            near = cyclic.start(own)
            entry = cyclic.entry(
                before + ALPHA_RATIO * near[0], last + ALPHA_RATIO * near[1]
            )
            _, _, values = cyclic.run(*entry, own)
            for j, value in enumerate(values):
                outs[case ^ j][u, rows, :] = value

        per_strip(plan, place, smu_z, smu_y, smu_x, edges, body)

    by_place(plan, place, with_place)


def spread(plan, pieces):
    moved = [swap(pieces[k], "tm", plan.steps, k) for k in range(plan.half - 1, -1, -1)]
    return moved[::-1]


def swap(values, axis, count, distance):
    if distance == 0:
        return values
    return lax.ppermute(values, axis, [(i, i ^ distance) for i in range(count)])


def on_device(plan, residual):
    steps, groups, half = plan.steps, plan.groups, plan.half
    ids = jnp.stack([lax.axis_index("tm"), lax.axis_index("gy")]).astype(jnp.int32)
    sine_rows = sine_table(plan.rows)
    smu_z, smu_y, smu_x = (
        STEP_SCALE * spectrum_of(count) for count in (plan.depth, plan.rows, plan.width)
    )
    smu_y = jnp.asarray(smu_y[:, None], jnp.float32)
    smu_x = jnp.asarray(smu_x[None, :], jnp.float32)
    edges = jnp.asarray(sine_rows[:, [0, plan.rows - 1]], jnp.float32)
    responses = edge_responses(steps, plan.depth, plan.rows, plan.width)
    field = residual[0]
    f32 = functools.partial(jax.ShapeDtypeStruct, dtype=jnp.float32)
    forth, back = fold_tables(plan)
    tables = call(
        functools.partial(fill_table, plan, FINE_ROWS),
        [jax.ShapeDtypeStruct((plan.width, plan.width), jnp.bfloat16)] * 2,
        4000 * plan.width * plan.width,
        (ids, angle_tables(plan.width, FINE_ROWS)),
    )
    work = []
    for chunk in CHUNKS:
        modes = f32((len(chunk), plan.rows, plan.block))
        count = len(chunk) * plan.rows * plan.width
        flops = 6 * count * (plan.width + plan.folds * plan.rows)
        pieces = call(
            functools.partial(forward, plan, chunk),
            [modes] * half,
            flops,
            (ids, forth, field, *tables),
        )
        pieces = spread(plan, pieces)
        smu_own = jnp.asarray(smu_z[list(chunk), None], jnp.float32)
        work.append((chunk, modes, flops, (ids, smu_own, smu_y, smu_x, edges), pieces))
    first, second = work[0][-1], work[1][-1]
    first[0], second[0] = lax.optimization_barrier((first[0], second[0]))
    ended = []
    for at, (chunk, modes, flops, small, pieces) in enumerate(work):
        seen = f32((2 * steps, len(chunk), plan.block))
        ends, view = call(
            functools.partial(half_end, plan),
            [f32((2,) + modes.shape), seen],
            (3000 if at else 40000) * modes.size * half,
            (*small, *pieces),
            [pltpu.VMEM((2 * steps, len(chunk), 8, plan.block), jnp.float32)],
        )
        ended.append([ends, seen, view])
    sums = {}
    far = None
    for (chunk, modes, flops, small, pieces), (ends, seen, view) in zip(work, ended):
        if far is not None:
            ends, far, beside_far = lax.optimization_barrier((ends, far, beside_far))
        far = swap(ends, "tm", steps, half)
        views = view[None]
        while views.shape[0] < groups:
            beyond = swap(views, "gy", groups, views.shape[0])
            views = jnp.concatenate([views, beyond])
        sides = pltpu.VMEM((groups, steps + 2) + seen.shape[1:], jnp.float32)
        beside = call(
            functools.partial(join_rows, plan),
            seen,
            100 * seen.size,
            (ids, jnp.asarray(responses[:, :, list(chunk)]), views),
            [pltpu.VMEM((groups,) + seen.shape, jnp.float32), sides, sides],
        )
        beside_far = swap(beside, "tm", steps, half)
        pieces = call(
            functools.partial(half_solve, plan),
            [modes] * half,
            100 * modes.size * half,
            (*small, *pieces, far, beside, beside_far),
        )
        pieces = spread(plan, pieces)
        last = chunk == CHUNKS[-1]
        part = pltpu.VMEM((len(chunk) * plan.rows, plan.width), jnp.bfloat16)
        hold = [part, part]
        if last:
            block = field.shape[:2] + (plan.block,)
            hold = [
                pltpu.VMEM((half,) + block, jnp.float32),
                pltpu.SemaphoreType.DMA((half,)),
            ] + hold
        ready = tuple(sorted(sums))
        parities = sorted(set(ready) | {c % 2 for c in chunk})
        result = call(
            functools.partial(backward, plan, chunk, ready, last),
            f32(field.shape)
            if last
            else [f32((plan.folds,) + field.shape[1:])] * len(parities),
            flops,
            (ids, back, *tables, *pieces, *(sums[parity] for parity in ready)),
            hold,
            pl.BlockSpec(memory_space=pltpu.HBM) if last else None,
        )
        if not last:
            sums = dict(zip(parities, result))
    return result[None]


def solution(mesh):
    spec = P("tm", None, "gy", None)

    def whole(residual):
        plan = Plan(mesh, residual.shape)
        return jax.shard_map(
            functools.partial(on_device, plan),
            mesh=mesh,
            in_specs=(spec,),
            out_specs=spec,
            check_vma=False,
        )(residual)

    return whole
```

```python
import functools
import math

import jax
import jax.numpy as jnp
import numpy as np
from jax import lax
from jax.experimental import pallas as pl
from jax.experimental.pallas import tpu as pltpu
from jax.sharding import PartitionSpec as P

ALPHA_RATIO = 0.95
STEP_SCALE = 0.26
LANES = 128
STRIP = 16
FINE_ROWS = 32
CHUNKS = ((0, 2, 4, 6), (1, 3, 5, 7))
VMEM_BYTES = 40 * 1024 * 1024


def sine_table(count):
    indices = np.arange(count, dtype=np.int64) + 1
    product = indices[:, None] * indices[None, :] % (2 * (count + 1))
    return math.sqrt(2.0 / (count + 1)) * np.sin(np.pi * product / (count + 1))


def spectrum_of(count):
    indices = np.arange(count, dtype=np.float64) + 1.0
    return 2.0 - 2.0 * np.cos(np.pi * indices / (count + 1))


def table_parts(table):
    table = table.astype(np.float32)
    high = table.astype(jnp.bfloat16)
    low = (table - high.astype(np.float32)).astype(jnp.bfloat16)
    return jnp.asarray(high), jnp.asarray(low)


def edge_responses(steps, depth, rows, width):
    freq = np.arange(steps // 2 + 1)
    turn = ALPHA_RATIO ** (1.0 / steps) * np.exp(-2j * np.pi * freq / steps)
    turn = turn[:, None, None]
    mu = spectrum_of(depth)[:, None] + spectrum_of(width)[None, :]
    scaled = STEP_SCALE * turn
    middle = ((1.0 - turn) ** 2 + scaled * (mu + 2.0)) / scaled
    root = np.sqrt(middle * middle / 4.0 - 1.0)
    ratio = middle / 2.0 - root
    ratio = np.where(np.abs(ratio) < 1.0, ratio, middle / 2.0 + root)
    bottom = 1.0 - ratio ** (2 * rows + 2)
    near = ratio * (1.0 - ratio ** (2 * rows)) / bottom
    far = ratio**rows * (1.0 - ratio * ratio) / bottom
    parts = np.stack([near.real, near.imag, far.real, far.imag], axis=1)
    return parts.astype(np.float32)


def parts_of(values):
    high = values.astype(jnp.bfloat16)
    return high, (values - high.astype(jnp.float32)).astype(jnp.bfloat16)


def dot(left, right):
    return jnp.dot(left, right, preferred_element_type=jnp.float32)


def dot_parts(left, right):
    return dot(left[0], right[0]) + dot(left[1], right[0]) + dot(left[0], right[1])


def call(kernel, out_shape, flops, args, scratch=(), out=None):
    smem = pl.BlockSpec(memory_space=pltpu.SMEM)
    vmem = pl.BlockSpec(memory_space=pltpu.VMEM)
    moved = sum(x.size * x.dtype.itemsize for x in args)
    return pl.pallas_call(
        kernel,
        out_shape=out_shape,
        in_specs=[smem] + [vmem] * (len(args) - 1),
        out_specs=out or jax.tree.map(lambda _: vmem, out_shape),
        scratch_shapes=scratch,
        compiler_params=pltpu.CompilerParams(vmem_limit_bytes=VMEM_BYTES),
        cost_estimate=pl.CostEstimate(
            flops=flops, bytes_accessed=moved, transcendentals=0
        ),
    )(*args)


class Plan:
    def __init__(self, mesh, shape):
        self.steps = mesh.shape["tm"]
        self.groups = mesh.shape["gy"]
        self.depth, self.width = shape[1], shape[3]
        self.rows = shape[2] // self.groups
        self.half = self.steps // 2
        self.block = self.width // self.half
        self.folds = self.depth // 2

    def columns(self, owner):
        return pl.ds(pl.multiple_of(owner * self.block, LANES), self.block)


def fill_table(plan, fine, ids, angles, high, low):
    coarse = plan.width // fine
    sine, cosine = (
        angles[2 * coarse + part * fine : 2 * coarse + (part + 1) * fine]
        for part in range(2)
    )

    def step(index, carry):
        rows = pl.ds(pl.multiple_of(index * fine, fine), fine)
        value = angles[pl.ds(index, 1), :] * cosine
        value = value + angles[pl.ds(coarse + index, 1), :] * sine
        high[rows, :], low[rows, :] = parts_of(value)
        return carry

    lax.fori_loop(0, plan.width // fine, step, 0)


def angle_tables(count, fine):
    scale = math.sqrt(2.0 / (count + 1))
    columns = np.arange(count, dtype=np.int64) + 1
    tables = []
    for rows, factor in (
        (np.arange(count // fine, dtype=np.int64) * fine, scale),
        (np.arange(fine, dtype=np.int64) + 1, 1.0),
    ):
        turns = rows[:, None] * columns[None, :] % (2 * (count + 1))
        angle = np.pi * turns / (count + 1)
        tables += [factor * np.sin(angle), factor * np.cos(angle)]
    return jnp.asarray(np.concatenate(tables), jnp.float32)


def fold_tables(plan):
    rows, folds = sine_table(plan.rows), plan.folds
    depth = sine_table(plan.depth)
    tables = [np.kron(depth[parity::2, :folds], rows) for parity in range(2)]
    forth = jnp.stack(table_parts(np.stack(tables)))
    back = jnp.stack(table_parts(np.stack([table.T for table in tables])))
    return forth, back


def by_parity(plan, chunk):
    start = 0
    for parity in range(2):
        places = [c // 2 for c in chunk if c % 2 == parity]
        if places:
            assert places == list(range(places[0], places[0] + len(places)))
            count = len(places) * plan.rows
            first = places[0] * plan.rows
            yield parity, slice(start, start + count), slice(first, first + count)
            start += count


def forward(plan, chunk, ids, both, x, sxh, sxl, *outs):
    place = lax.rem(ids[0], plan.half)
    folds = plan.folds
    mirror = jnp.stack([x[plan.depth - 1 - z] for z in range(folds)])
    left = []
    for parity, _, at in by_parity(plan, chunk):
        folded = x[:folds] - mirror if parity else x[:folds] + mirror
        folded = parts_of(folded.reshape(folds * plan.rows, plan.width))
        table = both[0, parity, at], both[1, parity, at]
        left.append(parts_of(dot_parts(table, folded)))
    for k in range(plan.half):
        columns = plan.columns(place ^ k)
        right = sxh[:, columns], sxl[:, columns]
        value = jnp.concatenate([dot_parts(part, right) for part in left])
        outs[k][...] = value.reshape(len(chunk), plan.rows, plan.block)


def backward(plan, chunk, ready, last, ids, both, sxh, sxl, *refs):
    place = lax.rem(ids[0], plan.half)
    pieces, refs = refs[: plan.half], refs[plan.half :]
    before = dict(zip(ready, refs))
    outs, (high, low) = refs[len(ready) : -2], refs[-2:]
    folds = plan.folds
    shape = folds, plan.rows, plan.block
    total = None
    for k in range(plan.half):
        at = plan.columns(place ^ k)
        piece = parts_of(pieces[k][...].reshape(-1, plan.block))
        value = dot_parts(piece, (sxh[at, :], sxl[at, :]))
        total = value if total is None else total + value
    high[...], low[...] = parts_of(total)
    for j in range(plan.half):
        columns = pl.ds(j * plan.block, plan.block)
        sums = {parity: before[parity][:, :, columns] for parity in ready}
        for parity, rows, at in by_parity(plan, chunk):
            table = both[0, parity, :, at], both[1, parity, :, at]
            value = dot_parts(table, (high[rows, columns], low[rows, columns]))
            value = value.reshape(shape)
            sums[parity] = sums[parity] + value if parity in sums else value
        if not last:
            for parity, out in zip(sorted(sums), outs):
                out[:, :, columns] = sums[parity]
            continue
        out, held, sent = outs
        held[j, :folds] = sums[0] + sums[1]
        other = sums[0] - sums[1]
        for z in range(folds):
            held[j, plan.depth - 1 - z] = other[z]
        pltpu.make_async_copy(held.at[j], out.at[:, :, columns], sent.at[j]).start()
    if last:
        for j in range(plan.half):
            columns = pl.ds(j * plan.block, plan.block)
            pltpu.make_async_copy(held.at[j], out.at[:, :, columns], sent.at[j]).wait()


def per_strip(plan, place, smu_z, smu_y, smu_x, edges, body):
    across = smu_x[:, plan.columns(place)]

    def step(index, carry):
        rows = pl.ds(pl.multiple_of(index * STRIP, STRIP), STRIP)
        plane = across + smu_y[rows, :]
        weights = edges[rows, 0:1], edges[rows, 1:2]
        for u in range(smu_z.shape[0]):
            body(u, rows, plane + smu_z[u : u + 1, :], weights)
        return carry

    lax.fori_loop(0, plan.rows // STRIP, step, 0)


class Cyclic:
    def __init__(self, smu, half):
        self.kappa = kappa = 2.0 - smu
        values = [jnp.zeros_like(kappa), jnp.ones_like(kappa)]
        for _ in range(half):
            values.append(kappa * values[-1] - values[-2])
        self.up, self.at, self.down = values[-1], values[-2], values[-3]
        det = (1.0 - ALPHA_RATIO) ** 2 + ALPHA_RATIO * (
            smu * (4.0 - smu) * (self.at * self.at)
        )
        inverse = 1.0 / det
        self.even = (0.5 * (1.0 - ALPHA_RATIO)) * (self.up - self.down) * inverse
        self.odd = (0.5 * (1.0 + ALPHA_RATIO)) * self.at * inverse

    def run(self, before, last, sources):
        values = []
        for source in sources:
            value = self.kappa * last - before
            before, last = last, value if source is None else value + source
            values.append(last)
        return before, last, values

    def start(self, sources):
        last = sources[0]
        before, last, _ = self.run(last, self.kappa * last + sources[1], sources[2:])
        return before, last

    def entry(self, p0, p1):
        return (
            self.even * p0 + self.odd * (2.0 * p1 - self.kappa * p0),
            self.even * p1 + self.odd * (self.kappa * p1 - 2.0 * p0),
        )

    def back(self, p0, p1):
        return self.up * p0 - self.at * p1, self.at * p0 - self.down * p1


def by_place(plan, place, body):
    for case in range(plan.half):
        pl.when(place == case)(functools.partial(body, case))


def half_end(plan, ids, smu_z, smu_y, smu_x, edges, *refs):
    pieces = refs[: plan.half]
    ends, seen, sums = refs[plan.half :]
    steps, half = plan.steps, plan.half
    place = lax.rem(ids[0], half)
    mine = ids[0] // half
    leaving = jnp.where(mine == 0, 1.0, ALPHA_RATIO).astype(jnp.float32)
    sums[...] = jnp.zeros_like(sums)

    def with_place(case):
        def body(u, rows, smu, weights):
            cyclic = Cyclic(smu, half)
            sources = [pieces[case ^ j][u, rows, :] for j in range(half)]
            before, last = cyclic.start(sources)
            ends[0, u, rows, :] = before
            ends[1, u, rows, :] = last
            entry = cyclic.entry(ALPHA_RATIO * before, ALPHA_RATIO * last)
            before, last, own = cyclic.run(*entry, sources)
            _, _, other = cyclic.run(leaving * before, leaving * last, [None] * half)
            for values, window in ((own, mine), (other, 1 - mine)):
                for j, value in enumerate(values):
                    for edge in range(2):
                        term = weights[edge] * value
                        term = sum(term[i : i + 8] for i in range(0, STRIP, 8))
                        sums[2 * (window * half + j) + edge, u] += term

        per_strip(plan, place, smu_z, smu_y, smu_x, edges, body)

    by_place(plan, place, with_place)
    seen[...] = jnp.sum(sums[...], axis=2)


def c_mul(a, b):
    return a[0] * b[0] - a[1] * b[1], a[0] * b[1] + a[1] * b[0]


def c_add(a, b):
    return a[0] + b[0], a[1] + b[1]


def c_gap(a, b):
    product = c_mul(a, b)
    real, imag = 1.0 - product[0], -product[1]
    inverse = 1.0 / (real * real + imag * imag)
    return real * inverse, -imag * inverse


def join_rows(plan, ids, responses, *refs):
    groups, steps = plan.groups, plan.steps
    views, out, seen, above, below = refs
    place = lax.rem(ids[0], plan.half)
    me = ids[1]
    columns = plan.columns(place)
    for k in range(groups):
        seen[me ^ k] = views[k]
    radius = ALPHA_RATIO ** (1.0 / steps)
    grow = [radius**n for n in range(steps)]
    nothing = jnp.zeros(out.shape[1:], jnp.float32)
    for freq in range(steps // 2 + 1):
        angle = [2.0 * math.pi * (freq * n % steps) / steps for n in range(steps)]

        def spectrum(block, edge):
            real, imag = nothing, nothing
            for n in range(steps):
                value = seen[block, 2 * n + edge]
                real = real + value * np.float32(grow[n] * math.cos(angle[n]))
                if freq % (steps // 2):
                    imag = imag - value * np.float32(grow[n] * math.sin(angle[n]))
            return real, imag

        head = [spectrum(block, 0) for block in range(groups)]
        tail = [spectrum(block, 1) for block in range(groups)]
        near, far = (
            tuple(
                responses[freq, 2 * kind + part, :, columns]
                for part in range(2)
            )
            for kind in range(2)
        )
        square = c_mul(far, far)
        gammas, downs, ups = [near], [tail[0]], [head[groups - 1]]
        for d in range(1, groups - 1):
            gamma = gammas[-1]
            gap = c_gap(gamma, near)
            through = c_mul(far, gap)
            e = groups - 1 - d
            downs.append(
                c_add(
                    tail[d], c_mul(through, c_add(downs[-1], c_mul(gamma, head[d])))
                )
            )
            ups.append(
                c_add(head[e], c_mul(through, c_add(ups[-1], c_mul(gamma, tail[e]))))
            )
            gammas.append(c_add(near, c_mul(square, c_mul(gamma, gap))))
        for d in range(groups - 1):
            down, up = downs[d], ups[groups - 2 - d]
            from_top, from_end = gammas[d], gammas[groups - 2 - d]
            gap = c_gap(from_top, from_end)
            last = c_mul(c_add(down, c_mul(from_top, up)), gap)
            start = c_mul(c_add(up, c_mul(from_end, down)), gap)
            for part in range(2):
                above[d + 1, 2 * freq + part] = last[part]
                below[d, 2 * freq + part] = start[part]
        for part in range(2):
            above[0, 2 * freq + part] = nothing
            below[groups - 1, 2 * freq + part] = nothing
    for edge, side in enumerate((above, below)):
        parts = [side[me, i] for i in range(steps + 2)]
        for n in range(steps):
            total = nothing
            shrink = STEP_SCALE / (steps * grow[n])
            if n == steps - 1:
                shrink *= ALPHA_RATIO
            for freq in range(steps // 2 + 1):
                angle = 2.0 * math.pi * (freq * n % steps) / steps
                single = freq % (steps // 2) == 0
                weight = shrink if single else 2.0 * shrink
                total = total + parts[2 * freq] * np.float32(weight * math.cos(angle))
                if not single:
                    total = total - parts[2 * freq + 1] * np.float32(
                        weight * math.sin(angle)
                    )
            out[2 * ((n + 1) % steps) + edge] = total


def half_solve(plan, ids, smu_z, smu_y, smu_x, edges, *refs):
    pieces = refs[: plan.half]
    far, beside, beside_far = refs[plan.half : plan.half + 3]
    outs = refs[plan.half + 3 :]
    half = plan.half
    place = lax.rem(ids[0], half)
    mine = ids[0] // half
    entering = jnp.where(mine == 0, ALPHA_RATIO, 1.0).astype(jnp.float32)

    def with_place(case):
        def body(u, rows, smu, weights):
            cyclic = Cyclic(smu, half)

            def source(window, j):
                total = None
                for edge in range(2):
                    at = 2 * (window * half + j) + edge
                    row = beside[at, u : u + 1, :] + beside_far[at, u : u + 1, :]
                    term = weights[edge] * row
                    total = term if total is None else total + term
                return total

            own = [pieces[case ^ j][u, rows, :] + source(mine, j) for j in range(half)]
            other = [source(1 - mine, j) for j in range(half)]
            before, last = cyclic.start(other)
            before = entering * (before + far[0, u, rows, :])
            last = entering * (last + far[1, u, rows, :])
            before, last = cyclic.back(before, last)
            near = cyclic.start(own)
            entry = cyclic.entry(
                before + ALPHA_RATIO * near[0], last + ALPHA_RATIO * near[1]
            )
            _, _, values = cyclic.run(*entry, own)
            for j, value in enumerate(values):
                outs[case ^ j][u, rows, :] = value

        per_strip(plan, place, smu_z, smu_y, smu_x, edges, body)

    by_place(plan, place, with_place)


def spread(plan, pieces):
    moved = [swap(pieces[k], "tm", plan.steps, k) for k in range(plan.half - 1, -1, -1)]
    return moved[::-1]


def swap(values, axis, count, distance):
    if distance == 0:
        return values
    return lax.ppermute(values, axis, [(i, i ^ distance) for i in range(count)])


def on_device(plan, residual):
    steps, groups, half = plan.steps, plan.groups, plan.half
    ids = jnp.stack([lax.axis_index("tm"), lax.axis_index("gy")]).astype(jnp.int32)
    sine_rows = sine_table(plan.rows)
    smu_z, smu_y, smu_x = (
        STEP_SCALE * spectrum_of(count) for count in (plan.depth, plan.rows, plan.width)
    )
    smu_y = jnp.asarray(smu_y[:, None], jnp.float32)
    smu_x = jnp.asarray(smu_x[None, :], jnp.float32)
    edges = jnp.asarray(sine_rows[:, [0, plan.rows - 1]], jnp.float32)
    responses = edge_responses(steps, plan.depth, plan.rows, plan.width)
    field = residual[0]
    f32 = functools.partial(jax.ShapeDtypeStruct, dtype=jnp.float32)
    forth, back = fold_tables(plan)
    tables = call(
        functools.partial(fill_table, plan, FINE_ROWS),
        [jax.ShapeDtypeStruct((plan.width, plan.width), jnp.bfloat16)] * 2,
        4000 * plan.width * plan.width,
        (ids, angle_tables(plan.width, FINE_ROWS)),
    )
    work = []
    for chunk in CHUNKS:
        modes = f32((len(chunk), plan.rows, plan.block))
        count = len(chunk) * plan.rows * plan.width
        flops = 6 * count * (plan.width + plan.folds * plan.rows)
        pieces = call(
            functools.partial(forward, plan, chunk),
            [modes] * half,
            flops,
            (ids, forth, field, *tables),
        )
        pieces = spread(plan, pieces)
        smu_own = jnp.asarray(smu_z[list(chunk), None], jnp.float32)
        work.append((chunk, modes, flops, (ids, smu_own, smu_y, smu_x, edges), pieces))
    first, second = work[0][-1], work[1][-1]
    first[0], second[0] = lax.optimization_barrier((first[0], second[0]))
    ended = []
    for at, (chunk, modes, flops, small, pieces) in enumerate(work):
        seen = f32((2 * steps, len(chunk), plan.block))
        ends, view = call(
            functools.partial(half_end, plan),
            [f32((2,) + modes.shape), seen],
            (3000 if at else 40000) * modes.size * half,
            (*small, *pieces),
            [pltpu.VMEM((2 * steps, len(chunk), 8, plan.block), jnp.float32)],
        )
        if at + 1 < len(work):
            later = work[at + 1][-1]
            view, *later[1:-1] = lax.optimization_barrier((view, *later[1:-1]))
        ended.append([ends, seen, view])
    sums = {}
    far = None
    for (chunk, modes, flops, small, pieces), (ends, seen, view) in zip(work, ended):
        if far is not None:
            ends, far, beside_far = lax.optimization_barrier((ends, far, beside_far))
        far = swap(ends, "tm", steps, half)
        views = view[None]
        while views.shape[0] < groups:
            beyond = swap(views, "gy", groups, views.shape[0])
            views = jnp.concatenate([views, beyond])
        sides = pltpu.VMEM((groups, steps + 2) + seen.shape[1:], jnp.float32)
        beside = call(
            functools.partial(join_rows, plan),
            seen,
            100 * seen.size,
            (ids, jnp.asarray(responses[:, :, list(chunk)]), views),
            [pltpu.VMEM((groups,) + seen.shape, jnp.float32), sides, sides],
        )
        beside_far = swap(beside, "tm", steps, half)
        pieces = call(
            functools.partial(half_solve, plan),
            [modes] * half,
            100 * modes.size * half,
            (*small, *pieces, far, beside, beside_far),
        )
        pieces = spread(plan, pieces)
        last = chunk == CHUNKS[-1]
        part = pltpu.VMEM((len(chunk) * plan.rows, plan.width), jnp.bfloat16)
        hold = [part, part]
        if last:
            block = field.shape[:2] + (plan.block,)
            hold = [
                pltpu.VMEM((half,) + block, jnp.float32),
                pltpu.SemaphoreType.DMA((half,)),
            ] + hold
        ready = tuple(sorted(sums))
        parities = sorted(set(ready) | {c % 2 for c in chunk})
        result = call(
            functools.partial(backward, plan, chunk, ready, last),
            f32(field.shape)
            if last
            else [f32((plan.folds,) + field.shape[1:])] * len(parities),
            flops,
            (ids, back, *tables, *pieces, *(sums[parity] for parity in ready)),
            hold,
            pl.BlockSpec(memory_space=pltpu.HBM) if last else None,
        )
        if not last:
            sums = dict(zip(parities, result))
    return result[None]


def solution(mesh):
    spec = P("tm", None, "gy", None)

    def whole(residual):
        plan = Plan(mesh, residual.shape)
        return jax.shard_map(
            functools.partial(on_device, plan),
            mesh=mesh,
            in_specs=(spec,),
            out_specs=spec,
            check_vma=False,
        )(residual)

    return whole
```

```python
import functools
import math

import jax
import jax.numpy as jnp
import numpy as np
from jax import lax
from jax.experimental import pallas as pl
from jax.experimental.pallas import tpu as pltpu
from jax.sharding import PartitionSpec as P

ALPHA_RATIO = 0.95
STEP_SCALE = 0.26
LANES = 128
STRIP = 16
FINE_ROWS = 32
CHUNKS = ((0, 2, 4, 6), (1, 3, 5, 7))
VMEM_BYTES = 40 * 1024 * 1024


def sine_table(count):
    indices = np.arange(count, dtype=np.int64) + 1
    product = indices[:, None] * indices[None, :] % (2 * (count + 1))
    return math.sqrt(2.0 / (count + 1)) * np.sin(np.pi * product / (count + 1))


def spectrum_of(count):
    indices = np.arange(count, dtype=np.float64) + 1.0
    return 2.0 - 2.0 * np.cos(np.pi * indices / (count + 1))


def table_parts(table):
    table = table.astype(np.float32)
    high = table.astype(jnp.bfloat16)
    low = (table - high.astype(np.float32)).astype(jnp.bfloat16)
    return jnp.asarray(high), jnp.asarray(low)


def edge_responses(steps, depth, rows, width):
    freq = np.arange(steps // 2 + 1)
    turn = ALPHA_RATIO ** (1.0 / steps) * np.exp(-2j * np.pi * freq / steps)
    turn = turn[:, None, None]
    mu = spectrum_of(depth)[:, None] + spectrum_of(width)[None, :]
    scaled = STEP_SCALE * turn
    middle = ((1.0 - turn) ** 2 + scaled * (mu + 2.0)) / scaled
    root = np.sqrt(middle * middle / 4.0 - 1.0)
    ratio = middle / 2.0 - root
    ratio = np.where(np.abs(ratio) < 1.0, ratio, middle / 2.0 + root)
    bottom = 1.0 - ratio ** (2 * rows + 2)
    near = ratio * (1.0 - ratio ** (2 * rows)) / bottom
    far = ratio**rows * (1.0 - ratio * ratio) / bottom
    parts = np.stack([near.real, near.imag, far.real, far.imag], axis=1)
    return parts.astype(np.float32)


def parts_of(values):
    high = values.astype(jnp.bfloat16)
    return high, (values - high.astype(jnp.float32)).astype(jnp.bfloat16)


def dot(left, right):
    return jnp.dot(left, right, preferred_element_type=jnp.float32)


def dot_parts(left, right):
    return dot(left[0], right[0]) + dot(left[1], right[0]) + dot(left[0], right[1])


def call(kernel, out_shape, flops, args, scratch=(), out=None):
    smem = pl.BlockSpec(memory_space=pltpu.SMEM)
    vmem = pl.BlockSpec(memory_space=pltpu.VMEM)
    moved = sum(x.size * x.dtype.itemsize for x in args)
    return pl.pallas_call(
        kernel,
        out_shape=out_shape,
        in_specs=[smem] + [vmem] * (len(args) - 1),
        out_specs=out or jax.tree.map(lambda _: vmem, out_shape),
        scratch_shapes=scratch,
        compiler_params=pltpu.CompilerParams(vmem_limit_bytes=VMEM_BYTES),
        cost_estimate=pl.CostEstimate(
            flops=flops, bytes_accessed=moved, transcendentals=0
        ),
    )(*args)


class Plan:
    def __init__(self, mesh, shape):
        self.steps = mesh.shape["tm"]
        self.groups = mesh.shape["gy"]
        self.depth, self.width = shape[1], shape[3]
        self.rows = shape[2] // self.groups
        self.half = self.steps // 2
        self.block = self.width // self.half
        self.folds = self.depth // 2

    def columns(self, owner):
        return pl.ds(pl.multiple_of(owner * self.block, LANES), self.block)


def fill_table(plan, fine, ids, angles, high, low):
    coarse = plan.width // fine
    sine, cosine = (
        angles[2 * coarse + part * fine : 2 * coarse + (part + 1) * fine]
        for part in range(2)
    )

    def step(index, carry):
        rows = pl.ds(pl.multiple_of(index * fine, fine), fine)
        value = angles[pl.ds(index, 1), :] * cosine
        value = value + angles[pl.ds(coarse + index, 1), :] * sine
        high[rows, :], low[rows, :] = parts_of(value)
        return carry

    lax.fori_loop(0, plan.width // fine, step, 0)


def angle_tables(count, fine):
    scale = math.sqrt(2.0 / (count + 1))
    columns = np.arange(count, dtype=np.int64) + 1
    tables = []
    for rows, factor in (
        (np.arange(count // fine, dtype=np.int64) * fine, scale),
        (np.arange(fine, dtype=np.int64) + 1, 1.0),
    ):
        turns = rows[:, None] * columns[None, :] % (2 * (count + 1))
        angle = np.pi * turns / (count + 1)
        tables += [factor * np.sin(angle), factor * np.cos(angle)]
    return jnp.asarray(np.concatenate(tables), jnp.float32)


def fold_tables(plan):
    rows, folds = sine_table(plan.rows), plan.folds
    depth = sine_table(plan.depth)
    tables = [np.kron(depth[parity::2, :folds], rows) for parity in range(2)]
    forth = jnp.stack(table_parts(np.stack(tables)))
    back = jnp.stack(table_parts(np.stack([table.T for table in tables])))
    return forth, back


def by_parity(plan, chunk):
    start = 0
    for parity in range(2):
        places = [c // 2 for c in chunk if c % 2 == parity]
        if places:
            assert places == list(range(places[0], places[0] + len(places)))
            count = len(places) * plan.rows
            first = places[0] * plan.rows
            yield parity, slice(start, start + count), slice(first, first + count)
            start += count


def forward(plan, chunk, ids, both, x, sxh, sxl, *outs):
    place = lax.rem(ids[0], plan.half)
    folds = plan.folds
    mirror = jnp.stack([x[plan.depth - 1 - z] for z in range(folds)])
    left = []
    for parity, _, at in by_parity(plan, chunk):
        folded = x[:folds] - mirror if parity else x[:folds] + mirror
        folded = parts_of(folded.reshape(folds * plan.rows, plan.width))
        table = both[0, parity, at], both[1, parity, at]
        left.append(parts_of(dot_parts(table, folded)))
    for k in range(plan.half):
        columns = plan.columns(place ^ k)
        right = sxh[:, columns], sxl[:, columns]
        value = jnp.concatenate([dot_parts(part, right) for part in left])
        outs[k][...] = value.reshape(len(chunk), plan.rows, plan.block)


def backward(plan, chunk, ready, last, ids, both, sxh, sxl, *refs):
    place = lax.rem(ids[0], plan.half)
    pieces, refs = refs[: plan.half], refs[plan.half :]
    before = dict(zip(ready, refs))
    outs, (high, low) = refs[len(ready) : -2], refs[-2:]
    folds = plan.folds
    shape = folds, plan.rows, plan.block
    total = None
    for k in range(plan.half):
        at = plan.columns(place ^ k)
        piece = parts_of(pieces[k][...].reshape(-1, plan.block))
        value = dot_parts(piece, (sxh[at, :], sxl[at, :]))
        total = value if total is None else total + value
    high[...], low[...] = parts_of(total)
    for j in range(plan.half):
        columns = pl.ds(j * plan.block, plan.block)
        sums = {parity: before[parity][:, :, columns] for parity in ready}
        for parity, rows, at in by_parity(plan, chunk):
            table = both[0, parity, :, at], both[1, parity, :, at]
            value = dot_parts(table, (high[rows, columns], low[rows, columns]))
            value = value.reshape(shape)
            sums[parity] = sums[parity] + value if parity in sums else value
        if not last:
            for parity, out in zip(sorted(sums), outs):
                out[:, :, columns] = sums[parity]
            continue
        out, held, sent = outs
        held[j, :folds] = sums[0] + sums[1]
        other = sums[0] - sums[1]
        for z in range(folds):
            held[j, plan.depth - 1 - z] = other[z]
        pltpu.make_async_copy(held.at[j], out.at[:, :, columns], sent.at[j]).start()
    if last:
        for j in range(plan.half):
            columns = pl.ds(j * plan.block, plan.block)
            pltpu.make_async_copy(held.at[j], out.at[:, :, columns], sent.at[j]).wait()


def per_strip(plan, place, smu_z, smu_y, smu_x, edges, body):
    across = smu_x[:, plan.columns(place)]

    def step(index, carry):
        rows = pl.ds(pl.multiple_of(index * STRIP, STRIP), STRIP)
        plane = across + smu_y[rows, :]
        weights = edges[rows, 0:1], edges[rows, 1:2]
        for u in range(smu_z.shape[0]):
            body(u, rows, plane + smu_z[u : u + 1, :], weights)
        return carry

    lax.fori_loop(0, plan.rows // STRIP, step, 0)


class Cyclic:
    def __init__(self, smu, half):
        self.kappa = kappa = 2.0 - smu
        values = [jnp.zeros_like(kappa), jnp.ones_like(kappa)]
        for _ in range(half):
            values.append(kappa * values[-1] - values[-2])
        self.up, self.at, self.down = values[-1], values[-2], values[-3]
        det = (1.0 - ALPHA_RATIO) ** 2 + ALPHA_RATIO * (
            smu * (4.0 - smu) * (self.at * self.at)
        )
        inverse = 1.0 / det
        self.even = (0.5 * (1.0 - ALPHA_RATIO)) * (self.up - self.down) * inverse
        self.odd = (0.5 * (1.0 + ALPHA_RATIO)) * self.at * inverse

    def run(self, before, last, sources):
        values = []
        for source in sources:
            value = self.kappa * last - before
            before, last = last, value if source is None else value + source
            values.append(last)
        return before, last, values

    def start(self, sources):
        last = sources[0]
        before, last, _ = self.run(last, self.kappa * last + sources[1], sources[2:])
        return before, last

    def entry(self, p0, p1):
        return (
            self.even * p0 + self.odd * (2.0 * p1 - self.kappa * p0),
            self.even * p1 + self.odd * (self.kappa * p1 - 2.0 * p0),
        )

    def back(self, p0, p1):
        return self.up * p0 - self.at * p1, self.at * p0 - self.down * p1


def by_place(plan, place, body):
    for case in range(plan.half):
        pl.when(place == case)(functools.partial(body, case))


def half_end(plan, ids, smu_z, smu_y, smu_x, edges, *refs):
    pieces = refs[: plan.half]
    ends, seen, sums = refs[plan.half :]
    steps, half = plan.steps, plan.half
    place = lax.rem(ids[0], half)
    mine = ids[0] // half
    leaving = jnp.where(mine == 0, 1.0, ALPHA_RATIO).astype(jnp.float32)
    sums[...] = jnp.zeros_like(sums)

    def with_place(case):
        def body(u, rows, smu, weights):
            cyclic = Cyclic(smu, half)
            sources = [pieces[case ^ j][u, rows, :] for j in range(half)]
            before, last = cyclic.start(sources)
            ends[0, u, rows, :] = before
            ends[1, u, rows, :] = last
            entry = cyclic.entry(ALPHA_RATIO * before, ALPHA_RATIO * last)
            before, last, own = cyclic.run(*entry, sources)
            _, _, other = cyclic.run(leaving * before, leaving * last, [None] * half)
            for values, window in ((own, mine), (other, 1 - mine)):
                for j, value in enumerate(values):
                    for edge in range(2):
                        term = weights[edge] * value
                        term = sum(term[i : i + 8] for i in range(0, STRIP, 8))
                        sums[2 * (window * half + j) + edge, u] += term

        per_strip(plan, place, smu_z, smu_y, smu_x, edges, body)

    by_place(plan, place, with_place)
    seen[...] = jnp.sum(sums[...], axis=2)


def c_mul(a, b):
    return a[0] * b[0] - a[1] * b[1], a[0] * b[1] + a[1] * b[0]


def c_add(a, b):
    return a[0] + b[0], a[1] + b[1]


def c_gap(a, b):
    product = c_mul(a, b)
    real, imag = 1.0 - product[0], -product[1]
    inverse = 1.0 / (real * real + imag * imag)
    return real * inverse, -imag * inverse


def join_rows(plan, ids, responses, *refs):
    groups, steps = plan.groups, plan.steps
    views = refs[:groups]
    out, seen, above, below = refs[groups:]
    place = lax.rem(ids[0], plan.half)
    me = ids[1]
    columns = plan.columns(place)
    for k in range(groups):
        seen[me ^ k] = views[k][...]
    radius = ALPHA_RATIO ** (1.0 / steps)
    grow = [radius**n for n in range(steps)]
    nothing = jnp.zeros(out.shape[1:], jnp.float32)
    for freq in range(steps // 2 + 1):
        angle = [2.0 * math.pi * (freq * n % steps) / steps for n in range(steps)]

        def spectrum(block, edge):
            real, imag = nothing, nothing
            for n in range(steps):
                value = seen[block, 2 * n + edge]
                real = real + value * np.float32(grow[n] * math.cos(angle[n]))
                if freq % (steps // 2):
                    imag = imag - value * np.float32(grow[n] * math.sin(angle[n]))
            return real, imag

        head = [spectrum(block, 0) for block in range(groups)]
        tail = [spectrum(block, 1) for block in range(groups)]
        near, far = (
            tuple(
                responses[freq, 2 * kind + part, :, columns]
                for part in range(2)
            )
            for kind in range(2)
        )
        square = c_mul(far, far)
        gammas, downs, ups = [near], [tail[0]], [head[groups - 1]]
        for d in range(1, groups - 1):
            gamma = gammas[-1]
            gap = c_gap(gamma, near)
            through = c_mul(far, gap)
            e = groups - 1 - d
            downs.append(
                c_add(
                    tail[d], c_mul(through, c_add(downs[-1], c_mul(gamma, head[d])))
                )
            )
            ups.append(
                c_add(head[e], c_mul(through, c_add(ups[-1], c_mul(gamma, tail[e]))))
            )
            gammas.append(c_add(near, c_mul(square, c_mul(gamma, gap))))
        for d in range(groups - 1):
            down, up = downs[d], ups[groups - 2 - d]
            from_top, from_end = gammas[d], gammas[groups - 2 - d]
            gap = c_gap(from_top, from_end)
            last = c_mul(c_add(down, c_mul(from_top, up)), gap)
            start = c_mul(c_add(up, c_mul(from_end, down)), gap)
            for part in range(2):
                above[d + 1, 2 * freq + part] = last[part]
                below[d, 2 * freq + part] = start[part]
        for part in range(2):
            above[0, 2 * freq + part] = nothing
            below[groups - 1, 2 * freq + part] = nothing
    for edge, side in enumerate((above, below)):
        parts = [side[me, i] for i in range(steps + 2)]
        for n in range(steps):
            total = nothing
            shrink = STEP_SCALE / (steps * grow[n])
            if n == steps - 1:
                shrink *= ALPHA_RATIO
            for freq in range(steps // 2 + 1):
                angle = 2.0 * math.pi * (freq * n % steps) / steps
                single = freq % (steps // 2) == 0
                weight = shrink if single else 2.0 * shrink
                total = total + parts[2 * freq] * np.float32(weight * math.cos(angle))
                if not single:
                    total = total - parts[2 * freq + 1] * np.float32(
                        weight * math.sin(angle)
                    )
            out[2 * ((n + 1) % steps) + edge] = total


def half_solve(plan, ids, smu_z, smu_y, smu_x, edges, *refs):
    pieces = refs[: plan.half]
    far, beside, beside_far = refs[plan.half : plan.half + 3]
    outs = refs[plan.half + 3 :]
    half = plan.half
    place = lax.rem(ids[0], half)
    mine = ids[0] // half
    entering = jnp.where(mine == 0, ALPHA_RATIO, 1.0).astype(jnp.float32)

    def with_place(case):
        def body(u, rows, smu, weights):
            cyclic = Cyclic(smu, half)

            def source(window, j):
                total = None
                for edge in range(2):
                    at = 2 * (window * half + j) + edge
                    row = beside[at, u : u + 1, :] + beside_far[at, u : u + 1, :]
                    term = weights[edge] * row
                    total = term if total is None else total + term
                return total

            own = [pieces[case ^ j][u, rows, :] + source(mine, j) for j in range(half)]
            other = [source(1 - mine, j) for j in range(half)]
            before, last = cyclic.start(other)
            before = entering * (before + far[0, u, rows, :])
            last = entering * (last + far[1, u, rows, :])
            before, last = cyclic.back(before, last)
            near = cyclic.start(own)
            entry = cyclic.entry(
                before + ALPHA_RATIO * near[0], last + ALPHA_RATIO * near[1]
            )
            _, _, values = cyclic.run(*entry, own)
            for j, value in enumerate(values):
                outs[case ^ j][u, rows, :] = value

        per_strip(plan, place, smu_z, smu_y, smu_x, edges, body)

    by_place(plan, place, with_place)


def swap(values, axis, count, distance):
    if distance == 0:
        return values
    return lax.ppermute(values, axis, [(i, i ^ distance) for i in range(count)])


def on_device(plan, residual):
    steps, groups, half = plan.steps, plan.groups, plan.half
    ids = jnp.stack([lax.axis_index("tm"), lax.axis_index("gy")]).astype(jnp.int32)
    sine_rows = sine_table(plan.rows)
    smu_z, smu_y, smu_x = (
        STEP_SCALE * spectrum_of(count) for count in (plan.depth, plan.rows, plan.width)
    )
    smu_y = jnp.asarray(smu_y[:, None], jnp.float32)
    smu_x = jnp.asarray(smu_x[None, :], jnp.float32)
    edges = jnp.asarray(sine_rows[:, [0, plan.rows - 1]], jnp.float32)
    responses = edge_responses(steps, plan.depth, plan.rows, plan.width)
    field = residual[0]
    f32 = functools.partial(jax.ShapeDtypeStruct, dtype=jnp.float32)
    forth, back = fold_tables(plan)
    tables = call(
        functools.partial(fill_table, plan, FINE_ROWS),
        [jax.ShapeDtypeStruct((plan.width, plan.width), jnp.bfloat16)] * 2,
        4000 * plan.width * plan.width,
        (ids, angle_tables(plan.width, FINE_ROWS)),
    )
    work = []
    for chunk in CHUNKS:
        modes = f32((len(chunk), plan.rows, plan.block))
        count = len(chunk) * plan.rows * plan.width
        flops = 6 * count * (plan.width + plan.folds * plan.rows)
        pieces = call(
            functools.partial(forward, plan, chunk),
            [modes] * half,
            flops,
            (ids, forth, field, *tables),
        )
        pieces = [swap(v, "tm", steps, k) for k, v in enumerate(pieces)]
        smu_own = jnp.asarray(smu_z[list(chunk), None], jnp.float32)
        work.append((chunk, modes, flops, (ids, smu_own, smu_y, smu_x, edges), pieces))
    first, second = work[0][-1], work[1][-1]
    first[0], second[0] = lax.optimization_barrier((first[0], second[0]))
    sums = {}
    far = None
    for chunk, modes, flops, small, pieces in work:
        seen = f32((2 * steps, len(chunk), plan.block))
        ends, view = call(
            functools.partial(half_end, plan),
            [f32((2,) + modes.shape), seen],
            100 * modes.size * half,
            (*small, *pieces),
            [pltpu.VMEM((2 * steps, len(chunk), 8, plan.block), jnp.float32)],
        )
        if far is not None:
            ends, far, beside_far = lax.optimization_barrier((ends, far, beside_far))
        far = swap(ends, "tm", steps, half)
        views = [swap(view, "gy", groups, k) for k in range(groups)]
        sides = pltpu.VMEM((groups, steps + 2) + seen.shape[1:], jnp.float32)
        beside = call(
            functools.partial(join_rows, plan),
            seen,
            100 * seen.size,
            (ids, jnp.asarray(responses[:, :, list(chunk)]), *views),
            [pltpu.VMEM((groups,) + seen.shape, jnp.float32), sides, sides],
        )
        beside_far = swap(beside, "tm", steps, half)
        pieces = call(
            functools.partial(half_solve, plan),
            [modes] * half,
            100 * modes.size * half,
            (*small, *pieces, far, beside, beside_far),
        )
        pieces = [swap(v, "tm", steps, k) for k, v in enumerate(pieces)]
        last = chunk == CHUNKS[-1]
        part = pltpu.VMEM((len(chunk) * plan.rows, plan.width), jnp.bfloat16)
        hold = [part, part]
        if last:
            block = field.shape[:2] + (plan.block,)
            hold = [
                pltpu.VMEM((half,) + block, jnp.float32),
                pltpu.SemaphoreType.DMA((half,)),
            ] + hold
        ready = tuple(sorted(sums))
        parities = sorted(set(ready) | {c % 2 for c in chunk})
        result = call(
            functools.partial(backward, plan, chunk, ready, last),
            f32(field.shape)
            if last
            else [f32((plan.folds,) + field.shape[1:])] * len(parities),
            flops,
            (ids, back, *tables, *pieces, *(sums[parity] for parity in ready)),
            hold,
            pl.BlockSpec(memory_space=pltpu.HBM) if last else None,
        )
        if not last:
            sums = dict(zip(parities, result))
    return result[None]


def solution(mesh):
    spec = P("tm", None, "gy", None)

    def whole(residual):
        plan = Plan(mesh, residual.shape)
        return jax.shard_map(
            functools.partial(on_device, plan),
            mesh=mesh,
            in_specs=(spec,),
            out_specs=spec,
            check_vma=False,
        )(residual)

    return whole
```

```python
import functools
import math

import jax
import jax.numpy as jnp
import numpy as np
from jax import lax
from jax.experimental import pallas as pl
from jax.experimental.pallas import tpu as pltpu
from jax.sharding import PartitionSpec as P

ALPHA_RATIO = 0.95
STEP_SCALE = 0.26
LANES = 128
STRIP = 16
FINE_ROWS = 32
CHUNKS = ((0, 2, 4, 6), (1, 3, 5, 7))
VMEM_BYTES = 40 * 1024 * 1024


def sine_table(count):
    indices = np.arange(count, dtype=np.int64) + 1
    product = indices[:, None] * indices[None, :] % (2 * (count + 1))
    return math.sqrt(2.0 / (count + 1)) * np.sin(np.pi * product / (count + 1))


def spectrum_of(count):
    indices = np.arange(count, dtype=np.float64) + 1.0
    return 2.0 - 2.0 * np.cos(np.pi * indices / (count + 1))


def table_parts(table):
    table = table.astype(np.float32)
    high = table.astype(jnp.bfloat16)
    low = (table - high.astype(np.float32)).astype(jnp.bfloat16)
    return jnp.asarray(high), jnp.asarray(low)


def edge_responses(steps, depth, rows, width):
    freq = np.arange(steps // 2 + 1)
    turn = ALPHA_RATIO ** (1.0 / steps) * np.exp(-2j * np.pi * freq / steps)
    turn = turn[:, None, None]
    mu = spectrum_of(depth)[:, None] + spectrum_of(width)[None, :]
    scaled = STEP_SCALE * turn
    middle = ((1.0 - turn) ** 2 + scaled * (mu + 2.0)) / scaled
    root = np.sqrt(middle * middle / 4.0 - 1.0)
    ratio = middle / 2.0 - root
    ratio = np.where(np.abs(ratio) < 1.0, ratio, middle / 2.0 + root)
    bottom = 1.0 - ratio ** (2 * rows + 2)
    near = ratio * (1.0 - ratio ** (2 * rows)) / bottom
    far = ratio**rows * (1.0 - ratio * ratio) / bottom
    parts = np.stack([near.real, near.imag, far.real, far.imag], axis=1)
    return parts.astype(np.float32)


def parts_of(values):
    high = values.astype(jnp.bfloat16)
    return high, (values - high.astype(jnp.float32)).astype(jnp.bfloat16)


def dot(left, right):
    return jnp.dot(left, right, preferred_element_type=jnp.float32)


def dot_parts(left, right):
    return dot(left[0], right[0]) + dot(left[1], right[0]) + dot(left[0], right[1])


def call(kernel, out_shape, flops, args, scratch=(), out=None):
    smem = pl.BlockSpec(memory_space=pltpu.SMEM)
    vmem = pl.BlockSpec(memory_space=pltpu.VMEM)
    moved = sum(x.size * x.dtype.itemsize for x in args)
    return pl.pallas_call(
        kernel,
        out_shape=out_shape,
        in_specs=[smem] + [vmem] * (len(args) - 1),
        out_specs=out or jax.tree.map(lambda _: vmem, out_shape),
        scratch_shapes=scratch,
        compiler_params=pltpu.CompilerParams(vmem_limit_bytes=VMEM_BYTES),
        cost_estimate=pl.CostEstimate(
            flops=flops, bytes_accessed=moved, transcendentals=0
        ),
    )(*args)


class Plan:
    def __init__(self, mesh, shape):
        self.steps = mesh.shape["tm"]
        self.groups = mesh.shape["gy"]
        self.depth, self.width = shape[1], shape[3]
        self.rows = shape[2] // self.groups
        self.half = self.steps // 2
        self.block = self.width // self.half
        self.folds = self.depth // 2

    def columns(self, owner):
        return pl.ds(pl.multiple_of(owner * self.block, LANES), self.block)


def fill_table(plan, fine, ids, angles, high, low):
    coarse = plan.width // fine
    sine, cosine = (
        angles[2 * coarse + part * fine : 2 * coarse + (part + 1) * fine]
        for part in range(2)
    )

    def step(index, carry):
        rows = pl.ds(pl.multiple_of(index * fine, fine), fine)
        value = angles[pl.ds(index, 1), :] * cosine
        value = value + angles[pl.ds(coarse + index, 1), :] * sine
        high[rows, :], low[rows, :] = parts_of(value)
        return carry

    lax.fori_loop(0, plan.width // fine, step, 0)


def angle_tables(count, fine):
    scale = math.sqrt(2.0 / (count + 1))
    columns = np.arange(count, dtype=np.int64) + 1
    tables = []
    for rows, factor in (
        (np.arange(count // fine, dtype=np.int64) * fine, scale),
        (np.arange(fine, dtype=np.int64) + 1, 1.0),
    ):
        turns = rows[:, None] * columns[None, :] % (2 * (count + 1))
        angle = np.pi * turns / (count + 1)
        tables += [factor * np.sin(angle), factor * np.cos(angle)]
    return jnp.asarray(np.concatenate(tables), jnp.float32)


def fold_tables(plan):
    rows, folds = sine_table(plan.rows), plan.folds
    depth = sine_table(plan.depth)
    tables = [np.kron(depth[parity::2, :folds], rows) for parity in range(2)]
    forth = jnp.stack(table_parts(np.stack(tables)))
    back = jnp.stack(table_parts(np.stack([table.T for table in tables])))
    return forth, back


def by_parity(plan, chunk):
    start = 0
    for parity in range(2):
        places = [c // 2 for c in chunk if c % 2 == parity]
        if places:
            assert places == list(range(places[0], places[0] + len(places)))
            count = len(places) * plan.rows
            first = places[0] * plan.rows
            yield parity, slice(start, start + count), slice(first, first + count)
            start += count


def forward(plan, chunk, ids, both, x, sxh, sxl, *refs):
    place = lax.rem(ids[0], plan.half)
    outs, (high, low) = refs[:-2], refs[-2:]
    folds = plan.folds
    mirror = jnp.stack([x[plan.depth - 1 - z] for z in range(folds)])
    left = []
    for parity, _, at in by_parity(plan, chunk):
        folded = x[:folds] - mirror if parity else x[:folds] + mirror
        folded = parts_of(folded.reshape(folds * plan.rows, plan.width))
        table = both[0, parity, at], both[1, parity, at]
        left.append(dot_parts(table, folded))
    high[...], low[...] = parts_of(jnp.concatenate(left))
    for k in range(1, plan.half):
        columns = plan.columns(place ^ k)
        value = dot_parts((high[...], low[...]), (sxh[:, columns], sxl[:, columns]))
        outs[k - 1][...] = value.reshape(len(chunk), plan.rows, plan.block)


def forward_own(plan, chunk, ids, high, low, sxh, sxl, out):
    columns = plan.columns(lax.rem(ids[0], plan.half))
    value = dot_parts((high[...], low[...]), (sxh[:, columns], sxl[:, columns]))
    out[...] = value.reshape(len(chunk), plan.rows, plan.block)


def x_rows(plan, place, pieces, start, sxh, sxl):
    total = None
    for k, piece in enumerate(pieces, start):
        at = plan.columns(place ^ k)
        piece = parts_of(piece[...].reshape(-1, plan.block))
        value = dot_parts(piece, (sxh[at, :], sxl[at, :]))
        total = value if total is None else total + value
    return total


def first_rows(plan, ids, sxh, sxl, *refs):
    place = lax.rem(ids[0], plan.half)
    refs[-1][...] = x_rows(plan, place, refs[:-1], 0, sxh, sxl)


def backward(plan, chunk, ready, last, ids, both, sxh, sxl, *refs):
    place = lax.rem(ids[0], plan.half)
    count = 2 if last else plan.half
    pieces, refs = refs[:count], refs[count:]
    before = dict(zip(ready, refs))
    outs, (high, low) = refs[len(ready) : -2], refs[-2:]
    folds = plan.folds
    shape = folds, plan.rows, plan.block
    if last:
        total = pieces[0][...] + x_rows(plan, place, pieces[1:], plan.half - 1, sxh, sxl)
    else:
        total = x_rows(plan, place, pieces, 0, sxh, sxl)
    high[...], low[...] = parts_of(total)
    for j in range(plan.half):
        columns = pl.ds(j * plan.block, plan.block)
        sums = {parity: before[parity][:, :, columns] for parity in ready}
        for parity, rows, at in by_parity(plan, chunk):
            table = both[0, parity, :, at], both[1, parity, :, at]
            value = dot_parts(table, (high[rows, columns], low[rows, columns]))
            value = value.reshape(shape)
            sums[parity] = sums[parity] + value if parity in sums else value
        if not last:
            for parity, out in zip(sorted(sums), outs):
                out[:, :, columns] = sums[parity]
            continue
        out, held, sent = outs
        held[j, :folds] = sums[0] + sums[1]
        other = sums[0] - sums[1]
        for z in range(folds):
            held[j, plan.depth - 1 - z] = other[z]
        pltpu.make_async_copy(held.at[j], out.at[:, :, columns], sent.at[j]).start()
    if last:
        for j in range(plan.half):
            columns = pl.ds(j * plan.block, plan.block)
            pltpu.make_async_copy(held.at[j], out.at[:, :, columns], sent.at[j]).wait()


def per_strip(plan, place, smu_z, smu_y, smu_x, edges, body):
    across = smu_x[:, plan.columns(place)]

    def step(index, carry):
        rows = pl.ds(pl.multiple_of(index * STRIP, STRIP), STRIP)
        plane = across + smu_y[rows, :]
        weights = edges[rows, 0:1], edges[rows, 1:2]
        for u in range(smu_z.shape[0]):
            body(u, rows, plane + smu_z[u : u + 1, :], weights)
        return carry

    lax.fori_loop(0, plan.rows // STRIP, step, 0)


class Cyclic:
    def __init__(self, smu, half):
        self.kappa = kappa = 2.0 - smu
        values = [jnp.zeros_like(kappa), jnp.ones_like(kappa)]
        for _ in range(half):
            values.append(kappa * values[-1] - values[-2])
        self.up, self.at, self.down = values[-1], values[-2], values[-3]
        det = (1.0 - ALPHA_RATIO) ** 2 + ALPHA_RATIO * (
            smu * (4.0 - smu) * (self.at * self.at)
        )
        inverse = 1.0 / det
        self.even = (0.5 * (1.0 - ALPHA_RATIO)) * (self.up - self.down) * inverse
        self.odd = (0.5 * (1.0 + ALPHA_RATIO)) * self.at * inverse

    def run(self, before, last, sources):
        values = []
        for source in sources:
            value = self.kappa * last - before
            before, last = last, value if source is None else value + source
            values.append(last)
        return before, last, values

    def start(self, sources):
        last = sources[0]
        before, last, _ = self.run(last, self.kappa * last + sources[1], sources[2:])
        return before, last

    def entry(self, p0, p1):
        return (
            self.even * p0 + self.odd * (2.0 * p1 - self.kappa * p0),
            self.even * p1 + self.odd * (self.kappa * p1 - 2.0 * p0),
        )

    def back(self, p0, p1):
        return self.up * p0 - self.at * p1, self.at * p0 - self.down * p1


def by_place(plan, place, body):
    for case in range(plan.half):
        pl.when(place == case)(functools.partial(body, case))


def half_end(plan, ids, smu_z, smu_y, smu_x, edges, *refs):
    pieces, ends = refs[: plan.half], refs[plan.half]
    place = lax.rem(ids[0], plan.half)

    def with_place(case):
        def body(u, rows, smu, weights):
            kappa = 2.0 - smu
            before = pieces[case][u, rows, :]
            last = kappa * before + pieces[case ^ 1][u, rows, :]
            for j in range(2, plan.half):
                value = pieces[case ^ j][u, rows, :]
                before, last = last, kappa * last - before + value
            ends[0, u, rows, :] = before
            ends[1, u, rows, :] = last

        per_strip(plan, place, smu_z, smu_y, smu_x, edges, body)

    by_place(plan, place, with_place)


def edge_rows(plan, ids, smu_z, smu_y, smu_x, edges, *refs):
    pieces = refs[: plan.half]
    ends, seen, sums = refs[plan.half :]
    half = plan.half
    place = lax.rem(ids[0], half)
    mine = ids[0] // half
    leaving = jnp.where(mine == 0, 1.0, ALPHA_RATIO).astype(jnp.float32)
    sums[...] = jnp.zeros_like(sums)

    def with_place(case):
        def body(u, rows, smu, weights):
            cyclic = Cyclic(smu, half)
            sources = [pieces[case ^ j][u, rows, :] for j in range(half)]
            before, last = ends[0, u, rows, :], ends[1, u, rows, :]
            entry = cyclic.entry(ALPHA_RATIO * before, ALPHA_RATIO * last)
            before, last, own = cyclic.run(*entry, sources)
            _, _, other = cyclic.run(leaving * before, leaving * last, [None] * half)
            for values, window in ((own, mine), (other, 1 - mine)):
                for j, value in enumerate(values):
                    for edge in range(2):
                        term = weights[edge] * value
                        term = sum(term[i : i + 8] for i in range(0, STRIP, 8))
                        sums[2 * (window * half + j) + edge, u] += term

        per_strip(plan, place, smu_z, smu_y, smu_x, edges, body)

    by_place(plan, place, with_place)
    seen[...] = jnp.sum(sums[...], axis=2)


def c_mul(a, b):
    return a[0] * b[0] - a[1] * b[1], a[0] * b[1] + a[1] * b[0]


def c_add(a, b):
    return a[0] + b[0], a[1] + b[1]


def c_gap(a, b):
    product = c_mul(a, b)
    real, imag = 1.0 - product[0], -product[1]
    inverse = 1.0 / (real * real + imag * imag)
    return real * inverse, -imag * inverse


def join_rows(plan, ids, responses, *refs):
    groups, steps = plan.groups, plan.steps
    views = refs[:groups]
    out, seen, above, below = refs[groups:]
    place = lax.rem(ids[0], plan.half)
    me = ids[1]
    columns = plan.columns(place)
    for k in range(groups):
        seen[me ^ k] = views[k][...]
    radius = ALPHA_RATIO ** (1.0 / steps)
    grow = [radius**n for n in range(steps)]
    nothing = jnp.zeros(out.shape[1:], jnp.float32)
    for freq in range(steps // 2 + 1):
        angle = [2.0 * math.pi * (freq * n % steps) / steps for n in range(steps)]

        def spectrum(block, edge):
            real, imag = nothing, nothing
            for n in range(steps):
                value = seen[block, 2 * n + edge]
                real = real + value * np.float32(grow[n] * math.cos(angle[n]))
                if freq % (steps // 2):
                    imag = imag - value * np.float32(grow[n] * math.sin(angle[n]))
            return real, imag

        head = [spectrum(block, 0) for block in range(groups)]
        tail = [spectrum(block, 1) for block in range(groups)]
        near, far = (
            tuple(
                responses[freq, 2 * kind + part, :, columns]
                for part in range(2)
            )
            for kind in range(2)
        )
        square = c_mul(far, far)
        gammas, downs, ups = [near], [tail[0]], [head[groups - 1]]
        for d in range(1, groups - 1):
            gamma = gammas[-1]
            gap = c_gap(gamma, near)
            through = c_mul(far, gap)
            e = groups - 1 - d
            downs.append(
                c_add(
                    tail[d], c_mul(through, c_add(downs[-1], c_mul(gamma, head[d])))
                )
            )
            ups.append(
                c_add(head[e], c_mul(through, c_add(ups[-1], c_mul(gamma, tail[e]))))
            )
            gammas.append(c_add(near, c_mul(square, c_mul(gamma, gap))))
        for d in range(groups - 1):
            down, up = downs[d], ups[groups - 2 - d]
            from_top, from_end = gammas[d], gammas[groups - 2 - d]
            gap = c_gap(from_top, from_end)
            last = c_mul(c_add(down, c_mul(from_top, up)), gap)
            start = c_mul(c_add(up, c_mul(from_end, down)), gap)
            for part in range(2):
                above[d + 1, 2 * freq + part] = last[part]
                below[d, 2 * freq + part] = start[part]
        for part in range(2):
            above[0, 2 * freq + part] = nothing
            below[groups - 1, 2 * freq + part] = nothing
    for edge, side in enumerate((above, below)):
        parts = [side[me, i] for i in range(steps + 2)]
        for n in range(steps):
            total = nothing
            shrink = STEP_SCALE / (steps * grow[n])
            if n == steps - 1:
                shrink *= ALPHA_RATIO
            for freq in range(steps // 2 + 1):
                angle = 2.0 * math.pi * (freq * n % steps) / steps
                single = freq % (steps // 2) == 0
                weight = shrink if single else 2.0 * shrink
                total = total + parts[2 * freq] * np.float32(weight * math.cos(angle))
                if not single:
                    total = total - parts[2 * freq + 1] * np.float32(
                        weight * math.sin(angle)
                    )
            out[2 * ((n + 1) % steps) + edge] = total


def half_solve(plan, ids, smu_z, smu_y, smu_x, edges, *refs):
    pieces = refs[: plan.half]
    far, beside, beside_far = refs[plan.half : plan.half + 3]
    outs = refs[plan.half + 3 :]
    half = plan.half
    place = lax.rem(ids[0], half)
    mine = ids[0] // half
    entering = jnp.where(mine == 0, ALPHA_RATIO, 1.0).astype(jnp.float32)

    def with_place(case):
        def body(u, rows, smu, weights):
            cyclic = Cyclic(smu, half)

            def source(window, j):
                total = None
                for edge in range(2):
                    at = 2 * (window * half + j) + edge
                    row = beside[at, u : u + 1, :] + beside_far[at, u : u + 1, :]
                    term = weights[edge] * row
                    total = term if total is None else total + term
                return total

            own = [pieces[case ^ j][u, rows, :] + source(mine, j) for j in range(half)]
            other = [source(1 - mine, j) for j in range(half)]
            before, last = cyclic.start(other)
            before = entering * (before + far[0, u, rows, :])
            last = entering * (last + far[1, u, rows, :])
            before, last = cyclic.back(before, last)
            near = cyclic.start(own)
            entry = cyclic.entry(
                before + ALPHA_RATIO * near[0], last + ALPHA_RATIO * near[1]
            )
            _, _, values = cyclic.run(*entry, own)
            for j, value in enumerate(values):
                outs[case ^ j][u, rows, :] = value

        per_strip(plan, place, smu_z, smu_y, smu_x, edges, body)

    by_place(plan, place, with_place)


def swap(values, axis, count, distance):
    if distance == 0:
        return values
    return lax.ppermute(values, axis, [(i, i ^ distance) for i in range(count)])


def on_device(plan, residual):
    steps, groups, half = plan.steps, plan.groups, plan.half
    ids = jnp.stack([lax.axis_index("tm"), lax.axis_index("gy")]).astype(jnp.int32)
    sine_rows = sine_table(plan.rows)
    smu_z, smu_y, smu_x = (
        STEP_SCALE * spectrum_of(count) for count in (plan.depth, plan.rows, plan.width)
    )
    smu_y = jnp.asarray(smu_y[:, None], jnp.float32)
    smu_x = jnp.asarray(smu_x[None, :], jnp.float32)
    edges = jnp.asarray(sine_rows[:, [0, plan.rows - 1]], jnp.float32)
    responses = edge_responses(steps, plan.depth, plan.rows, plan.width)
    field = residual[0]
    f32 = functools.partial(jax.ShapeDtypeStruct, dtype=jnp.float32)
    forth, back = fold_tables(plan)
    tables = call(
        functools.partial(fill_table, plan, FINE_ROWS),
        [jax.ShapeDtypeStruct((plan.width, plan.width), jnp.bfloat16)] * 2,
        4000 * plan.width * plan.width,
        (ids, angle_tables(plan.width, FINE_ROWS)),
    )
    work = []
    for chunk in CHUNKS:
        modes = f32((len(chunk), plan.rows, plan.block))
        count = len(chunk) * plan.rows * plan.width
        flops = 6 * count * (plan.width + plan.folds * plan.rows)
        part = jax.ShapeDtypeStruct((len(chunk) * plan.rows, plan.width), jnp.bfloat16)
        *pieces, high, low = call(
            functools.partial(forward, plan, chunk),
            [modes] * (half - 1) + [part, part],
            flops,
            (ids, forth, field, *tables),
        )
        own = call(
            functools.partial(forward_own, plan, chunk),
            modes,
            flops // plan.half,
            (ids, high, low, *tables),
        )
        pieces = [own, *pieces]
        pieces = [swap(v, "tm", steps, k) for k, v in enumerate(pieces)]
        smu_own = jnp.asarray(smu_z[list(chunk), None], jnp.float32)
        work.append((chunk, modes, flops, (ids, smu_own, smu_y, smu_x, edges), pieces))
    first, second = work[0][-1], work[1][-1]
    first[0], second[0] = lax.optimization_barrier((first[0], second[0]))
    sums = {}
    far = None
    for chunk, modes, flops, small, pieces in work:
        seen = f32((2 * steps, len(chunk), plan.block))
        ends = call(
            functools.partial(half_end, plan),
            f32((2,) + modes.shape),
            10 * modes.size * half,
            (*small, *pieces),
        )
        view = call(
            functools.partial(edge_rows, plan),
            seen,
            100 * modes.size * half,
            (*small, *pieces, ends),
            [pltpu.VMEM((2 * steps, len(chunk), 8, plan.block), jnp.float32)],
        )
        if far is not None:
            ends, far, beside_far = lax.optimization_barrier((ends, far, beside_far))
        far = swap(ends, "tm", steps, half)
        views = [swap(view, "gy", groups, k) for k in range(groups)]
        sides = pltpu.VMEM((groups, steps + 2) + seen.shape[1:], jnp.float32)
        beside = call(
            functools.partial(join_rows, plan),
            seen,
            100 * seen.size,
            (ids, jnp.asarray(responses[:, :, list(chunk)]), *views),
            [pltpu.VMEM((groups,) + seen.shape, jnp.float32), sides, sides],
        )
        beside_far = swap(beside, "tm", steps, half)
        pieces = call(
            functools.partial(half_solve, plan),
            [modes] * half,
            100 * modes.size * half,
            (*small, *pieces, far, beside, beside_far),
        )
        pieces = [swap(v, "tm", steps, k) for k, v in enumerate(pieces)]
        last = chunk == CHUNKS[-1]
        part = pltpu.VMEM((len(chunk) * plan.rows, plan.width), jnp.bfloat16)
        hold = [part, part]
        if last:
            block = field.shape[:2] + (plan.block,)
            hold = [
                pltpu.VMEM((half,) + block, jnp.float32),
                pltpu.SemaphoreType.DMA((half,)),
            ] + hold
            early = call(
                functools.partial(first_rows, plan),
                f32((len(chunk) * plan.rows, plan.width)),
                flops // 2,
                (ids, *tables, *pieces[:-1]),
            )
            pieces = [early, pieces[-1]]
        ready = tuple(sorted(sums))
        parities = sorted(set(ready) | {c % 2 for c in chunk})
        result = call(
            functools.partial(backward, plan, chunk, ready, last),
            f32(field.shape)
            if last
            else [f32((plan.folds,) + field.shape[1:])] * len(parities),
            flops,
            (ids, back, *tables, *pieces, *(sums[parity] for parity in ready)),
            hold,
            pl.BlockSpec(memory_space=pltpu.HBM) if last else None,
        )
        if not last:
            sums = dict(zip(parities, result))
    return result[None]


def solution(mesh):
    spec = P("tm", None, "gy", None)

    def whole(residual):
        plan = Plan(mesh, residual.shape)
        return jax.shard_map(
            functools.partial(on_device, plan),
            mesh=mesh,
            in_specs=(spec,),
            out_specs=spec,
            check_vma=False,
        )(residual)

    return whole
```

```python
import functools
import math

import jax
import jax.numpy as jnp
import numpy as np
from jax import lax
from jax.experimental import pallas as pl
from jax.experimental.pallas import tpu as pltpu
from jax.sharding import PartitionSpec as P

ALPHA_RATIO = 0.95
STEP_SCALE = 0.26
LANES = 128
STRIP = 16
FINE_ROWS = 32
CHUNKS = ((0, 2, 4, 6), (1, 3, 5, 7))
VMEM_BYTES = 40 * 1024 * 1024


def sine_table(count):
    indices = np.arange(count, dtype=np.int64) + 1
    product = indices[:, None] * indices[None, :] % (2 * (count + 1))
    return math.sqrt(2.0 / (count + 1)) * np.sin(np.pi * product / (count + 1))


def spectrum_of(count):
    indices = np.arange(count, dtype=np.float64) + 1.0
    return 2.0 - 2.0 * np.cos(np.pi * indices / (count + 1))


def table_parts(table):
    table = table.astype(np.float32)
    high = table.astype(jnp.bfloat16)
    low = (table - high.astype(np.float32)).astype(jnp.bfloat16)
    return jnp.asarray(high), jnp.asarray(low)


def edge_responses(steps, depth, rows, width):
    freq = np.arange(steps // 2 + 1)
    turn = ALPHA_RATIO ** (1.0 / steps) * np.exp(-2j * np.pi * freq / steps)
    turn = turn[:, None, None]
    mu = spectrum_of(depth)[:, None] + spectrum_of(width)[None, :]
    scaled = STEP_SCALE * turn
    middle = ((1.0 - turn) ** 2 + scaled * (mu + 2.0)) / scaled
    root = np.sqrt(middle * middle / 4.0 - 1.0)
    ratio = middle / 2.0 - root
    ratio = np.where(np.abs(ratio) < 1.0, ratio, middle / 2.0 + root)
    bottom = 1.0 - ratio ** (2 * rows + 2)
    near = ratio * (1.0 - ratio ** (2 * rows)) / bottom
    far = ratio**rows * (1.0 - ratio * ratio) / bottom
    parts = np.stack([near.real, near.imag, far.real, far.imag], axis=1)
    return parts.astype(np.float32)


def parts_of(values):
    high = values.astype(jnp.bfloat16)
    return high, (values - high.astype(jnp.float32)).astype(jnp.bfloat16)


def dot(left, right):
    return jnp.dot(left, right, preferred_element_type=jnp.float32)


def dot_parts(left, right):
    return dot(left[0], right[0]) + dot(left[1], right[0]) + dot(left[0], right[1])


def call(kernel, out_shape, flops, args, scratch=(), out=None):
    smem = pl.BlockSpec(memory_space=pltpu.SMEM)
    vmem = pl.BlockSpec(memory_space=pltpu.VMEM)
    moved = sum(x.size * x.dtype.itemsize for x in args)
    return pl.pallas_call(
        kernel,
        out_shape=out_shape,
        in_specs=[smem] + [vmem] * (len(args) - 1),
        out_specs=out or jax.tree.map(lambda _: vmem, out_shape),
        scratch_shapes=scratch,
        compiler_params=pltpu.CompilerParams(vmem_limit_bytes=VMEM_BYTES),
        cost_estimate=pl.CostEstimate(
            flops=flops, bytes_accessed=moved, transcendentals=0
        ),
    )(*args)


class Plan:
    def __init__(self, mesh, shape):
        self.steps = mesh.shape["tm"]
        self.groups = mesh.shape["gy"]
        self.depth, self.width = shape[1], shape[3]
        self.rows = shape[2] // self.groups
        self.half = self.steps // 2
        self.block = self.width // self.half
        self.folds = self.depth // 2

    def columns(self, owner):
        return pl.ds(pl.multiple_of(owner * self.block, LANES), self.block)


def fill_table(plan, fine, ids, angles, high, low):
    coarse = plan.width // fine
    sine, cosine = (
        angles[2 * coarse + part * fine : 2 * coarse + (part + 1) * fine]
        for part in range(2)
    )

    def step(index, carry):
        rows = pl.ds(pl.multiple_of(index * fine, fine), fine)
        value = angles[pl.ds(index, 1), :] * cosine
        value = value + angles[pl.ds(coarse + index, 1), :] * sine
        high[rows, :], low[rows, :] = parts_of(value)
        return carry

    lax.fori_loop(0, plan.width // fine, step, 0)


def angle_tables(count, fine):
    scale = math.sqrt(2.0 / (count + 1))
    columns = np.arange(count, dtype=np.int64) + 1
    tables = []
    for rows, factor in (
        (np.arange(count // fine, dtype=np.int64) * fine, scale),
        (np.arange(fine, dtype=np.int64) + 1, 1.0),
    ):
        turns = rows[:, None] * columns[None, :] % (2 * (count + 1))
        angle = np.pi * turns / (count + 1)
        tables += [factor * np.sin(angle), factor * np.cos(angle)]
    return jnp.asarray(np.concatenate(tables), jnp.float32)


def fold_tables(plan):
    rows, folds = sine_table(plan.rows), plan.folds
    depth = sine_table(plan.depth)
    tables = [np.kron(depth[parity::2, :folds], rows) for parity in range(2)]
    forth = jnp.stack(table_parts(np.stack(tables)))
    back = jnp.stack(table_parts(np.stack([table.T for table in tables])))
    return forth, back


def by_parity(plan, chunk):
    start = 0
    for parity in range(2):
        places = [c // 2 for c in chunk if c % 2 == parity]
        if places:
            assert places == list(range(places[0], places[0] + len(places)))
            count = len(places) * plan.rows
            first = places[0] * plan.rows
            yield parity, slice(start, start + count), slice(first, first + count)
            start += count


def forward(plan, chunk, ids, both, x, sxh, sxl, *outs):
    place = lax.rem(ids[0], plan.half)
    folds = plan.folds
    mirror = jnp.stack([x[plan.depth - 1 - z] for z in range(folds)])
    left = []
    for parity, _, at in by_parity(plan, chunk):
        folded = x[:folds] - mirror if parity else x[:folds] + mirror
        folded = parts_of(folded.reshape(folds * plan.rows, plan.width))
        table = both[0, parity, at], both[1, parity, at]
        left.append(parts_of(dot_parts(table, folded)))
    for k in range(plan.half):
        columns = plan.columns(place ^ k)
        right = sxh[:, columns], sxl[:, columns]
        value = jnp.concatenate([dot_parts(part, right) for part in left])
        outs[k][...] = value.reshape(len(chunk), plan.rows, plan.block)


def x_rows(plan, place, pieces, start, sxh, sxl):
    total = None
    for k, piece in enumerate(pieces, start):
        at = plan.columns(place ^ k)
        piece = parts_of(piece[...].reshape(-1, plan.block))
        value = dot_parts(piece, (sxh[at, :], sxl[at, :]))
        total = value if total is None else total + value
    return total


def first_rows(plan, ids, sxh, sxl, *refs):
    place = lax.rem(ids[0], plan.half)
    refs[-1][...] = x_rows(plan, place, refs[:-1], 0, sxh, sxl)


def backward(plan, chunk, ready, last, ids, both, sxh, sxl, *refs):
    place = lax.rem(ids[0], plan.half)
    count = 2 if last else plan.half
    pieces, refs = refs[:count], refs[count:]
    before = dict(zip(ready, refs))
    outs, (high, low) = refs[len(ready) : -2], refs[-2:]
    folds = plan.folds
    shape = folds, plan.rows, plan.block
    if last:
        total = pieces[0][...] + x_rows(plan, place, pieces[1:], plan.half - 1, sxh, sxl)
    else:
        total = x_rows(plan, place, pieces, 0, sxh, sxl)
    high[...], low[...] = parts_of(total)
    for j in range(plan.half):
        columns = pl.ds(j * plan.block, plan.block)
        sums = {parity: before[parity][:, :, columns] for parity in ready}
        for parity, rows, at in by_parity(plan, chunk):
            table = both[0, parity, :, at], both[1, parity, :, at]
            value = dot_parts(table, (high[rows, columns], low[rows, columns]))
            value = value.reshape(shape)
            sums[parity] = sums[parity] + value if parity in sums else value
        if not last:
            for parity, out in zip(sorted(sums), outs):
                out[:, :, columns] = sums[parity]
            continue
        out, held, sent = outs
        held[j, :folds] = sums[0] + sums[1]
        other = sums[0] - sums[1]
        for z in range(folds):
            held[j, plan.depth - 1 - z] = other[z]
        pltpu.make_async_copy(held.at[j], out.at[:, :, columns], sent.at[j]).start()
    if last:
        for j in range(plan.half):
            columns = pl.ds(j * plan.block, plan.block)
            pltpu.make_async_copy(held.at[j], out.at[:, :, columns], sent.at[j]).wait()


def per_strip(plan, place, smu_z, smu_y, smu_x, edges, body, strip=STRIP):
    across = smu_x[:, plan.columns(place)]

    def step(index, carry):
        rows = pl.ds(pl.multiple_of(index * strip, strip), strip)
        plane = across + smu_y[rows, :]
        weights = edges[rows, 0:1], edges[rows, 1:2]
        for u in range(smu_z.shape[0]):
            body(u, rows, plane + smu_z[u : u + 1, :], weights)
        return carry

    lax.fori_loop(0, plan.rows // strip, step, 0)


class Cyclic:
    def __init__(self, smu, half):
        self.kappa = kappa = 2.0 - smu
        values = [jnp.zeros_like(kappa), jnp.ones_like(kappa)]
        for _ in range(half):
            values.append(kappa * values[-1] - values[-2])
        self.up, self.at, self.down = values[-1], values[-2], values[-3]
        det = (1.0 - ALPHA_RATIO) ** 2 + ALPHA_RATIO * (
            smu * (4.0 - smu) * (self.at * self.at)
        )
        inverse = 1.0 / det
        self.even = (0.5 * (1.0 - ALPHA_RATIO)) * (self.up - self.down) * inverse
        self.odd = (0.5 * (1.0 + ALPHA_RATIO)) * self.at * inverse

    def run(self, before, last, sources):
        values = []
        for source in sources:
            value = self.kappa * last - before
            before, last = last, value if source is None else value + source
            values.append(last)
        return before, last, values

    def start(self, sources):
        last = sources[0]
        before, last, _ = self.run(last, self.kappa * last + sources[1], sources[2:])
        return before, last

    def entry(self, p0, p1):
        return (
            self.even * p0 + self.odd * (2.0 * p1 - self.kappa * p0),
            self.even * p1 + self.odd * (self.kappa * p1 - 2.0 * p0),
        )

    def back(self, p0, p1):
        return self.up * p0 - self.at * p1, self.at * p0 - self.down * p1


def by_place(plan, place, body):
    for case in range(plan.half):
        pl.when(place == case)(functools.partial(body, case))


def half_end(plan, ids, smu_z, smu_y, smu_x, edges, *refs):
    pieces = refs[: plan.half]
    ends, seen, sums = refs[plan.half :]
    steps, half = plan.steps, plan.half
    place = lax.rem(ids[0], half)
    mine = ids[0] // half
    leaving = jnp.where(mine == 0, 1.0, ALPHA_RATIO).astype(jnp.float32)
    sums[...] = jnp.zeros_like(sums)

    def with_place(case):
        def body(u, rows, smu, weights):
            cyclic = Cyclic(smu, half)
            sources = [pieces[case ^ j][u, rows, :] for j in range(half)]
            before, last = cyclic.start(sources)
            ends[0, u, rows, :] = before
            ends[1, u, rows, :] = last
            entry = cyclic.entry(ALPHA_RATIO * before, ALPHA_RATIO * last)
            before, last, own = cyclic.run(*entry, sources)
            _, _, other = cyclic.run(leaving * before, leaving * last, [None] * half)
            for values, window in ((own, mine), (other, 1 - mine)):
                for j, value in enumerate(values):
                    for edge in range(2):
                        term = weights[edge] * value
                        term = sum(term[i : i + 8] for i in range(0, STRIP, 8))
                        sums[2 * (window * half + j) + edge, u] += term

        per_strip(plan, place, smu_z, smu_y, smu_x, edges, body)

    by_place(plan, place, with_place)
    seen[...] = jnp.sum(sums[...], axis=2)


def c_mul(a, b):
    return a[0] * b[0] - a[1] * b[1], a[0] * b[1] + a[1] * b[0]


def c_add(a, b):
    return a[0] + b[0], a[1] + b[1]


def c_gap(a, b):
    product = c_mul(a, b)
    real, imag = 1.0 - product[0], -product[1]
    inverse = 1.0 / (real * real + imag * imag)
    return real * inverse, -imag * inverse


def join_rows(plan, ids, responses, *refs):
    groups, steps = plan.groups, plan.steps
    views = refs[:groups]
    out, seen, above, below = refs[groups:]
    place = lax.rem(ids[0], plan.half)
    me = ids[1]
    columns = plan.columns(place)
    for k in range(groups):
        seen[me ^ k] = views[k][...]
    radius = ALPHA_RATIO ** (1.0 / steps)
    grow = [radius**n for n in range(steps)]
    nothing = jnp.zeros(out.shape[1:], jnp.float32)
    for freq in range(steps // 2 + 1):
        angle = [2.0 * math.pi * (freq * n % steps) / steps for n in range(steps)]

        def spectrum(block, edge):
            real, imag = nothing, nothing
            for n in range(steps):
                value = seen[block, 2 * n + edge]
                real = real + value * np.float32(grow[n] * math.cos(angle[n]))
                if freq % (steps // 2):
                    imag = imag - value * np.float32(grow[n] * math.sin(angle[n]))
            return real, imag

        head = [spectrum(block, 0) for block in range(groups)]
        tail = [spectrum(block, 1) for block in range(groups)]
        near, far = (
            tuple(
                responses[freq, 2 * kind + part, :, columns]
                for part in range(2)
            )
            for kind in range(2)
        )
        square = c_mul(far, far)
        gammas, downs, ups = [near], [tail[0]], [head[groups - 1]]
        for d in range(1, groups - 1):
            gamma = gammas[-1]
            gap = c_gap(gamma, near)
            through = c_mul(far, gap)
            e = groups - 1 - d
            downs.append(
                c_add(
                    tail[d], c_mul(through, c_add(downs[-1], c_mul(gamma, head[d])))
                )
            )
            ups.append(
                c_add(head[e], c_mul(through, c_add(ups[-1], c_mul(gamma, tail[e]))))
            )
            gammas.append(c_add(near, c_mul(square, c_mul(gamma, gap))))
        for d in range(groups - 1):
            down, up = downs[d], ups[groups - 2 - d]
            from_top, from_end = gammas[d], gammas[groups - 2 - d]
            gap = c_gap(from_top, from_end)
            last = c_mul(c_add(down, c_mul(from_top, up)), gap)
            start = c_mul(c_add(up, c_mul(from_end, down)), gap)
            for part in range(2):
                above[d + 1, 2 * freq + part] = last[part]
                below[d, 2 * freq + part] = start[part]
        for part in range(2):
            above[0, 2 * freq + part] = nothing
            below[groups - 1, 2 * freq + part] = nothing
    for edge, side in enumerate((above, below)):
        parts = [side[me, i] for i in range(steps + 2)]
        for n in range(steps):
            total = nothing
            shrink = STEP_SCALE / (steps * grow[n])
            if n == steps - 1:
                shrink *= ALPHA_RATIO
            for freq in range(steps // 2 + 1):
                angle = 2.0 * math.pi * (freq * n % steps) / steps
                single = freq % (steps // 2) == 0
                weight = shrink if single else 2.0 * shrink
                total = total + parts[2 * freq] * np.float32(weight * math.cos(angle))
                if not single:
                    total = total - parts[2 * freq + 1] * np.float32(
                        weight * math.sin(angle)
                    )
            out[2 * ((n + 1) % steps) + edge] = total


def half_solve(plan, ids, smu_z, smu_y, smu_x, edges, *refs):
    pieces = refs[: plan.half]
    far, beside, beside_far = refs[plan.half : plan.half + 3]
    outs = refs[plan.half + 3 :]
    half = plan.half
    place = lax.rem(ids[0], half)
    mine = ids[0] // half
    entering = jnp.where(mine == 0, ALPHA_RATIO, 1.0).astype(jnp.float32)

    def with_place(case):
        def body(u, rows, smu, weights):
            cyclic = Cyclic(smu, half)

            def source(window, j):
                total = None
                for edge in range(2):
                    at = 2 * (window * half + j) + edge
                    row = beside[at, u : u + 1, :] + beside_far[at, u : u + 1, :]
                    term = weights[edge] * row
                    total = term if total is None else total + term
                return total

            own = [pieces[case ^ j][u, rows, :] + source(mine, j) for j in range(half)]
            other = [source(1 - mine, j) for j in range(half)]
            before, last = cyclic.start(other)
            before = entering * (before + far[0, u, rows, :])
            last = entering * (last + far[1, u, rows, :])
            before, last = cyclic.back(before, last)
            near = cyclic.start(own)
            entry = cyclic.entry(
                before + ALPHA_RATIO * near[0], last + ALPHA_RATIO * near[1]
            )
            _, _, values = cyclic.run(*entry, own)
            for j, value in enumerate(values):
                outs[case ^ j][u, rows, :] = value

        per_strip(plan, place, smu_z, smu_y, smu_x, edges, body, 2 * STRIP)

    by_place(plan, place, with_place)


def swap(values, axis, count, distance):
    if distance == 0:
        return values
    return lax.ppermute(values, axis, [(i, i ^ distance) for i in range(count)])


def on_device(plan, residual):
    steps, groups, half = plan.steps, plan.groups, plan.half
    ids = jnp.stack([lax.axis_index("tm"), lax.axis_index("gy")]).astype(jnp.int32)
    sine_rows = sine_table(plan.rows)
    smu_z, smu_y, smu_x = (
        STEP_SCALE * spectrum_of(count) for count in (plan.depth, plan.rows, plan.width)
    )
    smu_y = jnp.asarray(smu_y[:, None], jnp.float32)
    smu_x = jnp.asarray(smu_x[None, :], jnp.float32)
    edges = jnp.asarray(sine_rows[:, [0, plan.rows - 1]], jnp.float32)
    responses = edge_responses(steps, plan.depth, plan.rows, plan.width)
    field = residual[0]
    f32 = functools.partial(jax.ShapeDtypeStruct, dtype=jnp.float32)
    forth, back = fold_tables(plan)
    tables = call(
        functools.partial(fill_table, plan, FINE_ROWS),
        [jax.ShapeDtypeStruct((plan.width, plan.width), jnp.bfloat16)] * 2,
        4000 * plan.width * plan.width,
        (ids, angle_tables(plan.width, FINE_ROWS)),
    )
    work = []
    for chunk in CHUNKS:
        modes = f32((len(chunk), plan.rows, plan.block))
        count = len(chunk) * plan.rows * plan.width
        flops = 6 * count * (plan.width + plan.folds * plan.rows)
        pieces = call(
            functools.partial(forward, plan, chunk),
            [modes] * half,
            flops,
            (ids, forth, field, *tables),
        )
        pieces = [swap(v, "tm", steps, k) for k, v in enumerate(pieces)]
        smu_own = jnp.asarray(smu_z[list(chunk), None], jnp.float32)
        work.append((chunk, modes, flops, (ids, smu_own, smu_y, smu_x, edges), pieces))
    first, second = work[0][-1], work[1][-1]
    first[0], second[0] = lax.optimization_barrier((first[0], second[0]))
    sums = {}
    far = None
    for chunk, modes, flops, small, pieces in work:
        seen = f32((2 * steps, len(chunk), plan.block))
        ends, view = call(
            functools.partial(half_end, plan),
            [f32((2,) + modes.shape), seen],
            100 * modes.size * half,
            (*small, *pieces),
            [pltpu.VMEM((2 * steps, len(chunk), 8, plan.block), jnp.float32)],
        )
        if far is not None:
            ends, far, beside_far = lax.optimization_barrier((ends, far, beside_far))
        far = swap(ends, "tm", steps, half)
        views = [swap(view, "gy", groups, k) for k in range(groups)]
        sides = pltpu.VMEM((groups, steps + 2) + seen.shape[1:], jnp.float32)
        beside = call(
            functools.partial(join_rows, plan),
            seen,
            100 * seen.size,
            (ids, jnp.asarray(responses[:, :, list(chunk)]), *views),
            [pltpu.VMEM((groups,) + seen.shape, jnp.float32), sides, sides],
        )
        beside_far = swap(beside, "tm", steps, half)
        pieces = call(
            functools.partial(half_solve, plan),
            [modes] * half,
            100 * modes.size * half,
            (*small, *pieces, far, beside, beside_far),
        )
        pieces = [swap(v, "tm", steps, k) for k, v in enumerate(pieces)]
        last = chunk == CHUNKS[-1]
        part = pltpu.VMEM((len(chunk) * plan.rows, plan.width), jnp.bfloat16)
        hold = [part, part]
        if last:
            block = field.shape[:2] + (plan.block,)
            hold = [
                pltpu.VMEM((half,) + block, jnp.float32),
                pltpu.SemaphoreType.DMA((half,)),
            ] + hold
            early = call(
                functools.partial(first_rows, plan),
                f32((len(chunk) * plan.rows, plan.width)),
                flops // 2,
                (ids, *tables, *pieces[:-1]),
            )
            pieces = [early, pieces[-1]]
        ready = tuple(sorted(sums))
        parities = sorted(set(ready) | {c % 2 for c in chunk})
        result = call(
            functools.partial(backward, plan, chunk, ready, last),
            f32(field.shape)
            if last
            else [f32((plan.folds,) + field.shape[1:])] * len(parities),
            flops,
            (ids, back, *tables, *pieces, *(sums[parity] for parity in ready)),
            hold,
            pl.BlockSpec(memory_space=pltpu.HBM) if last else None,
        )
        if not last:
            sums = dict(zip(parities, result))
    return result[None]


def solution(mesh):
    spec = P("tm", None, "gy", None)

    def whole(residual):
        plan = Plan(mesh, residual.shape)
        return jax.shard_map(
            functools.partial(on_device, plan),
            mesh=mesh,
            in_specs=(spec,),
            out_specs=spec,
            check_vma=False,
        )(residual)

    return whole
```

```python
import functools
import math

import jax
import jax.numpy as jnp
import numpy as np
from jax import lax
from jax.experimental import pallas as pl
from jax.experimental.pallas import tpu as pltpu
from jax.sharding import PartitionSpec as P

ALPHA_RATIO = 0.95
STEP_SCALE = 0.26
LANES = 128
STRIP = 16
FINE_ROWS = 32
CHUNKS = ((0, 2, 4, 6), (1, 3, 5, 7))
VMEM_BYTES = 40 * 1024 * 1024


def sine_table(count):
    indices = np.arange(count, dtype=np.int64) + 1
    product = indices[:, None] * indices[None, :] % (2 * (count + 1))
    return math.sqrt(2.0 / (count + 1)) * np.sin(np.pi * product / (count + 1))


def spectrum_of(count):
    indices = np.arange(count, dtype=np.float64) + 1.0
    return 2.0 - 2.0 * np.cos(np.pi * indices / (count + 1))


def table_parts(table):
    table = table.astype(np.float32)
    high = table.astype(jnp.bfloat16)
    low = (table - high.astype(np.float32)).astype(jnp.bfloat16)
    return jnp.asarray(high), jnp.asarray(low)


def edge_responses(steps, depth, rows, width):
    freq = np.arange(steps // 2 + 1)
    turn = ALPHA_RATIO ** (1.0 / steps) * np.exp(-2j * np.pi * freq / steps)
    turn = turn[:, None, None]
    mu = spectrum_of(depth)[:, None] + spectrum_of(width)[None, :]
    scaled = STEP_SCALE * turn
    middle = ((1.0 - turn) ** 2 + scaled * (mu + 2.0)) / scaled
    root = np.sqrt(middle * middle / 4.0 - 1.0)
    ratio = middle / 2.0 - root
    ratio = np.where(np.abs(ratio) < 1.0, ratio, middle / 2.0 + root)
    bottom = 1.0 - ratio ** (2 * rows + 2)
    near = ratio * (1.0 - ratio ** (2 * rows)) / bottom
    far = ratio**rows * (1.0 - ratio * ratio) / bottom
    parts = np.stack([near.real, near.imag, far.real, far.imag], axis=1)
    return parts.astype(np.float32)


def parts_of(values):
    high = values.astype(jnp.bfloat16)
    return high, (values - high.astype(jnp.float32)).astype(jnp.bfloat16)


def dot(left, right):
    return jnp.dot(left, right, preferred_element_type=jnp.float32)


def dot_parts(left, right):
    return dot(left[0], right[0]) + dot(left[1], right[0]) + dot(left[0], right[1])


def call(kernel, out_shape, flops, args, scratch=(), out=None):
    smem = pl.BlockSpec(memory_space=pltpu.SMEM)
    vmem = pl.BlockSpec(memory_space=pltpu.VMEM)
    moved = sum(x.size * x.dtype.itemsize for x in args)
    return pl.pallas_call(
        kernel,
        out_shape=out_shape,
        in_specs=[smem] + [vmem] * (len(args) - 1),
        out_specs=out or jax.tree.map(lambda _: vmem, out_shape),
        scratch_shapes=scratch,
        compiler_params=pltpu.CompilerParams(vmem_limit_bytes=VMEM_BYTES),
        cost_estimate=pl.CostEstimate(
            flops=flops, bytes_accessed=moved, transcendentals=0
        ),
    )(*args)


class Plan:
    def __init__(self, mesh, shape):
        self.steps = mesh.shape["tm"]
        self.groups = mesh.shape["gy"]
        self.depth, self.width = shape[1], shape[3]
        self.rows = shape[2] // self.groups
        self.half = self.steps // 2
        self.block = self.width // self.half
        self.folds = self.depth // 2

    @property
    def order(self):
        return [0] + list(range(self.half - 1, 0, -1))

    def by_distance(self, refs):
        return [ref for _, ref in sorted(zip(self.order, refs), key=lambda x: x[0])]

    def columns(self, owner):
        return pl.ds(pl.multiple_of(owner * self.block, LANES), self.block)


def fill_table(plan, fine, ids, angles, high, low):
    coarse = plan.width // fine
    sine, cosine = (
        angles[2 * coarse + part * fine : 2 * coarse + (part + 1) * fine]
        for part in range(2)
    )

    def step(index, carry):
        rows = pl.ds(pl.multiple_of(index * fine, fine), fine)
        value = angles[pl.ds(index, 1), :] * cosine
        value = value + angles[pl.ds(coarse + index, 1), :] * sine
        high[rows, :], low[rows, :] = parts_of(value)
        return carry

    lax.fori_loop(0, plan.width // fine, step, 0)


def angle_tables(count, fine):
    scale = math.sqrt(2.0 / (count + 1))
    columns = np.arange(count, dtype=np.int64) + 1
    tables = []
    for rows, factor in (
        (np.arange(count // fine, dtype=np.int64) * fine, scale),
        (np.arange(fine, dtype=np.int64) + 1, 1.0),
    ):
        turns = rows[:, None] * columns[None, :] % (2 * (count + 1))
        angle = np.pi * turns / (count + 1)
        tables += [factor * np.sin(angle), factor * np.cos(angle)]
    return jnp.asarray(np.concatenate(tables), jnp.float32)


def fold_tables(plan):
    rows, folds = sine_table(plan.rows), plan.folds
    depth = sine_table(plan.depth)
    tables = [np.kron(depth[parity::2, :folds], rows) for parity in range(2)]
    forth = jnp.stack(table_parts(np.stack(tables)))
    back = jnp.stack(table_parts(np.stack([table.T for table in tables])))
    return forth, back


def by_parity(plan, chunk):
    start = 0
    for parity in range(2):
        places = [c // 2 for c in chunk if c % 2 == parity]
        if places:
            assert places == list(range(places[0], places[0] + len(places)))
            count = len(places) * plan.rows
            first = places[0] * plan.rows
            yield parity, slice(start, start + count), slice(first, first + count)
            start += count


def forward(plan, chunk, ids, both, x, sxh, sxl, *outs):
    place = lax.rem(ids[0], plan.half)
    folds = plan.folds
    mirror = jnp.stack([x[plan.depth - 1 - z] for z in range(folds)])
    left = []
    for parity, _, at in by_parity(plan, chunk):
        folded = x[:folds] - mirror if parity else x[:folds] + mirror
        folded = parts_of(folded.reshape(folds * plan.rows, plan.width))
        table = both[0, parity, at], both[1, parity, at]
        left.append(parts_of(dot_parts(table, folded)))
    for k in range(plan.half):
        columns = plan.columns(place ^ k)
        right = sxh[:, columns], sxl[:, columns]
        value = jnp.concatenate([dot_parts(part, right) for part in left])
        outs[k][...] = value.reshape(len(chunk), plan.rows, plan.block)


def x_rows(plan, place, pieces, start, sxh, sxl):
    total = None
    for k, piece in zip(plan.order[start:], pieces):
        at = plan.columns(place ^ k)
        piece = parts_of(piece[...].reshape(-1, plan.block))
        value = dot_parts(piece, (sxh[at, :], sxl[at, :]))
        total = value if total is None else total + value
    return total


def first_rows(plan, ids, sxh, sxl, *refs):
    place = lax.rem(ids[0], plan.half)
    refs[-1][...] = x_rows(plan, place, refs[:-1], 0, sxh, sxl)


def backward(plan, chunk, ready, last, ids, both, sxh, sxl, *refs):
    place = lax.rem(ids[0], plan.half)
    count = 2 if last else plan.half
    pieces, refs = refs[:count], refs[count:]
    before = dict(zip(ready, refs))
    outs, (high, low) = refs[len(ready) : -2], refs[-2:]
    folds = plan.folds
    shape = folds, plan.rows, plan.block
    if last:
        total = pieces[0][...] + x_rows(plan, place, pieces[1:], plan.half - 1, sxh, sxl)
    else:
        total = x_rows(plan, place, pieces, 0, sxh, sxl)
    high[...], low[...] = parts_of(total)
    for j in range(plan.half):
        columns = pl.ds(j * plan.block, plan.block)
        sums = {parity: before[parity][:, :, columns] for parity in ready}
        for parity, rows, at in by_parity(plan, chunk):
            table = both[0, parity, :, at], both[1, parity, :, at]
            value = dot_parts(table, (high[rows, columns], low[rows, columns]))
            value = value.reshape(shape)
            sums[parity] = sums[parity] + value if parity in sums else value
        if not last:
            for parity, out in zip(sorted(sums), outs):
                out[:, :, columns] = sums[parity]
            continue
        out, held, sent = outs
        held[j, :folds] = sums[0] + sums[1]
        other = sums[0] - sums[1]
        for z in range(folds):
            held[j, plan.depth - 1 - z] = other[z]
        pltpu.make_async_copy(held.at[j], out.at[:, :, columns], sent.at[j]).start()
    if last:
        for j in range(plan.half):
            columns = pl.ds(j * plan.block, plan.block)
            pltpu.make_async_copy(held.at[j], out.at[:, :, columns], sent.at[j]).wait()


def per_strip(plan, place, smu_z, smu_y, smu_x, edges, body, strip=STRIP):
    across = smu_x[:, plan.columns(place)]

    def step(index, carry):
        rows = pl.ds(pl.multiple_of(index * strip, strip), strip)
        plane = across + smu_y[rows, :]
        weights = edges[rows, 0:1], edges[rows, 1:2]
        for u in range(smu_z.shape[0]):
            body(u, rows, plane + smu_z[u : u + 1, :], weights)
        return carry

    lax.fori_loop(0, plan.rows // strip, step, 0)


class Cyclic:
    def __init__(self, smu, half):
        self.kappa = kappa = 2.0 - smu
        values = [jnp.zeros_like(kappa), jnp.ones_like(kappa)]
        for _ in range(half):
            values.append(kappa * values[-1] - values[-2])
        self.up, self.at, self.down = values[-1], values[-2], values[-3]
        det = (1.0 - ALPHA_RATIO) ** 2 + ALPHA_RATIO * (
            smu * (4.0 - smu) * (self.at * self.at)
        )
        inverse = 1.0 / det
        self.even = (0.5 * (1.0 - ALPHA_RATIO)) * (self.up - self.down) * inverse
        self.odd = (0.5 * (1.0 + ALPHA_RATIO)) * self.at * inverse

    def run(self, before, last, sources):
        values = []
        for source in sources:
            value = self.kappa * last - before
            before, last = last, value if source is None else value + source
            values.append(last)
        return before, last, values

    def start(self, sources):
        last = sources[0]
        before, last, _ = self.run(last, self.kappa * last + sources[1], sources[2:])
        return before, last

    def entry(self, p0, p1):
        return (
            self.even * p0 + self.odd * (2.0 * p1 - self.kappa * p0),
            self.even * p1 + self.odd * (self.kappa * p1 - 2.0 * p0),
        )

    def back(self, p0, p1):
        return self.up * p0 - self.at * p1, self.at * p0 - self.down * p1


def by_place(plan, place, body):
    for case in range(plan.half):
        pl.when(place == case)(functools.partial(body, case))


def half_end(plan, ids, smu_z, smu_y, smu_x, edges, *refs):
    pieces = plan.by_distance(refs[: plan.half])
    ends, seen, sums = refs[plan.half :]
    steps, half = plan.steps, plan.half
    place = lax.rem(ids[0], half)
    mine = ids[0] // half
    leaving = jnp.where(mine == 0, 1.0, ALPHA_RATIO).astype(jnp.float32)
    sums[...] = jnp.zeros_like(sums)

    def with_place(case):
        def body(u, rows, smu, weights):
            cyclic = Cyclic(smu, half)
            sources = [pieces[case ^ j][u, rows, :] for j in range(half)]
            before, last = cyclic.start(sources)
            ends[0, u, rows, :] = before
            ends[1, u, rows, :] = last
            entry = cyclic.entry(ALPHA_RATIO * before, ALPHA_RATIO * last)
            before, last, own = cyclic.run(*entry, sources)
            _, _, other = cyclic.run(leaving * before, leaving * last, [None] * half)
            for values, window in ((own, mine), (other, 1 - mine)):
                for j, value in enumerate(values):
                    for edge in range(2):
                        term = weights[edge] * value
                        term = sum(term[i : i + 8] for i in range(0, STRIP, 8))
                        sums[2 * (window * half + j) + edge, u] += term

        per_strip(plan, place, smu_z, smu_y, smu_x, edges, body)

    by_place(plan, place, with_place)
    seen[...] = jnp.sum(sums[...], axis=2)


def c_mul(a, b):
    return a[0] * b[0] - a[1] * b[1], a[0] * b[1] + a[1] * b[0]


def c_add(a, b):
    return a[0] + b[0], a[1] + b[1]


def c_gap(a, b):
    product = c_mul(a, b)
    real, imag = 1.0 - product[0], -product[1]
    inverse = 1.0 / (real * real + imag * imag)
    return real * inverse, -imag * inverse


def join_rows(plan, ids, responses, *refs):
    groups, steps = plan.groups, plan.steps
    views = refs[:groups]
    out, seen, above, below = refs[groups:]
    place = lax.rem(ids[0], plan.half)
    me = ids[1]
    columns = plan.columns(place)
    for k in range(groups):
        seen[me ^ k] = views[k][...]
    radius = ALPHA_RATIO ** (1.0 / steps)
    grow = [radius**n for n in range(steps)]
    nothing = jnp.zeros(out.shape[1:], jnp.float32)
    for freq in range(steps // 2 + 1):
        angle = [2.0 * math.pi * (freq * n % steps) / steps for n in range(steps)]

        def spectrum(block, edge):
            real, imag = nothing, nothing
            for n in range(steps):
                value = seen[block, 2 * n + edge]
                real = real + value * np.float32(grow[n] * math.cos(angle[n]))
                if freq % (steps // 2):
                    imag = imag - value * np.float32(grow[n] * math.sin(angle[n]))
            return real, imag

        head = [spectrum(block, 0) for block in range(groups)]
        tail = [spectrum(block, 1) for block in range(groups)]
        near, far = (
            tuple(
                responses[freq, 2 * kind + part, :, columns]
                for part in range(2)
            )
            for kind in range(2)
        )
        square = c_mul(far, far)
        gammas, downs, ups = [near], [tail[0]], [head[groups - 1]]
        for d in range(1, groups - 1):
            gamma = gammas[-1]
            gap = c_gap(gamma, near)
            through = c_mul(far, gap)
            e = groups - 1 - d
            downs.append(
                c_add(
                    tail[d], c_mul(through, c_add(downs[-1], c_mul(gamma, head[d])))
                )
            )
            ups.append(
                c_add(head[e], c_mul(through, c_add(ups[-1], c_mul(gamma, tail[e]))))
            )
            gammas.append(c_add(near, c_mul(square, c_mul(gamma, gap))))
        for d in range(groups - 1):
            down, up = downs[d], ups[groups - 2 - d]
            from_top, from_end = gammas[d], gammas[groups - 2 - d]
            gap = c_gap(from_top, from_end)
            last = c_mul(c_add(down, c_mul(from_top, up)), gap)
            start = c_mul(c_add(up, c_mul(from_end, down)), gap)
            for part in range(2):
                above[d + 1, 2 * freq + part] = last[part]
                below[d, 2 * freq + part] = start[part]
        for part in range(2):
            above[0, 2 * freq + part] = nothing
            below[groups - 1, 2 * freq + part] = nothing
    for edge, side in enumerate((above, below)):
        parts = [side[me, i] for i in range(steps + 2)]
        for n in range(steps):
            total = nothing
            shrink = STEP_SCALE / (steps * grow[n])
            if n == steps - 1:
                shrink *= ALPHA_RATIO
            for freq in range(steps // 2 + 1):
                angle = 2.0 * math.pi * (freq * n % steps) / steps
                single = freq % (steps // 2) == 0
                weight = shrink if single else 2.0 * shrink
                total = total + parts[2 * freq] * np.float32(weight * math.cos(angle))
                if not single:
                    total = total - parts[2 * freq + 1] * np.float32(
                        weight * math.sin(angle)
                    )
            out[2 * ((n + 1) % steps) + edge] = total


def half_solve(plan, ids, smu_z, smu_y, smu_x, edges, *refs):
    pieces = plan.by_distance(refs[: plan.half])
    far, beside, beside_far = refs[plan.half : plan.half + 3]
    outs = refs[plan.half + 3 :]
    half = plan.half
    place = lax.rem(ids[0], half)
    mine = ids[0] // half
    entering = jnp.where(mine == 0, ALPHA_RATIO, 1.0).astype(jnp.float32)

    def with_place(case):
        def body(u, rows, smu, weights):
            cyclic = Cyclic(smu, half)

            def source(window, j):
                total = None
                for edge in range(2):
                    at = 2 * (window * half + j) + edge
                    row = beside[at, u : u + 1, :] + beside_far[at, u : u + 1, :]
                    term = weights[edge] * row
                    total = term if total is None else total + term
                return total

            own = [pieces[case ^ j][u, rows, :] + source(mine, j) for j in range(half)]
            other = [source(1 - mine, j) for j in range(half)]
            before, last = cyclic.start(other)
            before = entering * (before + far[0, u, rows, :])
            last = entering * (last + far[1, u, rows, :])
            before, last = cyclic.back(before, last)
            near = cyclic.start(own)
            entry = cyclic.entry(
                before + ALPHA_RATIO * near[0], last + ALPHA_RATIO * near[1]
            )
            _, _, values = cyclic.run(*entry, own)
            for j, value in enumerate(values):
                outs[case ^ j][u, rows, :] = value

        per_strip(plan, place, smu_z, smu_y, smu_x, edges, body, 2 * STRIP)

    by_place(plan, place, with_place)


def swap(values, axis, count, distance):
    if distance == 0:
        return values
    return lax.ppermute(values, axis, [(i, i ^ distance) for i in range(count)])


def on_device(plan, residual):
    steps, groups, half = plan.steps, plan.groups, plan.half
    ids = jnp.stack([lax.axis_index("tm"), lax.axis_index("gy")]).astype(jnp.int32)
    sine_rows = sine_table(plan.rows)
    smu_z, smu_y, smu_x = (
        STEP_SCALE * spectrum_of(count) for count in (plan.depth, plan.rows, plan.width)
    )
    smu_y = jnp.asarray(smu_y[:, None], jnp.float32)
    smu_x = jnp.asarray(smu_x[None, :], jnp.float32)
    edges = jnp.asarray(sine_rows[:, [0, plan.rows - 1]], jnp.float32)
    responses = edge_responses(steps, plan.depth, plan.rows, plan.width)
    field = residual[0]
    f32 = functools.partial(jax.ShapeDtypeStruct, dtype=jnp.float32)
    forth, back = fold_tables(plan)
    tables = call(
        functools.partial(fill_table, plan, FINE_ROWS),
        [jax.ShapeDtypeStruct((plan.width, plan.width), jnp.bfloat16)] * 2,
        4000 * plan.width * plan.width,
        (ids, angle_tables(plan.width, FINE_ROWS)),
    )
    work = []
    for chunk in CHUNKS:
        modes = f32((len(chunk), plan.rows, plan.block))
        count = len(chunk) * plan.rows * plan.width
        flops = 6 * count * (plan.width + plan.folds * plan.rows)
        pieces = call(
            functools.partial(forward, plan, chunk),
            [modes] * half,
            flops,
            (ids, forth, field, *tables),
        )
        pieces = [swap(pieces[k], "tm", steps, k) for k in plan.order]
        smu_own = jnp.asarray(smu_z[list(chunk), None], jnp.float32)
        work.append((chunk, modes, flops, (ids, smu_own, smu_y, smu_x, edges), pieces))
    first, second = work[0][-1], work[1][-1]
    first[0], second[0] = lax.optimization_barrier((first[0], second[0]))
    sums = {}
    far = None
    for chunk, modes, flops, small, pieces in work:
        seen = f32((2 * steps, len(chunk), plan.block))
        ends, view = call(
            functools.partial(half_end, plan),
            [f32((2,) + modes.shape), seen],
            100 * modes.size * half,
            (*small, *pieces),
            [pltpu.VMEM((2 * steps, len(chunk), 8, plan.block), jnp.float32)],
        )
        if far is not None:
            ends, far, beside_far = lax.optimization_barrier((ends, far, beside_far))
        far = swap(ends, "tm", steps, half)
        views = [swap(view, "gy", groups, k) for k in range(groups)]
        sides = pltpu.VMEM((groups, steps + 2) + seen.shape[1:], jnp.float32)
        beside = call(
            functools.partial(join_rows, plan),
            seen,
            100 * seen.size,
            (ids, jnp.asarray(responses[:, :, list(chunk)]), *views),
            [pltpu.VMEM((groups,) + seen.shape, jnp.float32), sides, sides],
        )
        beside_far = swap(beside, "tm", steps, half)
        pieces = call(
            functools.partial(half_solve, plan),
            [modes] * half,
            100 * modes.size * half,
            (*small, *pieces, far, beside, beside_far),
        )
        pieces = [swap(pieces[k], "tm", steps, k) for k in plan.order]
        last = chunk == CHUNKS[-1]
        part = pltpu.VMEM((len(chunk) * plan.rows, plan.width), jnp.bfloat16)
        hold = [part, part]
        if last:
            block = field.shape[:2] + (plan.block,)
            hold = [
                pltpu.VMEM((half,) + block, jnp.float32),
                pltpu.SemaphoreType.DMA((half,)),
            ] + hold
            early = call(
                functools.partial(first_rows, plan),
                f32((len(chunk) * plan.rows, plan.width)),
                flops // 2,
                (ids, *tables, *pieces[:-1]),
            )
            pieces = [early, pieces[-1]]
        ready = tuple(sorted(sums))
        parities = sorted(set(ready) | {c % 2 for c in chunk})
        result = call(
            functools.partial(backward, plan, chunk, ready, last),
            f32(field.shape)
            if last
            else [f32((plan.folds,) + field.shape[1:])] * len(parities),
            flops,
            (ids, back, *tables, *pieces, *(sums[parity] for parity in ready)),
            hold,
            pl.BlockSpec(memory_space=pltpu.HBM) if last else None,
        )
        if not last:
            sums = dict(zip(parities, result))
    return result[None]


def solution(mesh):
    spec = P("tm", None, "gy", None)

    def whole(residual):
        plan = Plan(mesh, residual.shape)
        return jax.shard_map(
            functools.partial(on_device, plan),
            mesh=mesh,
            in_specs=(spec,),
            out_specs=spec,
            check_vma=False,
        )(residual)

    return whole
```

```python
import functools
import math

import jax
import jax.numpy as jnp
import numpy as np
from jax import lax
from jax.experimental import pallas as pl
from jax.experimental.pallas import tpu as pltpu
from jax.sharding import PartitionSpec as P

ALPHA_RATIO = 0.95
STEP_SCALE = 0.26
LANES = 128
STRIP = 16
FINE_ROWS = 32
CHUNKS = ((0, 2, 4, 6), (1, 3, 5, 7))
VMEM_BYTES = 40 * 1024 * 1024


def sine_table(count):
    indices = np.arange(count, dtype=np.int64) + 1
    product = indices[:, None] * indices[None, :] % (2 * (count + 1))
    return math.sqrt(2.0 / (count + 1)) * np.sin(np.pi * product / (count + 1))


def spectrum_of(count):
    indices = np.arange(count, dtype=np.float64) + 1.0
    return 2.0 - 2.0 * np.cos(np.pi * indices / (count + 1))


def table_parts(table):
    table = table.astype(np.float32)
    high = table.astype(jnp.bfloat16)
    low = (table - high.astype(np.float32)).astype(jnp.bfloat16)
    return jnp.asarray(high), jnp.asarray(low)


def edge_responses(steps, depth, rows, width):
    freq = np.arange(steps // 2 + 1)
    turn = ALPHA_RATIO ** (1.0 / steps) * np.exp(-2j * np.pi * freq / steps)
    turn = turn[:, None, None]
    mu = spectrum_of(depth)[:, None] + spectrum_of(width)[None, :]
    scaled = STEP_SCALE * turn
    middle = ((1.0 - turn) ** 2 + scaled * (mu + 2.0)) / scaled
    root = np.sqrt(middle * middle / 4.0 - 1.0)
    ratio = middle / 2.0 - root
    ratio = np.where(np.abs(ratio) < 1.0, ratio, middle / 2.0 + root)
    bottom = 1.0 - ratio ** (2 * rows + 2)
    near = ratio * (1.0 - ratio ** (2 * rows)) / bottom
    far = ratio**rows * (1.0 - ratio * ratio) / bottom
    parts = np.stack([near.real, near.imag, far.real, far.imag], axis=1)
    return parts.astype(np.float32)


def parts_of(values):
    high = values.astype(jnp.bfloat16)
    return high, (values - high.astype(jnp.float32)).astype(jnp.bfloat16)


def dot(left, right):
    return jnp.dot(left, right, preferred_element_type=jnp.float32)


def dot_parts(left, right):
    return dot(left[0], right[0]) + dot(left[1], right[0]) + dot(left[0], right[1])


def call(kernel, out_shape, flops, args, scratch=(), out=None):
    smem = pl.BlockSpec(memory_space=pltpu.SMEM)
    vmem = pl.BlockSpec(memory_space=pltpu.VMEM)
    moved = sum(x.size * x.dtype.itemsize for x in args)
    return pl.pallas_call(
        kernel,
        out_shape=out_shape,
        in_specs=[smem] + [vmem] * (len(args) - 1),
        out_specs=out or jax.tree.map(lambda _: vmem, out_shape),
        scratch_shapes=scratch,
        compiler_params=pltpu.CompilerParams(vmem_limit_bytes=VMEM_BYTES),
        cost_estimate=pl.CostEstimate(
            flops=flops, bytes_accessed=moved, transcendentals=0
        ),
    )(*args)


class Plan:
    def __init__(self, mesh, shape):
        self.steps = mesh.shape["tm"]
        self.groups = mesh.shape["gy"]
        self.depth, self.width = shape[1], shape[3]
        self.rows = shape[2] // self.groups
        self.half = self.steps // 2
        self.block = self.width // self.half
        self.folds = self.depth // 2

    def columns(self, owner):
        return pl.ds(pl.multiple_of(owner * self.block, LANES), self.block)


def fill_table(plan, fine, ids, angles, high, low):
    coarse = plan.width // fine
    sine, cosine = (
        angles[2 * coarse + part * fine : 2 * coarse + (part + 1) * fine]
        for part in range(2)
    )

    def step(index, carry):
        rows = pl.ds(pl.multiple_of(index * fine, fine), fine)
        value = angles[pl.ds(index, 1), :] * cosine
        value = value + angles[pl.ds(coarse + index, 1), :] * sine
        high[rows, :], low[rows, :] = parts_of(value)
        return carry

    lax.fori_loop(0, plan.width // fine, step, 0)


def angle_tables(count, fine):
    scale = math.sqrt(2.0 / (count + 1))
    columns = np.arange(count, dtype=np.int64) + 1
    tables = []
    for rows, factor in (
        (np.arange(count // fine, dtype=np.int64) * fine, scale),
        (np.arange(fine, dtype=np.int64) + 1, 1.0),
    ):
        turns = rows[:, None] * columns[None, :] % (2 * (count + 1))
        angle = np.pi * turns / (count + 1)
        tables += [factor * np.sin(angle), factor * np.cos(angle)]
    return jnp.asarray(np.concatenate(tables), jnp.float32)


def fold_tables(plan):
    rows, folds = sine_table(plan.rows), plan.folds
    depth = sine_table(plan.depth)
    tables = [np.kron(depth[parity::2, :folds], rows) for parity in range(2)]
    forth = jnp.stack(table_parts(np.stack(tables)))
    back = jnp.stack(table_parts(np.stack([table.T for table in tables])))
    return forth, back


def by_parity(plan, chunk):
    start = 0
    for parity in range(2):
        places = [c // 2 for c in chunk if c % 2 == parity]
        if places:
            assert places == list(range(places[0], places[0] + len(places)))
            count = len(places) * plan.rows
            first = places[0] * plan.rows
            yield parity, slice(start, start + count), slice(first, first + count)
            start += count


def forward(plan, chunk, ids, both, x, sxh, sxl, *outs):
    place = lax.rem(ids[0], plan.half)
    folds = plan.folds
    mirror = jnp.stack([x[plan.depth - 1 - z] for z in range(folds)])
    left = []
    for parity, _, at in by_parity(plan, chunk):
        folded = x[:folds] - mirror if parity else x[:folds] + mirror
        folded = parts_of(folded.reshape(folds * plan.rows, plan.width))
        table = both[0, parity, at], both[1, parity, at]
        left.append(parts_of(dot_parts(table, folded)))
    for k in range(plan.half):
        columns = plan.columns(place ^ k)
        right = sxh[:, columns], sxl[:, columns]
        value = jnp.concatenate([dot_parts(part, right) for part in left])
        outs[k][...] = value.reshape(len(chunk), plan.rows, plan.block)


def x_rows(plan, place, pieces, start, sxh, sxl):
    total = None
    for k, piece in enumerate(pieces, start):
        at = plan.columns(place ^ k)
        piece = parts_of(piece[...].reshape(-1, plan.block))
        value = dot_parts(piece, (sxh[at, :], sxl[at, :]))
        total = value if total is None else total + value
    return total


def first_rows(plan, ids, sxh, sxl, *refs):
    place = lax.rem(ids[0], plan.half)
    refs[-1][...] = x_rows(plan, place, refs[:-1], 0, sxh, sxl)


def backward(plan, chunk, ready, last, ids, both, sxh, sxl, *refs):
    place = lax.rem(ids[0], plan.half)
    count = 2 if last else plan.half
    pieces, refs = refs[:count], refs[count:]
    before = dict(zip(ready, refs))
    outs, (high, low) = refs[len(ready) : -2], refs[-2:]
    folds = plan.folds
    shape = folds, plan.rows, plan.block
    if last:
        total = pieces[0][...] + x_rows(plan, place, pieces[1:], plan.half - 1, sxh, sxl)
    else:
        total = x_rows(plan, place, pieces, 0, sxh, sxl)
    high[...], low[...] = parts_of(total)
    for j in range(plan.half):
        columns = pl.ds(j * plan.block, plan.block)
        sums = {parity: before[parity][:, :, columns] for parity in ready}
        for parity, rows, at in by_parity(plan, chunk):
            table = both[0, parity, :, at], both[1, parity, :, at]
            value = dot_parts(table, (high[rows, columns], low[rows, columns]))
            value = value.reshape(shape)
            sums[parity] = sums[parity] + value if parity in sums else value
        if not last:
            for parity, out in zip(sorted(sums), outs):
                out[:, :, columns] = sums[parity]
            continue
        out, held, sent = outs
        held[j, :folds] = sums[0] + sums[1]
        other = sums[0] - sums[1]
        for z in range(folds):
            held[j, plan.depth - 1 - z] = other[z]
        pltpu.make_async_copy(held.at[j], out.at[:, :, columns], sent.at[j]).start()
    if last:
        for j in range(plan.half):
            columns = pl.ds(j * plan.block, plan.block)
            pltpu.make_async_copy(held.at[j], out.at[:, :, columns], sent.at[j]).wait()


def per_strip(plan, place, smu_z, smu_y, smu_x, edges, body, strip=STRIP):
    across = smu_x[:, plan.columns(place)]

    def step(index, carry):
        rows = pl.ds(pl.multiple_of(index * strip, strip), strip)
        plane = across + smu_y[rows, :]
        weights = edges[rows, :]
        for u in range(smu_z.shape[0]):
            body(u, rows, plane + smu_z[u : u + 1, :], weights)
        return carry

    lax.fori_loop(0, plan.rows // strip, step, 0)


class Cyclic:
    def __init__(self, smu, half):
        self.kappa = kappa = 2.0 - smu
        values = [jnp.zeros_like(kappa), jnp.ones_like(kappa)]
        for _ in range(half):
            values.append(kappa * values[-1] - values[-2])
        self.up, self.at, self.down = values[-1], values[-2], values[-3]
        det = (1.0 - ALPHA_RATIO) ** 2 + ALPHA_RATIO * (
            smu * (4.0 - smu) * (self.at * self.at)
        )
        inverse = 1.0 / det
        self.even = (0.5 * (1.0 - ALPHA_RATIO)) * (self.up - self.down) * inverse
        self.odd = (0.5 * (1.0 + ALPHA_RATIO)) * self.at * inverse

    def run(self, before, last, sources):
        values = []
        for source in sources:
            value = self.kappa * last - before
            before, last = last, value if source is None else value + source
            values.append(last)
        return before, last, values

    def start(self, sources):
        last = sources[0]
        before, last, _ = self.run(last, self.kappa * last + sources[1], sources[2:])
        return before, last

    def entry(self, p0, p1):
        return (
            self.even * p0 + self.odd * (2.0 * p1 - self.kappa * p0),
            self.even * p1 + self.odd * (self.kappa * p1 - 2.0 * p0),
        )

    def back(self, p0, p1):
        return self.up * p0 - self.at * p1, self.at * p0 - self.down * p1


def by_place(plan, place, body):
    for case in range(plan.half):
        pl.when(place == case)(functools.partial(body, case))


def row_sign():
    index = lax.broadcasted_iota(jnp.int32, (8, 1), 0)
    return (1 - 2 * (index % 2)).astype(jnp.float32)


def half_end(plan, ids, smu_z, smu_y, smu_x, edges, *refs):
    pieces = refs[: plan.half]
    ends, seen, sums = refs[plan.half :]
    steps, half = plan.steps, plan.half
    place = lax.rem(ids[0], half)
    mine = ids[0] // half
    leaving = jnp.where(mine == 0, 1.0, ALPHA_RATIO).astype(jnp.float32)
    sums[...] = jnp.zeros_like(sums)

    def with_place(case):
        def body(u, rows, smu, weights):
            cyclic = Cyclic(smu, half)
            sources = [pieces[case ^ j][u, rows, :] for j in range(half)]
            before, last = cyclic.start(sources)
            ends[0, u, rows, :] = before
            ends[1, u, rows, :] = last
            entry = cyclic.entry(ALPHA_RATIO * before, ALPHA_RATIO * last)
            before, last, own = cyclic.run(*entry, sources)
            _, _, other = cyclic.run(leaving * before, leaving * last, [None] * half)
            for values, window in ((own, mine), (other, 1 - mine)):
                for j, value in enumerate(values):
                    term = weights * value
                    term = sum(term[i : i + 8] for i in range(0, term.shape[0], 8))
                    sums[window * half + j, u] += term

        per_strip(plan, place, smu_z, smu_y, smu_x, edges, body, 2 * STRIP)

    by_place(plan, place, with_place)
    sign = row_sign()
    for n in range(steps):
        total = sums[n]
        seen[2 * n] = jnp.sum(total, axis=1)
        seen[2 * n + 1] = jnp.sum(total * sign, axis=1)


def c_mul(a, b):
    return a[0] * b[0] - a[1] * b[1], a[0] * b[1] + a[1] * b[0]


def c_add(a, b):
    return a[0] + b[0], a[1] + b[1]


def c_gap(a, b):
    product = c_mul(a, b)
    real, imag = 1.0 - product[0], -product[1]
    inverse = 1.0 / (real * real + imag * imag)
    return real * inverse, -imag * inverse


def join_rows(plan, ids, responses, *refs):
    groups, steps = plan.groups, plan.steps
    views = refs[:groups]
    out, seen, above, below = refs[groups:]
    place = lax.rem(ids[0], plan.half)
    me = ids[1]
    columns = plan.columns(place)
    for k in range(groups):
        seen[me ^ k] = views[k][...]
    radius = ALPHA_RATIO ** (1.0 / steps)
    grow = [radius**n for n in range(steps)]
    nothing = jnp.zeros(out.shape[1:], jnp.float32)
    for freq in range(steps // 2 + 1):
        angle = [2.0 * math.pi * (freq * n % steps) / steps for n in range(steps)]

        def spectrum(block, edge):
            real, imag = nothing, nothing
            for n in range(steps):
                value = seen[block, 2 * n + edge]
                real = real + value * np.float32(grow[n] * math.cos(angle[n]))
                if freq % (steps // 2):
                    imag = imag - value * np.float32(grow[n] * math.sin(angle[n]))
            return real, imag

        head = [spectrum(block, 0) for block in range(groups)]
        tail = [spectrum(block, 1) for block in range(groups)]
        near, far = (
            tuple(
                responses[freq, 2 * kind + part, :, columns]
                for part in range(2)
            )
            for kind in range(2)
        )
        square = c_mul(far, far)
        gammas, downs, ups = [near], [tail[0]], [head[groups - 1]]
        for d in range(1, groups - 1):
            gamma = gammas[-1]
            gap = c_gap(gamma, near)
            through = c_mul(far, gap)
            e = groups - 1 - d
            downs.append(
                c_add(
                    tail[d], c_mul(through, c_add(downs[-1], c_mul(gamma, head[d])))
                )
            )
            ups.append(
                c_add(head[e], c_mul(through, c_add(ups[-1], c_mul(gamma, tail[e]))))
            )
            gammas.append(c_add(near, c_mul(square, c_mul(gamma, gap))))
        for d in range(groups - 1):
            down, up = downs[d], ups[groups - 2 - d]
            from_top, from_end = gammas[d], gammas[groups - 2 - d]
            gap = c_gap(from_top, from_end)
            last = c_mul(c_add(down, c_mul(from_top, up)), gap)
            start = c_mul(c_add(up, c_mul(from_end, down)), gap)
            for part in range(2):
                above[d + 1, 2 * freq + part] = last[part]
                below[d, 2 * freq + part] = start[part]
        for part in range(2):
            above[0, 2 * freq + part] = nothing
            below[groups - 1, 2 * freq + part] = nothing
    for edge, side in enumerate((above, below)):
        parts = [side[me, i] for i in range(steps + 2)]
        for n in range(steps):
            total = nothing
            shrink = STEP_SCALE / (steps * grow[n])
            if n == steps - 1:
                shrink *= ALPHA_RATIO
            for freq in range(steps // 2 + 1):
                angle = 2.0 * math.pi * (freq * n % steps) / steps
                single = freq % (steps // 2) == 0
                weight = shrink if single else 2.0 * shrink
                total = total + parts[2 * freq] * np.float32(weight * math.cos(angle))
                if not single:
                    total = total - parts[2 * freq + 1] * np.float32(
                        weight * math.sin(angle)
                    )
            out[2 * ((n + 1) % steps) + edge] = total


def half_solve(plan, ids, smu_z, smu_y, smu_x, edges, *refs):
    pieces = refs[: plan.half]
    far, beside, beside_far = refs[plan.half : plan.half + 3]
    outs, around = refs[plan.half + 3 : -1], refs[-1]
    half = plan.half
    sign = row_sign()
    for n in range(plan.steps):
        for u in range(around.shape[1]):
            above, below = (
                beside[2 * n + edge, u : u + 1, :] + beside_far[2 * n + edge, u : u + 1, :]
                for edge in range(2)
            )
            around[n, u] = above + sign * below
    place = lax.rem(ids[0], half)
    mine = ids[0] // half
    entering = jnp.where(mine == 0, ALPHA_RATIO, 1.0).astype(jnp.float32)

    def with_place(case):
        def body(u, rows, smu, weights):
            cyclic = Cyclic(smu, half)

            def source(window, j):
                rows = around[window * half + j, u]
                return weights * jnp.concatenate([rows] * (weights.shape[0] // 8))

            own = [pieces[case ^ j][u, rows, :] + source(mine, j) for j in range(half)]
            other = [source(1 - mine, j) for j in range(half)]
            before, last = cyclic.start(other)
            before = entering * (before + far[0, u, rows, :])
            last = entering * (last + far[1, u, rows, :])
            before, last = cyclic.back(before, last)
            near = cyclic.start(own)
            entry = cyclic.entry(
                before + ALPHA_RATIO * near[0], last + ALPHA_RATIO * near[1]
            )
            _, _, values = cyclic.run(*entry, own)
            for j, value in enumerate(values):
                outs[case ^ j][u, rows, :] = value

        per_strip(plan, place, smu_z, smu_y, smu_x, edges, body, 2 * STRIP)

    by_place(plan, place, with_place)


def swap(values, axis, count, distance):
    if distance == 0:
        return values
    return lax.ppermute(values, axis, [(i, i ^ distance) for i in range(count)])


def on_device(plan, residual):
    steps, groups, half = plan.steps, plan.groups, plan.half
    ids = jnp.stack([lax.axis_index("tm"), lax.axis_index("gy")]).astype(jnp.int32)
    sine_rows = sine_table(plan.rows)
    smu_z, smu_y, smu_x = (
        STEP_SCALE * spectrum_of(count) for count in (plan.depth, plan.rows, plan.width)
    )
    smu_y = jnp.asarray(smu_y[:, None], jnp.float32)
    smu_x = jnp.asarray(smu_x[None, :], jnp.float32)
    edges = jnp.asarray(sine_rows[:, :1], jnp.float32)
    responses = edge_responses(steps, plan.depth, plan.rows, plan.width)
    field = residual[0]
    f32 = functools.partial(jax.ShapeDtypeStruct, dtype=jnp.float32)
    forth, back = fold_tables(plan)
    tables = call(
        functools.partial(fill_table, plan, FINE_ROWS),
        [jax.ShapeDtypeStruct((plan.width, plan.width), jnp.bfloat16)] * 2,
        4000 * plan.width * plan.width,
        (ids, angle_tables(plan.width, FINE_ROWS)),
    )
    work = []
    for chunk in CHUNKS:
        modes = f32((len(chunk), plan.rows, plan.block))
        count = len(chunk) * plan.rows * plan.width
        flops = 6 * count * (plan.width + plan.folds * plan.rows)
        pieces = call(
            functools.partial(forward, plan, chunk),
            [modes] * half,
            flops,
            (ids, forth, field, *tables),
        )
        pieces = [swap(v, "tm", steps, k) for k, v in enumerate(pieces)]
        smu_own = jnp.asarray(smu_z[list(chunk), None], jnp.float32)
        work.append((chunk, modes, flops, (ids, smu_own, smu_y, smu_x, edges), pieces))
    first, second = work[0][-1], work[1][-1]
    first[0], second[0] = lax.optimization_barrier((first[0], second[0]))
    sums = {}
    far = None
    for chunk, modes, flops, small, pieces in work:
        seen = f32((2 * steps, len(chunk), plan.block))
        ends, view = call(
            functools.partial(half_end, plan),
            [f32((2,) + modes.shape), seen],
            100 * modes.size * half,
            (*small, *pieces),
            [pltpu.VMEM((steps, len(chunk), 8, plan.block), jnp.float32)],
        )
        if far is not None:
            ends, far, beside_far = lax.optimization_barrier((ends, far, beside_far))
        far = swap(ends, "tm", steps, half)
        views = [swap(view, "gy", groups, k) for k in range(groups)]
        sides = pltpu.VMEM((groups, steps + 2) + seen.shape[1:], jnp.float32)
        beside = call(
            functools.partial(join_rows, plan),
            seen,
            100 * seen.size,
            (ids, jnp.asarray(responses[:, :, list(chunk)]), *views),
            [pltpu.VMEM((groups,) + seen.shape, jnp.float32), sides, sides],
        )
        beside_far = swap(beside, "tm", steps, half)
        pieces = call(
            functools.partial(half_solve, plan),
            [modes] * half,
            100 * modes.size * half,
            (*small, *pieces, far, beside, beside_far),
            [pltpu.VMEM((steps, len(chunk), 8, plan.block), jnp.float32)],
        )
        pieces = [swap(v, "tm", steps, k) for k, v in enumerate(pieces)]
        last = chunk == CHUNKS[-1]
        part = pltpu.VMEM((len(chunk) * plan.rows, plan.width), jnp.bfloat16)
        hold = [part, part]
        if last:
            block = field.shape[:2] + (plan.block,)
            hold = [
                pltpu.VMEM((half,) + block, jnp.float32),
                pltpu.SemaphoreType.DMA((half,)),
            ] + hold
            early = call(
                functools.partial(first_rows, plan),
                f32((len(chunk) * plan.rows, plan.width)),
                flops // 2,
                (ids, *tables, *pieces[:-1]),
            )
            pieces = [early, pieces[-1]]
        ready = tuple(sorted(sums))
        parities = sorted(set(ready) | {c % 2 for c in chunk})
        result = call(
            functools.partial(backward, plan, chunk, ready, last),
            f32(field.shape)
            if last
            else [f32((plan.folds,) + field.shape[1:])] * len(parities),
            flops,
            (ids, back, *tables, *pieces, *(sums[parity] for parity in ready)),
            hold,
            pl.BlockSpec(memory_space=pltpu.HBM) if last else None,
        )
        if not last:
            sums = dict(zip(parities, result))
    return result[None]


def solution(mesh):
    spec = P("tm", None, "gy", None)

    def whole(residual):
        plan = Plan(mesh, residual.shape)
        return jax.shard_map(
            functools.partial(on_device, plan),
            mesh=mesh,
            in_specs=(spec,),
            out_specs=spec,
            check_vma=False,
        )(residual)

    return whole
```

```python
import functools
import math

import jax
import jax.numpy as jnp
import numpy as np
from jax import lax
from jax.experimental import pallas as pl
from jax.experimental.pallas import tpu as pltpu
from jax.sharding import PartitionSpec as P

ALPHA_RATIO = 0.95
STEP_SCALE = 0.26
LANES = 128
STRIP = 16
FINE_ROWS = 32
CHUNKS = ((0, 2, 4, 6), (1, 3, 5, 7))
VMEM_BYTES = 40 * 1024 * 1024


def sine_table(count):
    indices = np.arange(count, dtype=np.int64) + 1
    product = indices[:, None] * indices[None, :] % (2 * (count + 1))
    return math.sqrt(2.0 / (count + 1)) * np.sin(np.pi * product / (count + 1))


def spectrum_of(count):
    indices = np.arange(count, dtype=np.float64) + 1.0
    return 2.0 - 2.0 * np.cos(np.pi * indices / (count + 1))


def table_parts(table):
    table = table.astype(np.float32)
    high = table.astype(jnp.bfloat16)
    low = (table - high.astype(np.float32)).astype(jnp.bfloat16)
    return jnp.asarray(high), jnp.asarray(low)


def edge_responses(steps, depth, rows, width):
    freq = np.arange(steps // 2 + 1)
    turn = ALPHA_RATIO ** (1.0 / steps) * np.exp(-2j * np.pi * freq / steps)
    turn = turn[:, None, None]
    mu = spectrum_of(depth)[:, None] + spectrum_of(width)[None, :]
    scaled = STEP_SCALE * turn
    middle = ((1.0 - turn) ** 2 + scaled * (mu + 2.0)) / scaled
    root = np.sqrt(middle * middle / 4.0 - 1.0)
    ratio = middle / 2.0 - root
    ratio = np.where(np.abs(ratio) < 1.0, ratio, middle / 2.0 + root)
    bottom = 1.0 - ratio ** (2 * rows + 2)
    near = ratio * (1.0 - ratio ** (2 * rows)) / bottom
    far = ratio**rows * (1.0 - ratio * ratio) / bottom
    parts = np.stack([near.real, near.imag, far.real, far.imag], axis=1)
    return parts.astype(np.float32)


def parts_of(values):
    high = values.astype(jnp.bfloat16)
    return high, (values - high.astype(jnp.float32)).astype(jnp.bfloat16)


def dot(left, right):
    return jnp.dot(left, right, preferred_element_type=jnp.float32)


def dot_parts(left, right):
    return dot(left[0], right[0]) + dot(left[1], right[0]) + dot(left[0], right[1])


def call(kernel, out_shape, flops, args, scratch=(), out=None):
    smem = pl.BlockSpec(memory_space=pltpu.SMEM)
    vmem = pl.BlockSpec(memory_space=pltpu.VMEM)
    moved = sum(x.size * x.dtype.itemsize for x in args)
    return pl.pallas_call(
        kernel,
        out_shape=out_shape,
        in_specs=[smem] + [vmem] * (len(args) - 1),
        out_specs=out or jax.tree.map(lambda _: vmem, out_shape),
        scratch_shapes=scratch,
        compiler_params=pltpu.CompilerParams(vmem_limit_bytes=VMEM_BYTES),
        cost_estimate=pl.CostEstimate(
            flops=flops, bytes_accessed=moved, transcendentals=0
        ),
    )(*args)


class Plan:
    def __init__(self, mesh, shape):
        self.steps = mesh.shape["tm"]
        self.groups = mesh.shape["gy"]
        self.depth, self.width = shape[1], shape[3]
        self.rows = shape[2] // self.groups
        self.half = self.steps // 2
        self.block = self.width // self.half
        self.folds = self.depth // 2

    def columns(self, owner):
        return pl.ds(pl.multiple_of(owner * self.block, LANES), self.block)


def fill_table(plan, fine, ids, angles, high, low):
    coarse = plan.width // fine
    sine, cosine = (
        angles[2 * coarse + part * fine : 2 * coarse + (part + 1) * fine]
        for part in range(2)
    )

    def step(index, carry):
        rows = pl.ds(pl.multiple_of(index * fine, fine), fine)
        value = angles[pl.ds(index, 1), :] * cosine
        value = value + angles[pl.ds(coarse + index, 1), :] * sine
        high[rows, :], low[rows, :] = parts_of(value)
        return carry

    lax.fori_loop(0, plan.width // fine, step, 0)


def angle_tables(count, fine):
    scale = math.sqrt(2.0 / (count + 1))
    columns = np.arange(count, dtype=np.int64) + 1
    tables = []
    for rows, factor in (
        (np.arange(count // fine, dtype=np.int64) * fine, scale),
        (np.arange(fine, dtype=np.int64) + 1, 1.0),
    ):
        turns = rows[:, None] * columns[None, :] % (2 * (count + 1))
        angle = np.pi * turns / (count + 1)
        tables += [factor * np.sin(angle), factor * np.cos(angle)]
    return jnp.asarray(np.concatenate(tables), jnp.float32)


def fold_tables(plan):
    rows, folds = sine_table(plan.rows), plan.folds
    depth = sine_table(plan.depth)
    tables = [np.kron(depth[parity::2, :folds], rows) for parity in range(2)]
    forth = jnp.stack(table_parts(np.stack(tables)))
    back = jnp.stack(table_parts(np.stack([table.T for table in tables])))
    return forth, back


def by_parity(plan, chunk):
    start = 0
    for parity in range(2):
        places = [c // 2 for c in chunk if c % 2 == parity]
        if places:
            assert places == list(range(places[0], places[0] + len(places)))
            count = len(places) * plan.rows
            first = places[0] * plan.rows
            yield parity, slice(start, start + count), slice(first, first + count)
            start += count


def forward(plan, chunk, ids, both, x, sxh, sxl, *outs):
    place = lax.rem(ids[0], plan.half)
    folds = plan.folds
    mirror = jnp.stack([x[plan.depth - 1 - z] for z in range(folds)])
    left = []
    for parity, _, at in by_parity(plan, chunk):
        folded = x[:folds] - mirror if parity else x[:folds] + mirror
        folded = parts_of(folded.reshape(folds * plan.rows, plan.width))
        table = both[0, parity, at], both[1, parity, at]
        left.append(parts_of(dot_parts(table, folded)))
    for k in range(plan.half):
        columns = plan.columns(place ^ k)
        right = sxh[:, columns], sxl[:, columns]
        value = jnp.concatenate([dot_parts(part, right) for part in left])
        outs[k][...] = value.reshape(len(chunk), plan.rows, plan.block)


def x_rows(plan, place, pieces, start, sxh, sxl):
    total = None
    for k, piece in enumerate(pieces, start):
        at = plan.columns(place ^ k)
        piece = parts_of(piece[...].reshape(-1, plan.block))
        value = dot_parts(piece, (sxh[at, :], sxl[at, :]))
        total = value if total is None else total + value
    return total


def first_rows(plan, ids, both, sxh, sxl, *refs):
    place = lax.rem(ids[0], plan.half)
    total = parts_of(x_rows(plan, place, refs[:-1], 0, sxh, sxl))
    value = dot_parts((both[0, 1], both[1, 1]), total)
    refs[-1][...] = value.reshape(refs[-1].shape)


def finish(plan, ids, both, sxh, sxl, early, piece, even, out, held, sent):
    folds = plan.folds
    at = plan.columns(lax.rem(ids[0], plan.half) ^ (plan.half - 1))
    modes = parts_of(piece[...].reshape(-1, plan.block))
    left = parts_of(dot_parts((both[0, 1], both[1, 1]), modes))
    copies = []
    for j in range(plan.half):
        columns = pl.ds(j * plan.block, plan.block)
        value = dot_parts(left, (sxh[at, columns], sxl[at, columns]))
        value = value.reshape(folds, plan.rows, plan.block) + early[:, :, columns]
        other = even[:, :, columns]
        held[j, :folds] = other + value
        for z in range(folds):
            held[j, plan.depth - 1 - z] = other[z] - value[z]
        copies.append(
            pltpu.make_async_copy(held.at[j], out.at[:, :, columns], sent.at[j])
        )
        copies[-1].start()
    for copy in copies:
        copy.wait()


def backward(plan, chunk, ready, last, ids, both, sxh, sxl, *refs):
    place = lax.rem(ids[0], plan.half)
    count = 2 if last else plan.half
    pieces, refs = refs[:count], refs[count:]
    before = dict(zip(ready, refs))
    outs, (high, low) = refs[len(ready) : -2], refs[-2:]
    folds = plan.folds
    shape = folds, plan.rows, plan.block
    if last:
        total = pieces[0][...] + x_rows(plan, place, pieces[1:], plan.half - 1, sxh, sxl)
    else:
        total = x_rows(plan, place, pieces, 0, sxh, sxl)
    high[...], low[...] = parts_of(total)
    for j in range(plan.half):
        columns = pl.ds(j * plan.block, plan.block)
        sums = {parity: before[parity][:, :, columns] for parity in ready}
        for parity, rows, at in by_parity(plan, chunk):
            table = both[0, parity, :, at], both[1, parity, :, at]
            value = dot_parts(table, (high[rows, columns], low[rows, columns]))
            value = value.reshape(shape)
            sums[parity] = sums[parity] + value if parity in sums else value
        if not last:
            for parity, out in zip(sorted(sums), outs):
                out[:, :, columns] = sums[parity]
            continue
        out, held, sent = outs
        held[j, :folds] = sums[0] + sums[1]
        other = sums[0] - sums[1]
        for z in range(folds):
            held[j, plan.depth - 1 - z] = other[z]
        pltpu.make_async_copy(held.at[j], out.at[:, :, columns], sent.at[j]).start()
    if last:
        for j in range(plan.half):
            columns = pl.ds(j * plan.block, plan.block)
            pltpu.make_async_copy(held.at[j], out.at[:, :, columns], sent.at[j]).wait()


def per_strip(plan, place, smu_z, smu_y, smu_x, edges, body, strip=STRIP):
    across = smu_x[:, plan.columns(place)]

    def step(index, carry):
        rows = pl.ds(pl.multiple_of(index * strip, strip), strip)
        plane = across + smu_y[rows, :]
        weights = edges[rows, :]
        for u in range(smu_z.shape[0]):
            body(u, rows, plane + smu_z[u : u + 1, :], weights)
        return carry

    lax.fori_loop(0, plan.rows // strip, step, 0)


class Cyclic:
    def __init__(self, smu, half):
        self.kappa = kappa = 2.0 - smu
        values = [jnp.zeros_like(kappa), jnp.ones_like(kappa)]
        for _ in range(half):
            values.append(kappa * values[-1] - values[-2])
        self.up, self.at, self.down = values[-1], values[-2], values[-3]
        det = (1.0 - ALPHA_RATIO) ** 2 + ALPHA_RATIO * (
            smu * (4.0 - smu) * (self.at * self.at)
        )
        inverse = 1.0 / det
        self.even = (0.5 * (1.0 - ALPHA_RATIO)) * (self.up - self.down) * inverse
        self.odd = (0.5 * (1.0 + ALPHA_RATIO)) * self.at * inverse

    def run(self, before, last, sources):
        values = []
        for source in sources:
            value = self.kappa * last - before
            before, last = last, value if source is None else value + source
            values.append(last)
        return before, last, values

    def start(self, sources):
        last = sources[0]
        before, last, _ = self.run(last, self.kappa * last + sources[1], sources[2:])
        return before, last

    def entry(self, p0, p1):
        return (
            self.even * p0 + self.odd * (2.0 * p1 - self.kappa * p0),
            self.even * p1 + self.odd * (self.kappa * p1 - 2.0 * p0),
        )

    def back(self, p0, p1):
        return self.up * p0 - self.at * p1, self.at * p0 - self.down * p1


def by_place(plan, place, body):
    for case in range(plan.half):
        pl.when(place == case)(functools.partial(body, case))


def row_sign():
    index = lax.broadcasted_iota(jnp.int32, (8, 1), 0)
    return (1 - 2 * (index % 2)).astype(jnp.float32)


def half_end(plan, ids, smu_z, smu_y, smu_x, edges, *refs):
    pieces = refs[: plan.half]
    ends, seen, sums = refs[plan.half :]
    steps, half = plan.steps, plan.half
    place = lax.rem(ids[0], half)
    mine = ids[0] // half
    leaving = jnp.where(mine == 0, 1.0, ALPHA_RATIO).astype(jnp.float32)
    sums[...] = jnp.zeros_like(sums)

    def with_place(case):
        def body(u, rows, smu, weights):
            cyclic = Cyclic(smu, half)
            sources = [pieces[case ^ j][u, rows, :] for j in range(half)]
            before, last = cyclic.start(sources)
            ends[0, u, rows, :] = before
            ends[1, u, rows, :] = last
            entry = cyclic.entry(ALPHA_RATIO * before, ALPHA_RATIO * last)
            before, last, own = cyclic.run(*entry, sources)
            _, _, other = cyclic.run(leaving * before, leaving * last, [None] * half)
            for values, window in ((own, mine), (other, 1 - mine)):
                for j, value in enumerate(values):
                    term = weights * value
                    term = sum(term[i : i + 8] for i in range(0, term.shape[0], 8))
                    sums[window * half + j, u] += term

        per_strip(plan, place, smu_z, smu_y, smu_x, edges, body, 2 * STRIP)

    by_place(plan, place, with_place)
    sign = row_sign()
    for n in range(steps):
        total = sums[n]
        seen[2 * n] = jnp.sum(total, axis=1)
        seen[2 * n + 1] = jnp.sum(total * sign, axis=1)


def c_mul(a, b):
    return a[0] * b[0] - a[1] * b[1], a[0] * b[1] + a[1] * b[0]


def c_add(a, b):
    return a[0] + b[0], a[1] + b[1]


def c_gap(a, b):
    product = c_mul(a, b)
    real, imag = 1.0 - product[0], -product[1]
    inverse = 1.0 / (real * real + imag * imag)
    return real * inverse, -imag * inverse


def join_rows(plan, ids, responses, *refs):
    groups, steps = plan.groups, plan.steps
    views = refs[:groups]
    out, seen, above, below = refs[groups:]
    place = lax.rem(ids[0], plan.half)
    me = ids[1]
    columns = plan.columns(place)
    for k in range(groups):
        seen[me ^ k] = views[k][...]
    radius = ALPHA_RATIO ** (1.0 / steps)
    grow = [radius**n for n in range(steps)]
    nothing = jnp.zeros(out.shape[1:], jnp.float32)
    for freq in range(steps // 2 + 1):
        angle = [2.0 * math.pi * (freq * n % steps) / steps for n in range(steps)]

        def spectrum(block, edge):
            real, imag = nothing, nothing
            for n in range(steps):
                value = seen[block, 2 * n + edge]
                real = real + value * np.float32(grow[n] * math.cos(angle[n]))
                if freq % (steps // 2):
                    imag = imag - value * np.float32(grow[n] * math.sin(angle[n]))
            return real, imag

        head = [spectrum(block, 0) for block in range(groups)]
        tail = [spectrum(block, 1) for block in range(groups)]
        near, far = (
            tuple(
                responses[freq, 2 * kind + part, :, columns]
                for part in range(2)
            )
            for kind in range(2)
        )
        square = c_mul(far, far)
        gammas, downs, ups = [near], [tail[0]], [head[groups - 1]]
        for d in range(1, groups - 1):
            gamma = gammas[-1]
            gap = c_gap(gamma, near)
            through = c_mul(far, gap)
            e = groups - 1 - d
            downs.append(
                c_add(
                    tail[d], c_mul(through, c_add(downs[-1], c_mul(gamma, head[d])))
                )
            )
            ups.append(
                c_add(head[e], c_mul(through, c_add(ups[-1], c_mul(gamma, tail[e]))))
            )
            gammas.append(c_add(near, c_mul(square, c_mul(gamma, gap))))
        for d in range(groups - 1):
            down, up = downs[d], ups[groups - 2 - d]
            from_top, from_end = gammas[d], gammas[groups - 2 - d]
            gap = c_gap(from_top, from_end)
            last = c_mul(c_add(down, c_mul(from_top, up)), gap)
            start = c_mul(c_add(up, c_mul(from_end, down)), gap)
            for part in range(2):
                above[d + 1, 2 * freq + part] = last[part]
                below[d, 2 * freq + part] = start[part]
        for part in range(2):
            above[0, 2 * freq + part] = nothing
            below[groups - 1, 2 * freq + part] = nothing
    for edge, side in enumerate((above, below)):
        parts = [side[me, i] for i in range(steps + 2)]
        for n in range(steps):
            total = nothing
            shrink = STEP_SCALE / (steps * grow[n])
            if n == steps - 1:
                shrink *= ALPHA_RATIO
            for freq in range(steps // 2 + 1):
                angle = 2.0 * math.pi * (freq * n % steps) / steps
                single = freq % (steps // 2) == 0
                weight = shrink if single else 2.0 * shrink
                total = total + parts[2 * freq] * np.float32(weight * math.cos(angle))
                if not single:
                    total = total - parts[2 * freq + 1] * np.float32(
                        weight * math.sin(angle)
                    )
            out[2 * ((n + 1) % steps) + edge] = total


def half_solve(plan, ids, smu_z, smu_y, smu_x, edges, *refs):
    pieces = refs[: plan.half]
    far, beside, beside_far = refs[plan.half : plan.half + 3]
    outs, around = refs[plan.half + 3 : -1], refs[-1]
    half = plan.half
    sign = row_sign()
    for n in range(plan.steps):
        for u in range(around.shape[1]):
            above, below = (
                beside[2 * n + edge, u : u + 1, :] + beside_far[2 * n + edge, u : u + 1, :]
                for edge in range(2)
            )
            around[n, u] = above + sign * below
    place = lax.rem(ids[0], half)
    mine = ids[0] // half
    entering = jnp.where(mine == 0, ALPHA_RATIO, 1.0).astype(jnp.float32)

    def with_place(case):
        def body(u, rows, smu, weights):
            cyclic = Cyclic(smu, half)

            def source(window, j):
                rows = around[window * half + j, u]
                return weights * jnp.concatenate([rows] * (weights.shape[0] // 8))

            own = [pieces[case ^ j][u, rows, :] + source(mine, j) for j in range(half)]
            other = [source(1 - mine, j) for j in range(half)]
            before, last = cyclic.start(other)
            before = entering * (before + far[0, u, rows, :])
            last = entering * (last + far[1, u, rows, :])
            before, last = cyclic.back(before, last)
            near = cyclic.start(own)
            entry = cyclic.entry(
                before + ALPHA_RATIO * near[0], last + ALPHA_RATIO * near[1]
            )
            _, _, values = cyclic.run(*entry, own)
            for j, value in enumerate(values):
                outs[case ^ j][u, rows, :] = value

        per_strip(plan, place, smu_z, smu_y, smu_x, edges, body, 2 * STRIP)

    by_place(plan, place, with_place)


def swap(values, axis, count, distance):
    if distance == 0:
        return values
    return lax.ppermute(values, axis, [(i, i ^ distance) for i in range(count)])


def on_device(plan, residual):
    steps, groups, half = plan.steps, plan.groups, plan.half
    ids = jnp.stack([lax.axis_index("tm"), lax.axis_index("gy")]).astype(jnp.int32)
    sine_rows = sine_table(plan.rows)
    smu_z, smu_y, smu_x = (
        STEP_SCALE * spectrum_of(count) for count in (plan.depth, plan.rows, plan.width)
    )
    smu_y = jnp.asarray(smu_y[:, None], jnp.float32)
    smu_x = jnp.asarray(smu_x[None, :], jnp.float32)
    edges = jnp.asarray(sine_rows[:, :1], jnp.float32)
    responses = edge_responses(steps, plan.depth, plan.rows, plan.width)
    field = residual[0]
    f32 = functools.partial(jax.ShapeDtypeStruct, dtype=jnp.float32)
    forth, back = fold_tables(plan)
    tables = call(
        functools.partial(fill_table, plan, FINE_ROWS),
        [jax.ShapeDtypeStruct((plan.width, plan.width), jnp.bfloat16)] * 2,
        4000 * plan.width * plan.width,
        (ids, angle_tables(plan.width, FINE_ROWS)),
    )
    work = []
    for chunk in CHUNKS:
        modes = f32((len(chunk), plan.rows, plan.block))
        count = len(chunk) * plan.rows * plan.width
        flops = 6 * count * (plan.width + plan.folds * plan.rows)
        pieces = call(
            functools.partial(forward, plan, chunk),
            [modes] * half,
            flops,
            (ids, forth, field, *tables),
        )
        pieces = [swap(v, "tm", steps, k) for k, v in enumerate(pieces)]
        smu_own = jnp.asarray(smu_z[list(chunk), None], jnp.float32)
        work.append((chunk, modes, flops, (ids, smu_own, smu_y, smu_x, edges), pieces))
    first, second = work[0][-1], work[1][-1]
    first[0], second[0] = lax.optimization_barrier((first[0], second[0]))
    sums = {}
    far = None
    for chunk, modes, flops, small, pieces in work:
        seen = f32((2 * steps, len(chunk), plan.block))
        ends, view = call(
            functools.partial(half_end, plan),
            [f32((2,) + modes.shape), seen],
            100 * modes.size * half,
            (*small, *pieces),
            [pltpu.VMEM((steps, len(chunk), 8, plan.block), jnp.float32)],
        )
        if far is not None:
            ends, far, beside_far = lax.optimization_barrier((ends, far, beside_far))
        far = swap(ends, "tm", steps, half)
        views = [swap(view, "gy", groups, k) for k in range(groups)]
        sides = pltpu.VMEM((groups, steps + 2) + seen.shape[1:], jnp.float32)
        beside = call(
            functools.partial(join_rows, plan),
            seen,
            100 * seen.size,
            (ids, jnp.asarray(responses[:, :, list(chunk)]), *views),
            [pltpu.VMEM((groups,) + seen.shape, jnp.float32), sides, sides],
        )
        beside_far = swap(beside, "tm", steps, half)
        pieces = call(
            functools.partial(half_solve, plan),
            [modes] * half,
            100 * modes.size * half,
            (*small, *pieces, far, beside, beside_far),
            [pltpu.VMEM((steps, len(chunk), 8, plan.block), jnp.float32)],
        )
        pieces = [swap(v, "tm", steps, k) for k, v in enumerate(pieces)]
        last = chunk == CHUNKS[-1]
        part = pltpu.VMEM((len(chunk) * plan.rows, plan.width), jnp.bfloat16)
        hold = [part, part]
        if last:
            block = field.shape[:2] + (plan.block,)
            hold = [
                pltpu.VMEM((half,) + block, jnp.float32),
                pltpu.SemaphoreType.DMA((half,)),
            ] + hold
            early = call(
                functools.partial(first_rows, plan),
                f32((plan.folds,) + field.shape[1:]),
                flops // 2,
                (ids, back, *tables, *pieces[:-1]),
            )
            result = call(
                functools.partial(finish, plan),
                f32(field.shape),
                flops // 2,
                (ids, back, *tables, early, pieces[-1], sums[0]),
                hold[:2],
                pl.BlockSpec(memory_space=pltpu.HBM),
            )
            break
        ready = tuple(sorted(sums))
        parities = sorted(set(ready) | {c % 2 for c in chunk})
        result = call(
            functools.partial(backward, plan, chunk, ready, last),
            f32(field.shape)
            if last
            else [f32((plan.folds,) + field.shape[1:])] * len(parities),
            flops,
            (ids, back, *tables, *pieces, *(sums[parity] for parity in ready)),
            hold,
            pl.BlockSpec(memory_space=pltpu.HBM) if last else None,
        )
        if not last:
            sums = dict(zip(parities, result))
    return result[None]


def solution(mesh):
    spec = P("tm", None, "gy", None)

    def whole(residual):
        plan = Plan(mesh, residual.shape)
        return jax.shard_map(
            functools.partial(on_device, plan),
            mesh=mesh,
            in_specs=(spec,),
            out_specs=spec,
            check_vma=False,
        )(residual)

    return whole
```
